32 devices in a mesh: row: 4 (over x, core), col: 8 (over z, y).
Axes of the slice: x: 2, y: 2, z: 4, core: 2. Of those that a mesh axis runs over, the one named last changes fastest.
Arguments:
- first_slc: bfloat16 [2, 2048, 2048], P(None, ('row', 'col')), may hold values from -200 to 200, as said below
- second_slc: bfloat16 [2, 2048, 2048], P(None, ('row', 'col')), may hold values from -200 to 200, as said below
Outputs:
- solution: float32 [2048, 2048], P('row', 'col')
- residual: float32 [2048, 2048], P('row', 'col')
The draws below stay inside these ranges and needn't reach their ends.
Inputs may be any that keep to these rules, and one draw needn't show every extreme that they name: `first_slc`: parts of a complex image. `second_slc`: parts of a complex image.
All inputs are finite; a program needn't handle non-finite values.
Results may differ from the reference program's by a relative error of at most 0.00155.
Values may be sent and summed in bfloat16 or wider, within the bound.
No kernel may reach another device: no remote copies, remote signals or barrier semaphores. Data moves between devices by JAX's collectives and lax.ppermute only.
A program may use at most 128 MiB of HBM per device.

```python
import math
import jax
import jax.numpy as jnp
from jax import lax

TILE_AZ = 512
TILE_RG = 256
ITERS = 2
AZ = 2048
RG = 2048
N_ROW = 4
N_COL = 8


def scene_parts(key):
    keys = jax.random.split(key, 5)
    base = jnp.clip(jax.random.normal(keys[0], (2, AZ, RG), jnp.float32), -6.0, 6.0)
    noise = jnp.clip(jax.random.normal(keys[1], (2, AZ, RG), jnp.float32), -6.0, 6.0)
    slopes = jax.random.uniform(keys[2], (4,), jnp.float32, -1.0, 1.0)
    line = jnp.arange(AZ).astype(jnp.float32)[:, None]
    pixel = jnp.arange(RG).astype(jnp.float32)[None, :]
    phase = 0.5 * slopes[0] * line + 0.5 * slopes[1] * pixel
    phase = phase + 4.0 * jnp.sin(0.03 * (1.0 + slopes[2]) * line + 0.02 * (1.0 + slopes[3]) * pixel)
    phase = phase + jax.random.uniform(keys[3], (AZ, RG), jnp.float32, -1.0, 1.0)
    coherence = jax.random.uniform(keys[4], (AZ, RG), jnp.float32, 0.2, 0.95)
    return (base, noise, phase, coherence)


def line_scales(key, spread):
    return jnp.exp(jax.random.uniform(key, (1, AZ, 1), jnp.float32, 0.0, spread))


def draw_first_slc(key, part):
    base, noise, phase, coherence = scene_parts(key)
    key = jax.random.fold_in(key, 11)
    scales = line_scales(key, 0.0)
    return (base * scales).astype(jnp.bfloat16)


def draw_second_slc(key, part):
    base, noise, phase, coherence = scene_parts(key)
    key = jax.random.fold_in(key, 23)
    cosine = jnp.cos(phase)
    sine = jnp.sin(phase)
    turned_re = base[0] * cosine + base[1] * sine
    turned_im = base[1] * cosine - base[0] * sine
    rest = jnp.sqrt(1.0 - coherence * coherence)
    value = jnp.stack([coherence * turned_re + rest * noise[0], coherence * turned_im + rest * noise[1]])
    scales = line_scales(key, 0.0)
    return (value * scales).astype(jnp.bfloat16)


def setup_inputs(seed: int = 0) -> dict:
    arg_keys = jax.random.split(jax.random.key(seed), 3)
    first_slc = draw_first_slc(jax.random.fold_in(arg_keys[2], 71), 0)
    second_slc = draw_second_slc(jax.random.fold_in(arg_keys[2], 71), 0)
    return {"first_slc": first_slc, "second_slc": second_slc}


EPS = 1e-05
DAMPING = 0.0001

def kernel_taps():
    offsets = jnp.arange(-4, 5).astype(jnp.float32)
    weights = jnp.exp(-offsets * offsets / 8.0)
    return weights / jnp.sum(weights)

def channel_products(first_re, first_im, second_re, second_im):
    first_re = first_re.astype(jnp.float32)
    first_im = first_im.astype(jnp.float32)
    second_re = second_re.astype(jnp.float32)
    second_im = second_im.astype(jnp.float32)
    return jnp.stack([first_re * second_re + first_im * second_im, first_im * second_re - first_re * second_im, first_re * first_re + first_im * first_im, second_re * second_re + second_im * second_im])

def smooth_range(field):
    kernel = kernel_taps()
    width = field.shape[2]
    padded = jnp.pad(field, ((0, 0), (0, 0), (4, 4)))
    running = kernel[0] * padded[:, :, 0:width]
    for offset in range(1, 9):
        running = running + kernel[offset] * padded[:, :, offset:offset + width]
    return running

def azimuth_valid(padded):
    kernel = kernel_taps()
    height = padded.shape[1] - 8
    running = kernel[0] * padded[:, 0:height]
    for offset in range(1, 9):
        running = running + kernel[offset] * padded[:, offset:offset + height]
    return running

def edge_pair(current, following):
    cross_re = following[0] * current[0] + following[1] * current[1]
    cross_im = following[1] * current[0] - following[0] * current[1]
    magnitude = jnp.sqrt(cross_re * cross_re + cross_im * cross_im)
    weight = (magnitude + cross_re) / (2.0 * (current[2] + EPS) * (following[2] + EPS))
    return (weight, weight * jnp.arctan2(cross_im, cross_re))

def cosine_table(count):
    position = jnp.arange(count).astype(jnp.float32)
    table = jnp.cos(math.pi * position[:, None] * (position[None, :] + 0.5) / count)
    factor = jnp.where(position == 0, jnp.sqrt(1.0 / count), jnp.sqrt(2.0 / count))
    return table * factor[:, None]

def eigen_table(count_az, count_rg):
    along_az = 2.0 - 2.0 * jnp.cos(math.pi * jnp.arange(count_az).astype(jnp.float32) / count_az)
    along_rg = 2.0 - 2.0 * jnp.cos(math.pi * jnp.arange(count_rg).astype(jnp.float32) / count_rg)
    return DAMPING + along_az[:, None] + along_rg[None, :]

def precondition(field):
    highest = lax.Precision.HIGHEST
    table_az = cosine_table(TILE_AZ)
    table_rg = cosine_table(TILE_RG)
    blocks = field.reshape(N_ROW, TILE_AZ, N_COL, TILE_RG)
    coef = jnp.einsum('ja,xayb->xjyb', table_az, blocks, precision=highest)
    coef = jnp.einsum('xjyb,kb->xjyk', coef, table_rg, precision=highest)
    coef = coef / eigen_table(TILE_AZ, TILE_RG)[None, :, None, :]
    back = jnp.einsum('ja,xjyk->xayk', table_az, coef, precision=highest)
    back = jnp.einsum('xayk,kb->xayb', back, table_rg, precision=highest)
    return back.reshape(AZ, RG)

def operate(field, weight_x, weight_left, weight_y, weight_up):
    right = jnp.pad(field[:, 1:], ((0, 0), (0, 1)))
    left = jnp.pad(field[:, :-1], ((0, 0), (1, 0)))
    below = jnp.pad(field[1:], ((0, 1), (0, 0)))
    above = jnp.pad(field[:-1], ((1, 0), (0, 0)))
    return DAMPING * field + weight_x * (field - right) + weight_left * (field - left) + weight_y * (field - below) + weight_up * (field - above)

def reference(first_slc, second_slc):
    fields = channel_products(first_slc[0], first_slc[1], second_slc[0], second_slc[1])
    ranged = smooth_range(fields)
    smoothed = azimuth_valid(jnp.pad(ranged, ((0, 0), (4, 4), (0, 0))))
    root = jnp.sqrt(smoothed[2] * smoothed[3])
    current = (smoothed[0], smoothed[1], root)
    beside = tuple((jnp.pad(part[:, 1:], ((0, 0), (0, 1))) for part in current))
    below = tuple((jnp.pad(part[1:], ((0, 1), (0, 0))) for part in current))
    weight_x, flux_x = edge_pair(current, beside)
    weight_y, flux_y = edge_pair(current, below)
    weight_left = jnp.pad(weight_x[:, :-1], ((0, 0), (1, 0)))
    flux_left = jnp.pad(flux_x[:, :-1], ((0, 0), (1, 0)))
    weight_up = jnp.pad(weight_y[:-1], ((1, 0), (0, 0)))
    flux_up = jnp.pad(flux_y[:-1], ((1, 0), (0, 0)))
    source = flux_left - flux_x + flux_up - flux_y
    solution = jnp.zeros_like(source)
    residual = source
    shaped = precondition(residual)
    residual_dot = jnp.sum(residual * shaped)
    direction = shaped
    for iteration in range(ITERS):
        operated = operate(direction, weight_x, weight_left, weight_y, weight_up)
        step_size = residual_dot / jnp.sum(direction * operated)
        solution = solution + step_size * direction
        residual = residual - step_size * operated
        if iteration + 1 < ITERS:
            shaped = precondition(residual)
            fresh_dot = jnp.sum(residual * shaped)
            direction = shaped + fresh_dot / residual_dot * direction
            residual_dot = fresh_dot
    return (solution, residual)
```

```python
import functools
import math

import jax
import jax.numpy as jnp
import ml_dtypes
import numpy as np
from jax import lax
from jax.experimental import pallas as pl
from jax.experimental.pallas import tpu as pltpu
from jax.sharding import PartitionSpec as P

EPS = 1e-05
DAMPING = 0.0001
RADIUS = 4
LANES = 128
HALO = 8
TURN = 2.0 * math.pi
VMEM_LIMIT = 40 * 1024 * 1024

ATAN = (
    0.1591549409219458,
    -0.05305126669892651,
    0.03181993346630217,
    -0.022611352052724496,
    0.016957432021882463,
    -0.011990188139443825,
    0.0068498925926071,
    -0.002591499099089036,
    0.00046210915702298266,
)
COS = (
    0.9999999997806517,
    -4.934802137228286,
    4.0587091643402005,
    -1.3352120566397616,
    0.23493755882899706,
    -0.024396716411350872,
)


def taps():
    offsets = np.arange(-RADIUS, RADIUS + 1).astype(np.float64)
    weights = np.exp(-offsets * offsets / 8.0)
    weights = weights / weights.sum()
    return [float(weights[RADIUS + j]) for j in range(RADIUS + 1)]


def cosine_table(count):
    j = np.arange(count)[:, None].astype(np.float64)
    i = np.arange(count)[None, :].astype(np.float64)
    table = np.cos(np.pi * j * (i + 0.5) / count) * np.sqrt(2.0 / count)
    table[0] = np.sqrt(1.0 / count)
    return table


def two_parts(table):
    table = table.astype(np.float32)
    high = table.astype(ml_dtypes.bfloat16)
    low = (table - high.astype(np.float32)).astype(ml_dtypes.bfloat16)
    return np.ascontiguousarray(high), np.ascontiguousarray(low)


def inverse_eigen(count_az, count_rg):
    along_az = 2.0 - 2.0 * np.cos(np.pi * np.arange(count_az) / count_az)
    along_rg = 2.0 - 2.0 * np.cos(np.pi * np.arange(count_rg) / count_rg)
    return (1.0 / (DAMPING + along_az[:, None] + along_rg[None, :])).astype(np.float32)


def poly(coefficients, y):
    value = jnp.full_like(y, coefficients[-1])
    for c in coefficients[-2::-1]:
        value = value * y + c
    return value


def angle_turns(im, re):
    a, b = jnp.abs(im), jnp.abs(re)
    big, small = jnp.maximum(a, b), jnp.minimum(a, b)
    t = small / jnp.maximum(big, 1e-37)
    p = t * poly(ATAN, t * t)
    p = jnp.where(a > b, 0.25 - p, p)
    p = jnp.where(re < 0.0, 0.5 - p, p)
    return jnp.where(im < 0.0, -p, p)


def edge(phase_p, gain_p, phase_q, gain_q):
    delta = phase_q - phase_p
    delta = delta - jnp.round(delta)
    half = poly(COS, delta * delta)
    weight = gain_p * gain_q * (half * half)
    return weight, weight * delta


def split(value):
    high = value.astype(jnp.bfloat16)
    return high, (value - high.astype(jnp.float32)).astype(jnp.bfloat16)


def dot3(a, b):
    f = functools.partial(jnp.dot, preferred_element_type=jnp.float32)
    return f(a[0], b[1]) + f(a[1], b[0]) + f(a[0], b[0])


def lanes_of(shape):
    return lax.broadcasted_iota(jnp.int32, shape, 1)


def call(body, outs, args, scratch, name, smem_first=True, flops=1000000):
    specs = [pl.BlockSpec(memory_space=pltpu.VMEM)] * len(args)
    if smem_first:
        specs[0] = pl.BlockSpec(memory_space=pltpu.SMEM)
    return pl.pallas_call(
        body,
        out_shape=[jax.ShapeDtypeStruct(s, d) for s, d in outs],
        in_specs=specs,
        out_specs=[pl.BlockSpec(memory_space=pltpu.VMEM)] * len(outs),
        scratch_shapes=scratch,
        compiler_params=pltpu.CompilerParams(vmem_limit_bytes=VMEM_LIMIT),
        cost_estimate=pl.CostEstimate(flops=flops, bytes_accessed=4000000, transcendentals=0),
        name=name,
    )(*args)


def strip_kernel(lines, width, tile, columns, exchange, ids, first, second, above, below, *rest):
    n_out = len(rest) - 3
    outs, (prod, ranged, field) = rest[:n_out], rest[n_out:]
    k = taps()
    own = ids[1]
    inside_above = jnp.where(ids[2] == 0, 0.0, 1.0).astype(jnp.float32)
    inside_below = jnp.where(ids[2] == ids[3] - 1, 0.0, 1.0).astype(jnp.float32)
    height = lines + 2 * HALO

    def products(ar, ai, br, bi, scale=None):
        ar, ai, br, bi = (v.astype(jnp.float32) for v in (ar, ai, br, bi))
        if scale is not None:
            ar, ai, br, bi = (v * scale for v in (ar, ai, br, bi))
        return (ar * br + ai * bi, ai * br - ar * bi, ar * ar + ai * ai, br * br + bi * bi)

    zero = jnp.zeros((height, LANES), jnp.float32)
    for f in range(4):
        prod[f, :, 0:LANES] = zero
        prod[f, :, LANES + width :] = zero
    step = min(width, 512)
    for c in range(0, width, step):
        at = slice(LANES + c, LANES + c + step)
        cs = slice(c, c + step)
        rows = min(lines, 16)
        for r in range(0, lines, rows):
            rs = slice(r, r + rows)
            values = products(first[0, rs, cs], first[1, rs, cs], second[0, rs, cs], second[1, rs, cs])
            for f in range(4):
                prod[f, HALO + r : HALO + r + rows, at] = values[f]
        for ref, r, scale in ((above, 0, inside_above), (below, HALO + lines, inside_below)):
            values = products(ref[0, :, cs], ref[1, :, cs], ref[2, :, cs], ref[3, :, cs], scale)
            for f in range(4):
                prod[f, r : r + HALO, at] = values[f]

    step = min(width, 1024)
    for f in range(4):
        for r in range(0, height, 8):
            for c in range(0, width, step):
                x = prod[f, r : r + 8, c : c + step + 2 * LANES]
                n = step + 2 * LANES
                total = k[0] * x
                for j in range(1, RADIUS + 1):
                    total = total + k[j] * (pltpu.roll(x, j, 1) + pltpu.roll(x, n - j, 1))
                ranged[f, r : r + 8, c : c + step] = total[:, LANES : LANES + step]

    def phase_gain(smoothed):
        re, im, one, two = smoothed
        gain = jnp.sqrt(re * re + im * im) / (jnp.sqrt(one * two) + EPS)
        return angle_turns(im, re), gain

    for f in range(2):
        field[f, :, 0:LANES] = zero[:lines]
        field[f, :, LANES + width :] = zero[:lines]
    rows = min(lines, 32)
    sub = lax.broadcasted_iota(jnp.int32, (HALO, 1), 0)
    low = jnp.zeros((HALO, 1), jnp.float32)
    high = jnp.zeros((HALO, 1), jnp.float32)
    for j in range(RADIUS + 1):
        low = jnp.where(sub == HALO - 1 - j, k[j], low)
        high = jnp.where(sub == j - 1, k[j], high)
    top, bottom = [], []
    for c in range(0, width, LANES):
        cs = slice(c, c + LANES)
        for r in range(0, lines, rows):
            smoothed = []
            for f in range(4):
                b = HALO + r
                total = k[0] * ranged[f, b : b + rows, cs]
                for j in range(1, RADIUS + 1):
                    total = total + k[j] * (
                        ranged[f, b - j : b - j + rows, cs] + ranged[f, b + j : b + j + rows, cs]
                    )
                smoothed.append(total)
            phase, gain = phase_gain(smoothed)
            field[0, r : r + rows, LANES + c : 2 * LANES + c] = phase
            field[1, r : r + rows, LANES + c : 2 * LANES + c] = gain

    step = min(width, 1024)
    low = low + jnp.zeros((HALO, step), jnp.float32)
    high = high + jnp.zeros((HALO, step), jnp.float32)
    mirror_low = jnp.zeros((HALO, 1), jnp.float32)
    mirror_high = jnp.zeros((HALO, 1), jnp.float32)
    for j in range(RADIUS + 1):
        mirror_high = jnp.where(sub == j, k[j], mirror_high)
        mirror_low = jnp.where(sub == HALO - j, k[j], mirror_low)
    ends = []
    for c in range(0, width, step):
        cs = slice(c, c + step)
        up = [
            jnp.sum(low * ranged[f, 0:HALO, cs] + high * ranged[f, HALO : 2 * HALO, cs], axis=0, keepdims=True)
            for f in range(4)
        ]
        down = [
            jnp.sum(
                mirror_low * ranged[f, lines : lines + HALO, cs]
                + mirror_high * ranged[f, lines + HALO : lines + 2 * HALO, cs],
                axis=0,
                keepdims=True,
            )
            for f in range(4)
        ]
        up_phase, up_gain = phase_gain(up)
        down_phase, down_gain = phase_gain(down)
        ends.append((up_phase, down_phase, up_gain * inside_above, down_gain * inside_below))
    for i, (a, b, c_, d) in enumerate(ends):
        at = slice(i * step, (i + 1) * step)
        prod[0, 0:1, at] = a
        prod[0, 1:2, at] = b
        prod[0, 2:3, at] = c_
        prod[0, 3:4, at] = d

    groups = lines // 8
    lane = lanes_of((8, LANES))

    def pack(out, start, aligned):
        hint = pl.multiple_of if aligned else (lambda v, _: v)
        out[0:lines, :] = field[0, :, pl.ds(hint(start + LANES, LANES), tile)]
        out[lines : 2 * lines, :] = field[1, :, pl.ds(hint(start + LANES, LANES), tile)]
        block = jnp.zeros((8, LANES), jnp.float32)
        for f in range(2):
            for side in range(2):
                offset = start if side == 0 else start + LANES + tile
                for g in range(groups):
                    target = (f * 2 + side) * groups + g
                    x = field[f, 8 * g : 8 * g + 8, pl.ds(hint(offset, LANES), LANES)]
                    shift = (target - (LANES - 1 if side == 0 else 0)) % LANES
                    if shift:
                        x = pltpu.roll(x, shift, 1)
                    block = jnp.where(lane == target, x, block)
        base = 2 * lines
        out[base : base + 8, 0:LANES] = block
        for i in range(4):
            for h in range(tile // LANES):
                out[base + 2 * i + h : base + 2 * i + h + 1, LANES : 2 * LANES] = prod[
                    0, i : i + 1, pl.ds(hint(start + h * LANES, LANES), LANES)
                ]

    if exchange == "permute":
        for s in range(columns):
            pack(outs[s], (own ^ s) * tile, True)
    else:
        for s in range(columns):
            pack(outs[0].at[s], s * tile, False)


def precondition(field, tables, inverse):
    az, az_t, rg, rg_t = tables
    coef = dot3(az, split(field))
    coef = dot3(split(coef), rg_t)
    coef = coef * inverse[...]
    back = dot3(az_t, split(coef))
    return dot3(split(back), rg)


def line_groups(ref, tile_az, edge_lane):
    lane = lanes_of((8, LANES))
    first = (edge_lane // LANES) * LANES
    block = jnp.zeros((8, LANES), jnp.float32)
    for g in range(tile_az // 8):
        x = ref[8 * g : 8 * g + 8, first : first + LANES]
        shift = (g - edge_lane) % LANES
        if shift:
            x = pltpu.roll(x, shift, 1)
        block = jnp.where(lane == g, x, block)
    return block


def spread_groups(block, first_group, count, target_lane, base=0):
    parts = []
    for g in range(first_group, first_group + count):
        shift = (target_lane - (base + g)) % LANES
        parts.append(pltpu.roll(block, shift, 1) if shift else block)
    return jnp.concatenate(parts, axis=0) if count > 1 else parts[0]


def shifted_right(x, left):
    lane = lanes_of(x.shape)
    if left is None:
        return jnp.where(lane == 0, 0.0, pltpu.roll(x, 1, 1))
    wide = jnp.concatenate([left] * (x.shape[1] // LANES), axis=1)
    return jnp.where(lane == 0, wide, pltpu.roll(x, 1, 1))


def shifted_left(x, right):
    lane = lanes_of(x.shape)
    wide = jnp.concatenate([right] * (x.shape[1] // LANES), axis=1)
    return jnp.where(lane == x.shape[1] - 1, wide, pltpu.roll(x, x.shape[1] - 1, 1))


def divergence(tile_az, step, along_x, rim_x, along_y, r):
    rs = slice(r, r + step)
    x = along_x[rs, :]
    return (x - shifted_left(x, rim_x[rs, :])) + along_y[rs, :] - along_y[r + 1 : r + 1 + step, :]


def tile_kernel(lines, tile_az, tile, columns, exchange, ids, *rest):
    chunks = rest[: columns if exchange == "permute" else 1]
    rest = rest[len(chunks) :]
    tables, inverse = rest[:8], rest[8]
    residual, shaped, weight_x, rim_x, weight_y, rows_out, left_out, right_out = rest[9:17]
    phase, gain, sides, ends, flux_x, flux_rim, flux_y = rest[17:]
    own = ids[1]
    pairs = [(tables[2 * i][...], tables[2 * i + 1][...]) for i in range(4)]

    for s in range(columns):
        if exchange == "permute":
            src, strip = chunks[s], own ^ s
        else:
            src, strip = chunks[0].at[s], s
        row = strip * lines
        if exchange == "permute":
            row = pl.multiple_of(row, 8)
        phase[pl.ds(HALO + row, lines), :] = src[0:lines, :]
        gain[pl.ds(HALO + row, lines), :] = src[lines : 2 * lines, :]
        base = 2 * lines
        at = pl.ds(pl.multiple_of(strip * 8, 8), 8) if exchange == "permute" else pl.ds(strip * 8, 8)
        sides[at, :] = src[base : base + 8, 0:LANES]
        ends[at, :] = src[base : base + 8, LANES : 2 * LANES]
    last = 8 * (columns - 1)
    for h in range(tile // LANES):
        cs = slice(h * LANES, (h + 1) * LANES)
        phase[HALO - 1 : HALO, cs] = ends[h : h + 1, :]
        gain[HALO - 1 : HALO, cs] = ends[4 + h : 5 + h, :]
        phase[HALO + tile_az : HALO + tile_az + 1, cs] = ends[last + 2 + h : last + 3 + h, :]
        gain[HALO + tile_az : HALO + tile_az + 1, cs] = ends[last + 6 + h : last + 7 + h, :]

    step = min(tile_az, 32)
    groups = lines // 8
    for r in range(0, tile_az, step):
        rs = slice(r, r + step)
        b = HALO + r
        p, g = phase[b : b + step, :], gain[b : b + step, :]
        halo = []
        for f in range(2):
            for side in range(2):
                parts = []
                for line_group in range(r // 8, (r + step) // 8):
                    strip, inner = divmod(line_group, groups)
                    block = sides[8 * strip : 8 * strip + 8, :]
                    source_lane = (f * 2 + side) * groups + inner
                    shift = ((0 if side == 0 else LANES - 1) - source_lane) % LANES
                    parts.append(pltpu.roll(block, shift, 1) if shift else block)
                halo.append(jnp.concatenate(parts, axis=0) if len(parts) > 1 else parts[0])
        w, f = edge(shifted_right(p, halo[0]), shifted_right(g, halo[2]), p, g)
        weight_x[rs, :] = w
        flux_x[rs, :] = f
        w, f = edge(p[:, tile - LANES :], g[:, tile - LANES :], halo[1], halo[3])
        rim_x[rs, :] = w
        flux_rim[rs, :] = f
        w, f = edge(phase[b - 1 : b - 1 + step, :], gain[b - 1 : b - 1 + step, :], p, g)
        weight_y[rs, :] = w
        flux_y[rs, :] = f
    b = HALO + tile_az
    w, f = edge(
        phase[b - 1 : b, :], gain[b - 1 : b, :], phase[b : b + 1, :], gain[b : b + 1, :]
    )
    weight_y[tile_az : tile_az + 8, :] = jnp.broadcast_to(w, (8, tile))
    flux_y[tile_az : tile_az + 8, :] = jnp.broadcast_to(f, (8, tile))

    for r in range(0, tile_az, step):
        residual[r : r + step, :] = TURN * divergence(tile_az, step, flux_x, flux_rim, flux_y, r)
    shaped[...] = precondition(residual[...], pairs, inverse)
    rows_out[0, 0:1, :] = shaped[0:1, :]
    rows_out[1, 0:1, :] = shaped[tile_az - 1 : tile_az, :]
    left_out[...] = line_groups(shaped, tile_az, 0)
    right_out[...] = line_groups(shaped, tile_az, tile - 1)


def apply_operator(tile_az, tile, u, weight_x, rim_x, weight_y, flux_x, flux_rim, flux_y, left, right, out):
    step = min(tile_az, 32)
    for r in range(0, tile_az, step):
        rs = slice(r, r + step)
        b = HALO + r
        x = u[b : b + step, :]
        l = None if left is None else spread_groups(left, r // 8, step // 8, 0)
        flux_x[rs, :] = weight_x[rs, :] * (x - shifted_right(x, l))
        edge_x = x[:, tile - LANES :]
        if right is None:
            flux_rim[rs, :] = -rim_x[rs, :] * edge_x
        else:
            flux_rim[rs, :] = rim_x[rs, :] * (spread_groups(right, r // 8, step // 8, LANES - 1) - edge_x)
        flux_y[rs, :] = weight_y[rs, :] * (x - u[b - 1 : b - 1 + step, :])
    b = HALO + tile_az
    flux_y[tile_az : tile_az + 1, :] = weight_y[tile_az : tile_az + 1, :] * (u[b : b + 1, :] - u[b - 1 : b, :])
    for r in range(0, tile_az, step):
        out[r : r + step, :] = DAMPING * u[HALO + r : HALO + r + step, :] + divergence(
            tile_az, step, flux_x, flux_rim, flux_y, r
        )


def inner(a, b, tile_az, offset_a=0, offset_b=0):
    total = jnp.zeros((32, a.shape[1]), jnp.float32)
    for r in range(0, tile_az, 32):
        total = total + a[offset_a + r : offset_a + r + 32, :] * b[offset_b + r : offset_b + r + 32, :]
    return jnp.sum(jnp.sum(total, axis=0, keepdims=True), axis=1, keepdims=True)


def second_kernel(
    tile_az, tile, residual, shaped, weight_x, rim_x, weight_y, up, down, left, right, *rest
):
    tables, inverse = rest[:8], rest[8]
    operated, shaped2, operated2, chunk = rest[9:13]
    u, flux_x, flux_rim, flux_y = rest[13:]
    pairs = [(tables[2 * i][...], tables[2 * i + 1][...]) for i in range(4)]
    u[HALO : HALO + tile_az, :] = shaped[...]
    u[HALO - 1 : HALO, :] = up[0:1, :]
    u[HALO + tile_az : HALO + tile_az + 1, :] = down[0:1, :]
    apply_operator(
        tile_az, tile, u, weight_x, rim_x, weight_y, flux_x, flux_rim, flux_y, left[...], right[...], operated
    )
    image = precondition(operated[...], pairs, inverse)
    shaped2[...] = image
    u[HALO : HALO + tile_az, :] = image
    zero = jnp.zeros((1, tile), jnp.float32)
    u[HALO - 1 : HALO, :] = zero
    u[HALO + tile_az : HALO + tile_az + 1, :] = zero
    apply_operator(
        tile_az, tile, u, weight_x, rim_x, weight_y, flux_x, flux_rim, flux_y, None, None, operated2
    )
    lane = lanes_of((1, LANES))
    sums = jnp.zeros((1, LANES), jnp.float32)
    for i, (a, b) in enumerate(
        (
            (residual, shaped),
            (shaped, operated),
            (residual, shaped2),
            (operated, shaped2),
            (shaped2, operated2),
        )
    ):
        sums = jnp.where(lane == i, inner(a, b, tile_az), sums)
    chunk[8:16, :] = jnp.broadcast_to(sums, (8, LANES))
    top = jnp.sqrt(weight_y[0:1, :]) * shaped2[0:1, :]
    bottom = jnp.sqrt(weight_y[tile_az : tile_az + 1, :]) * shaped2[tile_az - 1 : tile_az, :]
    for h in range(tile // LANES):
        cs = slice(h * LANES, (h + 1) * LANES)
        chunk[8 + 2 + h : 8 + 3 + h, :] = top[:, cs]
        chunk[8 + 4 + h : 8 + 5 + h, :] = bottom[:, cs]
    half = tile_az // 8
    left_rim = jnp.sqrt(line_groups(weight_x, tile_az, 0)) * line_groups(shaped2, tile_az, 0)
    right_rim = jnp.sqrt(line_groups(rim_x, tile_az, LANES - 1)) * line_groups(shaped2, tile_az, tile - 1)
    wide = lanes_of((8, LANES))
    chunk[0:8, :] = jnp.where(wide < half, left_rim, pltpu.roll(right_rim, half, 1))


def last_kernel(
    tile_az, tile, rows, columns, ids, gathered, residual, shaped, operated, shaped2, operated2, weight_x, rim_x,
    weight_y, solution_out, residual_out
):
    half = tile_az // 8
    lane = lanes_of((8, LANES))
    total = jnp.zeros((8, LANES), jnp.float32)
    cross_x = jnp.zeros((8, LANES), jnp.float32)
    cross_y = jnp.zeros((2, LANES), jnp.float32)
    for r in range(rows):
        for c in range(columns):
            i = r * columns + c
            total = total + gathered[i, 8:16, :]
            if c + 1 < columns:
                right = pltpu.roll(gathered[i, 0:8, :], LANES - half, 1)
                cross_x = cross_x + right * gathered[i + 1, 0:8, :]
            if r + 1 < rows:
                cross_y = cross_y + gathered[i, 12:14, :] * gathered[i + columns, 10:12, :]
    cross = jnp.sum(jnp.where(lane < half, cross_x, 0.0), keepdims=True) + jnp.sum(cross_y, keepdims=True)
    wide = total[0:1, :]
    first_lane = lanes_of((1, LANES))
    pick = [
        jnp.sum(jnp.where(first_lane == i, wide, 0.0), axis=1, keepdims=True) for i in range(5)
    ]
    dot0, curve0, mixed, cross_dot, curve2 = pick
    curve2 = curve2 - 2.0 * cross
    alpha = dot0 / curve0
    fresh = dot0 - alpha * (mixed + curve0) + alpha * alpha * cross_dot
    beta = fresh / dot0
    grown = 1.0 + beta
    curve1 = grown * grown * curve0 - 2.0 * alpha * grown * cross_dot + alpha * alpha * curve2
    step1 = fresh / curve1
    on_first = alpha + step1 * grown
    on_second = step1 * alpha

    row, col = ids[0], ids[1]
    here = row * columns + col

    def neighbour(ok, index):
        return jnp.where(ok, index, here), jnp.where(ok, 1.0, 0.0).astype(jnp.float32)

    up, up_ok = neighbour(row > 0, here - columns)
    down, down_ok = neighbour(row < rows - 1, here + columns)
    left, left_ok = neighbour(col > 0, here - 1)
    right, right_ok = neighbour(col < columns - 1, here + 1)
    from_left = pltpu.roll(gathered[left, 0:8, :], LANES - half, 1) * left_ok
    from_right = gathered[right, 0:8, :] * right_ok
    top = jnp.concatenate([gathered[up, 12 + h : 13 + h, :] for h in range(tile // LANES)], axis=1) * up_ok
    bottom = jnp.concatenate([gathered[down, 10 + h : 11 + h, :] for h in range(tile // LANES)], axis=1) * down_ok
    top = top * jnp.sqrt(weight_y[0:1, :])
    bottom = bottom * jnp.sqrt(weight_y[tile_az : tile_az + 1, :])
    from_left = from_left * jnp.sqrt(line_groups(weight_x, tile_az, 0))
    from_right = from_right * jnp.sqrt(line_groups(rim_x, tile_az, LANES - 1))
    step = min(tile_az, 32)
    for r in range(0, tile_az, step):
        rs = slice(r, r + step)
        solution_out[rs, :] = on_first * shaped[rs, :] - on_second * shaped2[rs, :]
        q = operated2[rs, :]
        wide = lanes_of((step, tile))
        l = jnp.concatenate([spread_groups(from_left, r // 8, step // 8, 0)] * (tile // LANES), axis=1)
        q = q - jnp.where(wide == 0, l, 0.0)
        l = jnp.concatenate([spread_groups(from_right, r // 8, step // 8, LANES - 1)] * (tile // LANES), axis=1)
        q = q - jnp.where(wide == tile - 1, l, 0.0)
        deep = lax.broadcasted_iota(jnp.int32, (step, tile), 0)
        if r == 0:
            q = q - jnp.where(deep == 0, jnp.broadcast_to(top, (step, tile)), 0.0)
        if r + step == tile_az:
            q = q - jnp.where(deep == step - 1, jnp.broadcast_to(bottom, (step, tile)), 0.0)
        residual_out[rs, :] = residual[rs, :] - on_first * operated[rs, :] + on_second * q


def around(value, axis, steps):
    count = lax.axis_size(axis)
    return lax.ppermute(value, axis, [(i, (i + steps) % count) for i in range(count)])


def shards(rows, columns, first_slc, second_slc):
    lines, width = first_slc.shape[1:]
    tile = width // columns
    tile_az = lines * columns
    axes = ("row", "col")
    exchange = "permute" if columns <= 8 else "all_to_all"
    row, col = lax.axis_index("row"), lax.axis_index("col")
    ids = jnp.stack([row, col, row * columns + col, jnp.int32(rows * columns)]).astype(jnp.int32)
    f32 = jnp.float32
    height = lines + 2 * HALO

    above = around(jnp.concatenate([first_slc[:, -HALO:], second_slc[:, -HALO:]], 0), axes, 1)
    below = around(jnp.concatenate([first_slc[:, :HALO], second_slc[:, :HALO]], 0), axes, -1)
    depth = 2 * lines + 8
    if exchange == "permute":
        outs = [((depth, tile), f32)] * columns
    else:
        outs = [((columns, depth, tile), f32)]
    sent = call(
        functools.partial(strip_kernel, lines, width, tile, columns, exchange),
        outs,
        (ids, first_slc, second_slc, above, below),
        [
            pltpu.VMEM((4, height, width + 2 * LANES), f32),
            pltpu.VMEM((4, height, width), f32),
            pltpu.VMEM((2, lines, width + 2 * LANES), f32),
        ],
        "strips",
    )
    if exchange == "permute":
        order = [4, 5, 6, 7, 2, 3, 1]
        arrived = [sent[0]] + [None] * (columns - 1)
        for s in order:
            if s < columns:
                arrived[s] = lax.ppermute(sent[s], "col", [(i, i ^ s) for i in range(columns)])
    else:
        arrived = [lax.all_to_all(sent[0], "col", 0, 0, tiled=True)]

    az, rg = cosine_table(tile_az), cosine_table(tile)
    tables = []
    for table in (az, az.T, rg, rg.T):
        tables.extend(jnp.asarray(part) for part in two_parts(table))
    inverse = jnp.asarray(inverse_eigen(tile_az, tile))

    whole = ((tile_az, tile), f32)
    column = ((8, LANES), f32)
    padded = pltpu.VMEM((tile_az + 2 * HALO, tile), f32)
    fluxes = [
        pltpu.VMEM((tile_az, tile), f32),
        pltpu.VMEM((tile_az, LANES), f32),
        pltpu.VMEM((tile_az + 8, tile), f32),
    ]
    residual, shaped, weight_x, rim_x, weight_y, ends, left_col, right_col = call(
        functools.partial(tile_kernel, lines, tile_az, tile, columns, exchange),
        [whole, whole, whole, ((tile_az, LANES), f32), ((tile_az + 8, tile), f32), ((2, 1, tile), f32), column, column],
        (ids, *arrived, *tables, inverse),
        [padded, padded, pltpu.VMEM((8 * columns, LANES), f32), pltpu.VMEM((8 * columns, LANES), f32), *fluxes],
        "tiles",
    )
    down = around(ends[0], "row", -1)
    up = around(ends[1], "row", 1)
    right = around(left_col, "col", -1)
    left = around(right_col, "col", 1)
    operated, shaped2, operated2, chunk = call(
        functools.partial(second_kernel, tile_az, tile),
        [whole, whole, whole, ((16, LANES), f32)],
        (residual, shaped, weight_x, rim_x, weight_y, up, down, left, right, *tables, inverse),
        [padded, *fluxes],
        "operator",
        smem_first=False,
    )
    spread = jnp.broadcast_to(chunk[None], (rows * columns, 16, LANES))
    gathered = lax.all_to_all(spread, axes, 0, 0, tiled=True)
    return tuple(
        call(
            functools.partial(last_kernel, tile_az, tile, rows, columns),
            [whole, whole],
            (ids, gathered, residual, shaped, operated, shaped2, operated2, weight_x, rim_x, weight_y),
            [],
            "finish",
        )
    )


def solution(mesh):
    placed = P(None, ("row", "col"), None)
    return jax.shard_map(
        functools.partial(shards, mesh.shape["row"], mesh.shape["col"]),
        mesh=mesh,
        in_specs=(placed, placed),
        out_specs=(P("row", "col"), P("row", "col")),
        check_vma=False,
    )
```

```python
import functools
import math

import jax
import jax.numpy as jnp
import ml_dtypes
import numpy as np
from jax import lax
from jax.experimental import pallas as pl
from jax.experimental.pallas import tpu as pltpu
from jax.sharding import PartitionSpec as P

EPS = 1e-05
DAMPING = 0.0001
RADIUS = 4
LANES = 128
HALO = 8
EDGE = 16
TURN = 2.0 * math.pi
CODE_SPAN = 248.0
VMEM_LIMIT = 40 * 1024 * 1024

ATAN = (
    0.1591549409219458,
    -0.05305126669892651,
    0.03181993346630217,
    -0.022611352052724496,
    0.016957432021882463,
    -0.011990188139443825,
    0.0068498925926071,
    -0.002591499099089036,
    0.00046210915702298266,
)
COS = (
    0.9999999997806517,
    -4.934802137228286,
    4.0587091643402005,
    -1.3352120566397616,
    0.23493755882899706,
    -0.024396716411350872,
)


def taps():
    offsets = np.arange(-RADIUS, RADIUS + 1).astype(np.float64)
    weights = np.exp(-offsets * offsets / 8.0)
    weights = weights / weights.sum()
    return [float(weights[RADIUS + j]) for j in range(RADIUS + 1)]


def cosine_table(count):
    j = np.arange(count)[:, None].astype(np.float64)
    i = np.arange(count)[None, :].astype(np.float64)
    table = np.cos(np.pi * j * (i + 0.5) / count) * np.sqrt(2.0 / count)
    table[0] = np.sqrt(1.0 / count)
    return table


def two_parts(table):
    table = table.astype(np.float32)
    high = table.astype(ml_dtypes.bfloat16)
    low = (table - high.astype(np.float32)).astype(ml_dtypes.bfloat16)
    return np.ascontiguousarray(high), np.ascontiguousarray(low)


def inverse_eigen(count_az, count_rg):
    along_az = 2.0 - 2.0 * np.cos(np.pi * np.arange(count_az) / count_az)
    along_rg = 2.0 - 2.0 * np.cos(np.pi * np.arange(count_rg) / count_rg)
    return (1.0 / (DAMPING + along_az[:, None] + along_rg[None, :])).astype(np.float32)


def poly(coefficients, y):
    value = jnp.full_like(y, coefficients[-1])
    for c in coefficients[-2::-1]:
        value = value * y + c
    return value


def angle_turns(im, re):
    a, b = jnp.abs(im), jnp.abs(re)
    big, small = jnp.maximum(a, b), jnp.minimum(a, b)
    t = small / jnp.maximum(big, 1e-37)
    p = t * poly(ATAN, t * t)
    p = jnp.where(a > b, 0.25 - p, p)
    p = jnp.where(re < 0.0, 0.5 - p, p)
    return jnp.where(im < 0.0, -p, p)


def edge(phase_p, gain_p, phase_q, gain_q):
    delta = phase_q - phase_p
    delta = delta - jnp.round(delta)
    half = gain_p * gain_q * poly(COS, delta * delta)
    weight = half * half
    return weight, weight * delta


def encode_gain(value):
    return jnp.exp2(value * CODE_SPAN - 0.5 * CODE_SPAN).astype(jnp.bfloat16)


def decode_gain(code):
    return (jnp.log2(code.astype(jnp.float32)) + 0.5 * CODE_SPAN) * (1.0 / CODE_SPAN)


def split(value):
    high = value.astype(jnp.bfloat16)
    return high, (value - high.astype(jnp.float32)).astype(jnp.bfloat16)


def dot3(a, b):
    f = functools.partial(jnp.dot, preferred_element_type=jnp.float32)
    return f(a[0], b[1]) + f(a[1], b[0]) + f(a[0], b[0])


def lanes_of(shape):
    return lax.broadcasted_iota(jnp.int32, shape, 1)


def call(body, outs, args, scratch, name, smem_first=True, flops=1000000):
    specs = [pl.BlockSpec(memory_space=pltpu.VMEM)] * len(args)
    if smem_first:
        specs[0] = pl.BlockSpec(memory_space=pltpu.SMEM)
    return pl.pallas_call(
        body,
        out_shape=[jax.ShapeDtypeStruct(s, d) for s, d in outs],
        in_specs=specs,
        out_specs=[pl.BlockSpec(memory_space=pltpu.VMEM)] * len(outs),
        scratch_shapes=scratch,
        compiler_params=pltpu.CompilerParams(vmem_limit_bytes=VMEM_LIMIT),
        cost_estimate=pl.CostEstimate(flops=flops, bytes_accessed=4000000, transcendentals=0),
        name=name,
    )(*args)


def interior(body, outs, args, scratch):
    return pl.pallas_call(
        body,
        out_shape=[jax.ShapeDtypeStruct(s, d) for s, d in outs],
        in_specs=[pl.BlockSpec(memory_space=pl.ANY)] * 2,
        out_specs=[pl.BlockSpec(memory_space=pltpu.VMEM)] * len(outs),
        scratch_shapes=scratch,
        compiler_params=pltpu.CompilerParams(vmem_limit_bytes=VMEM_LIMIT),
        cost_estimate=pl.CostEstimate(flops=8000000, bytes_accessed=4000000, transcendentals=0),
        name="interior",
    )(*args)


def phase_gain(smoothed):
    re, im, one, two = smoothed
    gain = jnp.sqrt(re * re + im * im) / (jnp.sqrt(one * two) + EPS)
    return angle_turns(im, re), jnp.sqrt(gain)


def products(ar, ai, br, bi, scale=None):
    ar, ai, br, bi = (v.astype(jnp.float32) for v in (ar, ai, br, bi))
    if scale is not None:
        ar, ai, br, bi = (v * scale for v in (ar, ai, br, bi))
    return (ar * br + ai * bi, ai * br - ar * bi, ar * ar + ai * ai, br * br + bi * bi)


def along_range(x):
    k = taps()
    n = x.shape[1]
    total = k[0] * x
    for j in range(1, RADIUS + 1):
        total = total + k[j] * (pltpu.roll(x, j, 1) + pltpu.roll(x, n - j, 1))
    return total


def along_azimuth(ref, f, row, rows, cs):
    k = taps()
    total = k[0] * ref[f, row : row + rows, cs]
    for j in range(1, RADIUS + 1):
        total = total + k[j] * (ref[f, row - j : row - j + rows, cs] + ref[f, row + j : row + j + rows, cs])
    return total


def end_weights(before):
    k = taps()
    sub = lax.broadcasted_iota(jnp.int32, (HALO, 1), 0)
    low = jnp.zeros((HALO, 1), jnp.float32)
    high = jnp.zeros((HALO, 1), jnp.float32)
    for j in range(RADIUS + 1):
        low = jnp.where(sub == (HALO - 1 - j if before else HALO - j), k[j], low)
        high = jnp.where(sub == (j - 1 if before else j), k[j], high)
    return low, high


def interior_kernel(lines, width, tile, columns, first, second, ranged, codes, rims, raw, prod, field, sems):
    chunk = 16
    copies = []
    for i in range(lines // chunk):
        rs = pl.ds(i * chunk, chunk)
        for a, ref in enumerate((first, second)):
            copy = pltpu.make_async_copy(ref.at[:, rs, :], raw.at[a, :, rs, :], sems.at[2 * i + a])
            copy.start()
            copies.append(copy)
    zero = jnp.zeros((lines, LANES), jnp.float32)
    for f in range(4):
        prod[f, :, 0:LANES] = zero[:chunk]
        prod[f, :, LANES + width :] = zero[:chunk]
        ranged[f, :, 0:LANES] = zero
        ranged[f, :, LANES + width :] = zero
    wide = min(width, 1024)
    for i in range(lines // chunk):
        copies[2 * i].wait()
        copies[2 * i + 1].wait()
        rs = slice(i * chunk, (i + 1) * chunk)
        for c in range(0, width, 512):
            cs = slice(c, c + 512)
            values = products(raw[0, 0, rs, cs], raw[0, 1, rs, cs], raw[1, 0, rs, cs], raw[1, 1, rs, cs])
            for f in range(4):
                prod[f, :, LANES + c : LANES + c + 512] = values[f]
        for f in range(4):
            for r in range(0, chunk, 8):
                for c in range(0, width, wide):
                    total = along_range(prod[f, r : r + 8, c : c + wide + 2 * LANES])
                    row = i * chunk + r
                    ranged[f, row : row + 8, LANES + c : LANES + c + wide] = total[:, LANES : LANES + wide]
    inner = lines - 2 * EDGE
    for f in range(2):
        field[f, :, 0:LANES] = zero[:inner]
        field[f, :, LANES + width :] = zero[:inner]
    for c in range(0, width, LANES):
        cs = slice(LANES + c, 2 * LANES + c)
        out = slice(c, c + LANES)
        for r in range(0, inner, 16):
            smoothed = [along_azimuth(ranged, f, EDGE + r, 16, cs) for f in range(4)]
            phase, gain = phase_gain(smoothed)
            field[0, r : r + 16, cs] = phase
            field[1, r : r + 16, cs] = gain
            codes[0, r : r + 16, out], codes[1, r : r + 16, out] = split(phase)
            codes[2, r : r + 16, out] = encode_gain(gain)
    groups = lines // 8
    for t in range(columns):
        rims[t] = rim_block(field, groups, range(EDGE // 8, (lines - EDGE) // 8), EDGE // 8, t * tile, tile, None)


def rim_block(field, groups, which, first_group, start, tile, block, hint=None):
    lane = lanes_of((8, LANES))
    if block is None:
        block = jnp.zeros((8, LANES), jnp.float32)
    for f in range(2):
        for side in range(2):
            offset = start if side == 0 else start + LANES + tile
            at = slice(offset, offset + LANES) if hint is None else pl.ds(hint(offset, LANES), LANES)
            for g in which:
                target = (f * 2 + side) * groups + g
                row = 8 * (g - first_group)
                x = field[f, row : row + 8, at]
                shift = (target - (LANES - 1 if side == 0 else 0)) % LANES
                if shift:
                    x = pltpu.roll(x, shift, 1)
                block = jnp.where(lane == target, x, block)
    return block


def border_kernel(lines, width, tile, columns, across, ids, ranged, codes, rims, from_pair, from_next, *rest):
    half = columns // 2
    outs, (prod, seg, field, ends) = rest[:half], rest[half:]
    own = ids[1]
    odd = ids[4]
    first_tile = (own & half) ^ (half if across else 0)
    span = half * tile + 2 * LANES
    start = pl.multiple_of(first_tile * tile, LANES)
    inside = (
        jnp.where(ids[2] == 0, 0.0, 1.0).astype(jnp.float32),
        jnp.where(ids[2] == ids[3] - 1, 0.0, 1.0).astype(jnp.float32),
    )
    zero = jnp.zeros((HALO, 2 * LANES), jnp.float32)
    own_rows = EDGE + HALO
    pixel = lanes_of((HALO, span)) + (start - LANES)
    in_image = jnp.logical_and(pixel >= 0, pixel < width)
    for e in range(2):
        flag = odd if e == 0 else 1 - odd
        keep = flag.astype(jnp.float32)
        for f in range(4):
            prod[f, :, 0 : 2 * LANES] = zero
            prod[f, :, 2 * LANES + width :] = zero
        for c in range(0, width, 512):
            cs = slice(c, c + 512)
            parts = [
                from_pair[i, :, cs].astype(jnp.float32) * keep + from_next[i, :, cs].astype(jnp.float32) * (1.0 - keep)
                for i in range(4)
            ]
            values = products(*parts, inside[e])
            for f in range(4):
                prod[f, :, 2 * LANES + c : 2 * LANES + c + 512] = values[f]
        for f in range(4):
            total = along_range(prod[f, :, pl.ds(start, span + 2 * LANES)])[:, LANES : LANES + span]
            total = jnp.where(in_image, total, 0.0)
            if e == 0:
                seg[e, f, 0:HALO, :] = total
                seg[e, f, HALO:, :] = ranged[f, 0:own_rows, pl.ds(start, span)]
            else:
                seg[e, f, own_rows:, :] = total
                seg[e, f, 0:own_rows, :] = ranged[f, lines - own_rows :, pl.ds(start, span)]
    for e in range(2):
        ref = seg.at[e]
        for c in range(0, span, LANES):
            cs = slice(c, c + LANES)
            smoothed = [along_azimuth(ref, f, HALO, EDGE, cs) for f in range(4)]
            phase, gain = phase_gain(smoothed)
            field[0, e * EDGE : (e + 1) * EDGE, cs] = phase
            field[1, e * EDGE : (e + 1) * EDGE, cs] = gain
        low, high = end_weights(e == 0)
        r = 0 if e == 0 else own_rows - HALO
        smoothed = [
            jnp.sum(low * ref[f, r : r + HALO, :] + high * ref[f, r + HALO : r + 2 * HALO, :], axis=0, keepdims=True)
            for f in range(4)
        ]
        phase, gain = phase_gain(smoothed)
        ends[e : e + 1, :] = phase
        ends[2 + e : 3 + e, :] = gain * inside[e]
    groups = lines // 8
    edge_groups = EDGE // 8
    inner = lines - 2 * EDGE
    for n, s in enumerate(range(half, columns) if across else range(half)):
        out = outs[n]
        target = own ^ s
        local = pl.multiple_of((target - first_tile) * tile, LANES)
        cs = pl.ds(pl.multiple_of(local + LANES, LANES), tile)
        wide = pl.ds(pl.multiple_of(target * tile, LANES), tile)
        for i in range(3):
            out[i * lines + EDGE : i * lines + EDGE + inner, :] = codes[i, :, wide]
        for e in range(2):
            row = 0 if e == 0 else lines - EDGE
            rs = slice(e * EDGE, (e + 1) * EDGE)
            out[row : row + EDGE, :], out[lines + row : lines + row + EDGE, :] = split(field[0, rs, cs])
            out[2 * lines + row : 2 * lines + row + EDGE, :] = encode_gain(field[1, rs, cs])
        block = rims[target]
        block = rim_block(field, groups, range(edge_groups), 0, local, tile, block, pl.multiple_of)
        block = rim_block(
            field, groups, range(groups - edge_groups, groups), groups - 2 * edge_groups, local, tile, block,
            pl.multiple_of,
        )
        rows = []
        for i in range(4):
            for h in range(tile // LANES):
                rows.append(ends[i : i + 1, pl.ds(pl.multiple_of(local + (h + 1) * LANES, LANES), LANES)])
        block = jnp.concatenate([block, jnp.concatenate(rows, axis=0)], axis=1)
        out[3 * lines :, :] = jnp.concatenate(split(block), axis=0)


def strip_kernel(lines, width, tile, columns, exchange, ids, first, second, above, below, *rest):
    n_out = len(rest) - 3
    outs, (prod, ranged, field) = rest[:n_out], rest[n_out:]
    k = taps()
    own = ids[1]
    inside_above = jnp.where(ids[2] == 0, 0.0, 1.0).astype(jnp.float32)
    inside_below = jnp.where(ids[2] == ids[3] - 1, 0.0, 1.0).astype(jnp.float32)
    height = lines + 2 * HALO

    zero = jnp.zeros((height, LANES), jnp.float32)
    for f in range(4):
        prod[f, :, 0:LANES] = zero
        prod[f, :, LANES + width :] = zero
    step = min(width, 512)
    for c in range(0, width, step):
        at = slice(LANES + c, LANES + c + step)
        cs = slice(c, c + step)
        rows = min(lines, 16)
        for r in range(0, lines, rows):
            rs = slice(r, r + rows)
            values = products(first[0, rs, cs], first[1, rs, cs], second[0, rs, cs], second[1, rs, cs])
            for f in range(4):
                prod[f, HALO + r : HALO + r + rows, at] = values[f]
        for ref, r, scale in ((above, 0, inside_above), (below, HALO + lines, inside_below)):
            values = products(ref[0, :, cs], ref[1, :, cs], ref[2, :, cs], ref[3, :, cs], scale)
            for f in range(4):
                prod[f, r : r + HALO, at] = values[f]

    step = min(width, 1024)
    for f in range(4):
        for r in range(0, height, 8):
            for c in range(0, width, step):
                x = prod[f, r : r + 8, c : c + step + 2 * LANES]
                n = step + 2 * LANES
                total = k[0] * x
                for j in range(1, RADIUS + 1):
                    total = total + k[j] * (pltpu.roll(x, j, 1) + pltpu.roll(x, n - j, 1))
                ranged[f, r : r + 8, c : c + step] = total[:, LANES : LANES + step]

    for f in range(2):
        field[f, :, 0:LANES] = zero[:lines]
        field[f, :, LANES + width :] = zero[:lines]
    rows = min(lines, 32)
    sub = lax.broadcasted_iota(jnp.int32, (HALO, 1), 0)
    low = jnp.zeros((HALO, 1), jnp.float32)
    high = jnp.zeros((HALO, 1), jnp.float32)
    for j in range(RADIUS + 1):
        low = jnp.where(sub == HALO - 1 - j, k[j], low)
        high = jnp.where(sub == j - 1, k[j], high)
    top, bottom = [], []
    for c in range(0, width, LANES):
        cs = slice(c, c + LANES)
        for r in range(0, lines, rows):
            smoothed = []
            for f in range(4):
                b = HALO + r
                total = k[0] * ranged[f, b : b + rows, cs]
                for j in range(1, RADIUS + 1):
                    total = total + k[j] * (
                        ranged[f, b - j : b - j + rows, cs] + ranged[f, b + j : b + j + rows, cs]
                    )
                smoothed.append(total)
            phase, gain = phase_gain(smoothed)
            field[0, r : r + rows, LANES + c : 2 * LANES + c] = phase
            field[1, r : r + rows, LANES + c : 2 * LANES + c] = gain

    step = min(width, 1024)
    low = low + jnp.zeros((HALO, step), jnp.float32)
    high = high + jnp.zeros((HALO, step), jnp.float32)
    mirror_low = jnp.zeros((HALO, 1), jnp.float32)
    mirror_high = jnp.zeros((HALO, 1), jnp.float32)
    for j in range(RADIUS + 1):
        mirror_high = jnp.where(sub == j, k[j], mirror_high)
        mirror_low = jnp.where(sub == HALO - j, k[j], mirror_low)
    ends = []
    for c in range(0, width, step):
        cs = slice(c, c + step)
        up = [
            jnp.sum(low * ranged[f, 0:HALO, cs] + high * ranged[f, HALO : 2 * HALO, cs], axis=0, keepdims=True)
            for f in range(4)
        ]
        down = [
            jnp.sum(
                mirror_low * ranged[f, lines : lines + HALO, cs]
                + mirror_high * ranged[f, lines + HALO : lines + 2 * HALO, cs],
                axis=0,
                keepdims=True,
            )
            for f in range(4)
        ]
        up_phase, up_gain = phase_gain(up)
        down_phase, down_gain = phase_gain(down)
        ends.append((up_phase, down_phase, up_gain * inside_above, down_gain * inside_below))
    for i, (a, b, c_, d) in enumerate(ends):
        at = slice(i * step, (i + 1) * step)
        prod[0, 0:1, at] = a
        prod[0, 1:2, at] = b
        prod[0, 2:3, at] = c_
        prod[0, 3:4, at] = d

    groups = lines // 8
    lane = lanes_of((8, LANES))

    def pack(out, start, aligned):
        hint = pl.multiple_of if aligned else (lambda v, _: v)
        out[0:lines, :] = field[0, :, pl.ds(hint(start + LANES, LANES), tile)]
        out[lines : 2 * lines, :] = field[1, :, pl.ds(hint(start + LANES, LANES), tile)]
        block = jnp.zeros((8, LANES), jnp.float32)
        for f in range(2):
            for side in range(2):
                offset = start if side == 0 else start + LANES + tile
                for g in range(groups):
                    target = (f * 2 + side) * groups + g
                    x = field[f, 8 * g : 8 * g + 8, pl.ds(hint(offset, LANES), LANES)]
                    shift = (target - (LANES - 1 if side == 0 else 0)) % LANES
                    if shift:
                        x = pltpu.roll(x, shift, 1)
                    block = jnp.where(lane == target, x, block)
        base = 2 * lines
        out[base : base + 8, 0:LANES] = block
        for i in range(4):
            for h in range(tile // LANES):
                out[base + 2 * i + h : base + 2 * i + h + 1, LANES : 2 * LANES] = prod[
                    0, i : i + 1, pl.ds(hint(start + h * LANES, LANES), LANES)
                ]

    if exchange == "permute":
        for s in range(columns):
            pack(outs[s], (own ^ s) * tile, True)
    else:
        for s in range(columns):
            pack(outs[0].at[s], s * tile, False)


def precondition(field, tables, inverse):
    az, az_t, rg, rg_t = tables
    coef = dot3(az, split(field))
    coef = dot3(split(coef), rg_t)
    coef = coef * inverse[...]
    back = dot3(az_t, split(coef))
    return dot3(split(back), rg)


def table_pairs(tables):
    pairs = []
    for ref in tables:
        n = ref.shape[1]
        parts = [ref[i * n : (i + 1) * n, :] for i in range(4)]
        pairs += [(parts[0], parts[1]), (parts[2], parts[3])]
    return pairs


def line_groups(ref, tile_az, edge_lane):
    lane = lanes_of((8, LANES))
    first = (edge_lane // LANES) * LANES
    block = jnp.zeros((8, LANES), jnp.float32)
    for g in range(tile_az // 8):
        x = ref[8 * g : 8 * g + 8, first : first + LANES]
        shift = (g - edge_lane) % LANES
        if shift:
            x = pltpu.roll(x, shift, 1)
        block = jnp.where(lane == g, x, block)
    return block


def spread_groups(block, first_group, count, target_lane, base=0):
    parts = []
    for g in range(first_group, first_group + count):
        shift = (target_lane - (base + g)) % LANES
        parts.append(pltpu.roll(block, shift, 1) if shift else block)
    return jnp.concatenate(parts, axis=0) if count > 1 else parts[0]


def shifted_right(x, left):
    lane = lanes_of(x.shape)
    if left is None:
        return jnp.where(lane == 0, 0.0, pltpu.roll(x, 1, 1))
    wide = jnp.concatenate([left] * (x.shape[1] // LANES), axis=1)
    return jnp.where(lane == 0, wide, pltpu.roll(x, 1, 1))


def shifted_left(x, right):
    lane = lanes_of(x.shape)
    wide = jnp.concatenate([right] * (x.shape[1] // LANES), axis=1)
    return jnp.where(lane == x.shape[1] - 1, wide, pltpu.roll(x, x.shape[1] - 1, 1))


def divergence(tile_az, step, along_x, rim_x, along_y, r):
    rs = slice(r, r + step)
    x = along_x[rs, :]
    return (x - shifted_left(x, rim_x[rs, :])) + along_y[rs, :] - along_y[r + 1 : r + 1 + step, :]


def tile_kernel(lines, tile_az, tile, columns, exchange, ids, *rest):
    chunks = rest[: columns if exchange == "permute" else 1]
    rest = rest[len(chunks) :]
    tables, inverse = rest[:2], rest[2]
    residual, shaped, weight_x, rim_x, weight_y, row_pair, row_next, col_pair, col_next = rest[3:12]
    phase, gain, sides, ends, flux_x, flux_rim, flux_y = rest[12:]
    own = ids[1]
    pairs = table_pairs(tables)

    for s in range(columns):
        if exchange == "permute":
            src, strip = chunks[s], own ^ s
        else:
            src, strip = chunks[0].at[s], s
        row = strip * lines
        if exchange == "permute":
            row = pl.multiple_of(row, 8)
        at = pl.ds(pl.multiple_of(strip * 8, 8), 8) if exchange == "permute" else pl.ds(strip * 8, 8)
        if exchange == "permute":
            phase[pl.ds(HALO + row, lines), :] = src[0:lines, :].astype(jnp.float32) + src[
                lines : 2 * lines, :
            ].astype(jnp.float32)
            gain[pl.ds(HALO + row, lines), :] = decode_gain(src[2 * lines : 3 * lines, :])
            both = src[3 * lines :, :].astype(jnp.float32)
            block = both[0:8, :] + both[8:16, :]
        else:
            phase[pl.ds(HALO + row, lines), :] = src[0:lines, :]
            gain[pl.ds(HALO + row, lines), :] = src[lines : 2 * lines, :]
            block = src[2 * lines : 2 * lines + 8, :]
        sides[at, :] = block[:, 0:LANES]
        ends[at, :] = block[:, LANES : 2 * LANES]
    last = 8 * (columns - 1)
    for h in range(tile // LANES):
        cs = slice(h * LANES, (h + 1) * LANES)
        phase[HALO - 1 : HALO, cs] = ends[h : h + 1, :]
        gain[HALO - 1 : HALO, cs] = ends[4 + h : 5 + h, :]
        phase[HALO + tile_az : HALO + tile_az + 1, cs] = ends[last + 2 + h : last + 3 + h, :]
        gain[HALO + tile_az : HALO + tile_az + 1, cs] = ends[last + 6 + h : last + 7 + h, :]

    step = min(tile_az, 32)
    groups = lines // 8
    for r in range(0, tile_az, step):
        rs = slice(r, r + step)
        b = HALO + r
        p, g = phase[b : b + step, :], gain[b : b + step, :]
        halo = []
        for f in range(2):
            for side in range(2):
                parts = []
                for line_group in range(r // 8, (r + step) // 8):
                    strip, inner = divmod(line_group, groups)
                    block = sides[8 * strip : 8 * strip + 8, :]
                    source_lane = (f * 2 + side) * groups + inner
                    shift = ((0 if side == 0 else LANES - 1) - source_lane) % LANES
                    parts.append(pltpu.roll(block, shift, 1) if shift else block)
                halo.append(jnp.concatenate(parts, axis=0) if len(parts) > 1 else parts[0])
        w, f = edge(shifted_right(p, halo[0]), shifted_right(g, halo[2]), p, g)
        weight_x[rs, :] = w
        flux_x[rs, :] = f
        w, f = edge(p[:, tile - LANES :], g[:, tile - LANES :], halo[1], halo[3])
        rim_x[rs, :] = w
        flux_rim[rs, :] = f
        w, f = edge(phase[b - 1 : b - 1 + step, :], gain[b - 1 : b - 1 + step, :], p, g)
        weight_y[rs, :] = w
        flux_y[rs, :] = f
    b = HALO + tile_az
    w, f = edge(
        phase[b - 1 : b, :], gain[b - 1 : b, :], phase[b : b + 1, :], gain[b : b + 1, :]
    )
    weight_y[tile_az : tile_az + 8, :] = jnp.broadcast_to(w, (8, tile))
    flux_y[tile_az : tile_az + 8, :] = jnp.broadcast_to(f, (8, tile))

    for r in range(0, tile_az, step):
        residual[r : r + step, :] = TURN * divergence(tile_az, step, flux_x, flux_rim, flux_y, r)
    shaped[...] = precondition(residual[...], pairs, inverse)
    row_odd, col_odd = ids[5] == 1, ids[4] == 1
    top = jnp.concatenate([shaped[0:1, h : h + LANES] for h in range(0, tile, LANES)], axis=0)
    bottom = jnp.concatenate([shaped[tile_az - 1 : tile_az, h : h + LANES] for h in range(0, tile, LANES)], axis=0)
    row_pair[0:2, :] = jnp.where(row_odd, top, bottom)
    row_next[0:2, :] = jnp.where(row_odd, bottom, top)
    left = line_groups(shaped, tile_az, 0)
    right = line_groups(shaped, tile_az, tile - 1)
    col_pair[...] = jnp.where(col_odd, left, right)
    col_next[...] = jnp.where(col_odd, right, left)


def apply_operator(tile_az, tile, u, weight_x, rim_x, weight_y, flux_x, flux_rim, flux_y, left, right, out):
    step = min(tile_az, 32)
    for r in range(0, tile_az, step):
        rs = slice(r, r + step)
        b = HALO + r
        x = u[b : b + step, :]
        l = None if left is None else spread_groups(left, r // 8, step // 8, 0)
        flux_x[rs, :] = weight_x[rs, :] * (x - shifted_right(x, l))
        edge_x = x[:, tile - LANES :]
        if right is None:
            flux_rim[rs, :] = -rim_x[rs, :] * edge_x
        else:
            flux_rim[rs, :] = rim_x[rs, :] * (spread_groups(right, r // 8, step // 8, LANES - 1) - edge_x)
        flux_y[rs, :] = weight_y[rs, :] * (x - u[b - 1 : b - 1 + step, :])
    b = HALO + tile_az
    flux_y[tile_az : tile_az + 1, :] = weight_y[tile_az : tile_az + 1, :] * (u[b : b + 1, :] - u[b - 1 : b, :])
    for r in range(0, tile_az, step):
        out[r : r + step, :] = DAMPING * u[HALO + r : HALO + r + step, :] + divergence(
            tile_az, step, flux_x, flux_rim, flux_y, r
        )


def inner(a, b, tile_az, offset_a=0, offset_b=0):
    total = jnp.zeros((32, a.shape[1]), jnp.float32)
    for r in range(0, tile_az, 32):
        total = total + a[offset_a + r : offset_a + r + 32, :] * b[offset_b + r : offset_b + r + 32, :]
    return jnp.sum(jnp.sum(total, axis=0, keepdims=True), axis=1, keepdims=True)


def second_kernel(
    tile_az, tile, ids, residual, shaped, weight_x, rim_x, weight_y, row_pair, row_next, col_pair, col_next, *rest
):
    tables, inverse = rest[:2], rest[2]
    operated, shaped2, operated2, chunk = rest[3:7]
    u, flux_x, flux_rim, flux_y = rest[7:]
    pairs = table_pairs(tables)
    row_odd, col_odd = ids[5] == 1, ids[4] == 1
    up = jnp.where(row_odd, row_pair[0:2, :], row_next[0:2, :])
    down = jnp.where(row_odd, row_next[0:2, :], row_pair[0:2, :])
    left = jnp.where(col_odd, col_pair[...], col_next[...])
    right = jnp.where(col_odd, col_next[...], col_pair[...])
    u[HALO : HALO + tile_az, :] = shaped[...]
    for h in range(tile // LANES):
        cs = slice(h * LANES, (h + 1) * LANES)
        u[HALO - 1 : HALO, cs] = up[h : h + 1, :]
        u[HALO + tile_az : HALO + tile_az + 1, cs] = down[h : h + 1, :]
    apply_operator(
        tile_az, tile, u, weight_x, rim_x, weight_y, flux_x, flux_rim, flux_y, left, right, operated
    )
    image = precondition(operated[...], pairs, inverse)
    shaped2[...] = image
    u[HALO : HALO + tile_az, :] = image
    zero = jnp.zeros((1, tile), jnp.float32)
    u[HALO - 1 : HALO, :] = zero
    u[HALO + tile_az : HALO + tile_az + 1, :] = zero
    apply_operator(
        tile_az, tile, u, weight_x, rim_x, weight_y, flux_x, flux_rim, flux_y, None, None, operated2
    )
    lane = lanes_of((1, LANES))
    sums = jnp.zeros((1, LANES), jnp.float32)
    for i, (a, b) in enumerate(
        (
            (residual, shaped),
            (shaped, operated),
            (residual, shaped2),
            (operated, shaped2),
            (shaped2, operated2),
        )
    ):
        sums = jnp.where(lane == i, inner(a, b, tile_az), sums)
    chunk[8:16, :] = jnp.broadcast_to(sums, (8, LANES))
    top = jnp.sqrt(weight_y[0:1, :]) * shaped2[0:1, :]
    bottom = jnp.sqrt(weight_y[tile_az : tile_az + 1, :]) * shaped2[tile_az - 1 : tile_az, :]
    for h in range(tile // LANES):
        cs = slice(h * LANES, (h + 1) * LANES)
        chunk[8 + 2 + h : 8 + 3 + h, :] = top[:, cs]
        chunk[8 + 4 + h : 8 + 5 + h, :] = bottom[:, cs]
    half = tile_az // 8
    left_rim = jnp.sqrt(line_groups(weight_x, tile_az, 0)) * line_groups(shaped2, tile_az, 0)
    right_rim = jnp.sqrt(line_groups(rim_x, tile_az, LANES - 1)) * line_groups(shaped2, tile_az, tile - 1)
    wide = lanes_of((8, LANES))
    chunk[0:8, :] = jnp.where(wide < half, left_rim, pltpu.roll(right_rim, half, 1))


def last_kernel(
    tile_az, tile, rows, columns, ids, gathered, residual, shaped, operated, shaped2, operated2, weight_x, rim_x,
    weight_y, solution_out, residual_out
):
    half = tile_az // 8
    lane = lanes_of((8, LANES))
    total = jnp.zeros((8, LANES), jnp.float32)
    cross_x = jnp.zeros((8, LANES), jnp.float32)
    cross_y = jnp.zeros((2, LANES), jnp.float32)
    for r in range(rows):
        for c in range(columns):
            i = r * columns + c
            total = total + gathered[i, 8:16, :]
            if c + 1 < columns:
                right = pltpu.roll(gathered[i, 0:8, :], LANES - half, 1)
                cross_x = cross_x + right * gathered[i + 1, 0:8, :]
            if r + 1 < rows:
                cross_y = cross_y + gathered[i, 12:14, :] * gathered[i + columns, 10:12, :]
    cross = jnp.sum(jnp.where(lane < half, cross_x, 0.0), keepdims=True) + jnp.sum(cross_y, keepdims=True)
    wide = total[0:1, :]
    first_lane = lanes_of((1, LANES))
    pick = [
        jnp.sum(jnp.where(first_lane == i, wide, 0.0), axis=1, keepdims=True) for i in range(5)
    ]
    dot0, curve0, mixed, cross_dot, curve2 = pick
    curve2 = curve2 - 2.0 * cross
    alpha = dot0 / curve0
    fresh = dot0 - alpha * (mixed + curve0) + alpha * alpha * cross_dot
    beta = fresh / dot0
    grown = 1.0 + beta
    curve1 = grown * grown * curve0 - 2.0 * alpha * grown * cross_dot + alpha * alpha * curve2
    step1 = fresh / curve1
    on_first = alpha + step1 * grown
    on_second = step1 * alpha

    row, col = ids[0], ids[1]
    here = row * columns + col

    def neighbour(ok, index):
        return jnp.where(ok, index, here), jnp.where(ok, 1.0, 0.0).astype(jnp.float32)

    up, up_ok = neighbour(row > 0, here - columns)
    down, down_ok = neighbour(row < rows - 1, here + columns)
    left, left_ok = neighbour(col > 0, here - 1)
    right, right_ok = neighbour(col < columns - 1, here + 1)
    from_left = pltpu.roll(gathered[left, 0:8, :], LANES - half, 1) * left_ok
    from_right = gathered[right, 0:8, :] * right_ok
    top = jnp.concatenate([gathered[up, 12 + h : 13 + h, :] for h in range(tile // LANES)], axis=1) * up_ok
    bottom = jnp.concatenate([gathered[down, 10 + h : 11 + h, :] for h in range(tile // LANES)], axis=1) * down_ok
    top = top * jnp.sqrt(weight_y[0:1, :])
    bottom = bottom * jnp.sqrt(weight_y[tile_az : tile_az + 1, :])
    from_left = from_left * jnp.sqrt(line_groups(weight_x, tile_az, 0))
    from_right = from_right * jnp.sqrt(line_groups(rim_x, tile_az, LANES - 1))
    step = min(tile_az, 32)
    for r in range(0, tile_az, step):
        rs = slice(r, r + step)
        solution_out[rs, :] = on_first * shaped[rs, :] - on_second * shaped2[rs, :]
        q = operated2[rs, :]
        wide = lanes_of((step, tile))
        l = jnp.concatenate([spread_groups(from_left, r // 8, step // 8, 0)] * (tile // LANES), axis=1)
        q = q - jnp.where(wide == 0, l, 0.0)
        l = jnp.concatenate([spread_groups(from_right, r // 8, step // 8, LANES - 1)] * (tile // LANES), axis=1)
        q = q - jnp.where(wide == tile - 1, l, 0.0)
        deep = lax.broadcasted_iota(jnp.int32, (step, tile), 0)
        if r == 0:
            q = q - jnp.where(deep == 0, jnp.broadcast_to(top, (step, tile)), 0.0)
        if r + step == tile_az:
            q = q - jnp.where(deep == step - 1, jnp.broadcast_to(bottom, (step, tile)), 0.0)
        residual_out[rs, :] = residual[rs, :] - on_first * operated[rs, :] + on_second * q


def swapped(value, axis, count, step):
    if step == 0:
        pairs = [(i, i ^ 1) for i in range(count)]
    else:
        pairs = [(i, (i + 1 if i % 2 else i - 1) % count) for i in range(count)]
    return lax.ppermute(value, axis, pairs)


def shards(rows, columns, first_slc, second_slc):
    lines, width = first_slc.shape[1:]
    tile = width // columns
    tile_az = lines * columns
    axes = ("row", "col")
    exchange = "permute" if lines >= 4 * EDGE and columns <= 8 else "all_to_all"
    row, col = lax.axis_index("row"), lax.axis_index("col")
    ids = jnp.stack([row, col, row * columns + col, jnp.int32(rows * columns), col % 2, row % 2]).astype(jnp.int32)
    f32, bf16 = jnp.float32, jnp.bfloat16

    head = jnp.concatenate([first_slc[:, :HALO], second_slc[:, :HALO]], 0)
    tail = jnp.concatenate([first_slc[:, -HALO:], second_slc[:, -HALO:]], 0)
    odd = col % 2 == 1
    from_pair = swapped(jnp.where(odd, head, tail), axes, rows * columns, 0)
    from_next = swapped(jnp.where(odd, tail, head), axes, rows * columns, 1)
    wide = width + 2 * LANES
    if exchange == "permute":
        ranged, codes, rims = interior(
            functools.partial(interior_kernel, lines, width, tile, columns),
            [((4, lines, wide), f32), ((3, lines - 2 * EDGE, width), bf16), ((columns, 8, LANES), f32)],
            (first_slc, second_slc),
            [
                pltpu.VMEM((2, 2, lines, width), bf16),
                pltpu.VMEM((4, 16, wide), f32),
                pltpu.VMEM((2, lines - 2 * EDGE, wide), f32),
                pltpu.SemaphoreType.DMA((lines // 8,)),
            ],
        )
        half = columns // 2
        span = half * tile + 2 * LANES
        sent = [None] * columns
        for across in (True, False):
            part = call(
                functools.partial(border_kernel, lines, width, tile, columns, across),
                [((3 * lines + 16, tile), bf16)] * half,
                (ids, ranged, codes, rims, from_pair, from_next),
                [
                    pltpu.VMEM((4, HALO, width + 4 * LANES), f32),
                    pltpu.VMEM((2, 4, EDGE + 2 * HALO, span), f32),
                    pltpu.VMEM((2, 2 * EDGE, span), f32),
                    pltpu.VMEM((8, span), f32),
                ],
                "borders",
            )
            for i, value in enumerate(part):
                sent[i + (half if across else 0)] = value
        arrived = [sent[0]] + [
            lax.ppermute(sent[s], "col", [(i, i ^ s) for i in range(columns)]) for s in range(1, columns)
        ]
    else:
        above = jnp.where(odd, from_pair, from_next)
        below = jnp.where(odd, from_next, from_pair)
        height = lines + 2 * HALO
        sent = call(
            functools.partial(strip_kernel, lines, width, tile, columns, exchange),
            [((columns, 2 * lines + 8, tile), f32)],
            (ids, first_slc, second_slc, above, below),
            [pltpu.VMEM((4, height, wide), f32), pltpu.VMEM((4, height, width), f32), pltpu.VMEM((2, lines, wide), f32)],
            "strips",
        )
        arrived = [lax.all_to_all(sent[0], "col", 0, 0, tiled=True)]

    tables = []
    for table in (cosine_table(tile_az), cosine_table(tile)):
        parts = [*two_parts(table), *two_parts(table.T)]
        tables.append(jnp.asarray(np.concatenate(parts, axis=0)))
    inverse = jnp.asarray(inverse_eigen(tile_az, tile))

    whole = ((tile_az, tile), f32)
    block = ((8, LANES), f32)
    padded = pltpu.VMEM((tile_az + 2 * HALO, tile), f32)
    fluxes = [
        pltpu.VMEM((tile_az, tile), f32),
        pltpu.VMEM((tile_az, LANES), f32),
        pltpu.VMEM((tile_az + 8, tile), f32),
    ]
    residual, shaped, weight_x, rim_x, weight_y, row_pair, row_next, col_pair, col_next = call(
        functools.partial(tile_kernel, lines, tile_az, tile, columns, exchange),
        [whole, whole, whole, ((tile_az, LANES), f32), ((tile_az + 8, tile), f32), block, block, block, block],
        (ids, *arrived, *tables, inverse),
        [padded, padded, pltpu.VMEM((8 * columns, LANES), f32), pltpu.VMEM((8 * columns, LANES), f32), *fluxes],
        "tiles",
    )
    rims = (
        swapped(row_pair, "row", rows, 0),
        swapped(row_next, "row", rows, 1),
        swapped(col_pair, "col", columns, 0),
        swapped(col_next, "col", columns, 1),
    )
    operated, shaped2, operated2, chunk = call(
        functools.partial(second_kernel, tile_az, tile),
        [whole, whole, whole, ((16, LANES), f32)],
        (ids, residual, shaped, weight_x, rim_x, weight_y, *rims, *tables, inverse),
        [padded, *fluxes],
        "operator",
    )
    spread = jnp.broadcast_to(chunk[None], (rows * columns, 16, LANES))
    gathered = lax.all_to_all(spread, axes, 0, 0, tiled=True)
    return tuple(
        call(
            functools.partial(last_kernel, tile_az, tile, rows, columns),
            [whole, whole],
            (ids, gathered, residual, shaped, operated, shaped2, operated2, weight_x, rim_x, weight_y),
            [],
            "finish",
        )
    )


def solution(mesh):
    placed = P(None, ("row", "col"), None)
    return jax.shard_map(
        functools.partial(shards, mesh.shape["row"], mesh.shape["col"]),
        mesh=mesh,
        in_specs=(placed, placed),
        out_specs=(P("row", "col"), P("row", "col")),
        check_vma=False,
    )
```

```python
import functools
import math

import jax
import jax.numpy as jnp
import ml_dtypes
import numpy as np
from jax import lax
from jax.experimental import pallas as pl
from jax.experimental.pallas import tpu as pltpu
from jax.sharding import PartitionSpec as P

EPS = 1e-05
DAMPING = 0.0001
RADIUS = 4
LANES = 128
HALO = 8
EDGE = 16
TURN = 2.0 * math.pi
CODE_SPAN = 248.0
POWER_BASE = 2.0**7.5
TINY = 1e-30
SCALE_LANE = 5
VMEM_LIMIT = 40 * 1024 * 1024

ATAN = (
    0.1591549409219458,
    -0.05305126669892651,
    0.03181993346630217,
    -0.022611352052724496,
    0.016957432021882463,
    -0.011990188139443825,
    0.0068498925926071,
    -0.002591499099089036,
    0.00046210915702298266,
)
COS = (
    0.9999999997806517,
    -4.934802137228286,
    4.0587091643402005,
    -1.3352120566397616,
    0.23493755882899706,
    -0.024396716411350872,
)


def taps():
    offsets = np.arange(-RADIUS, RADIUS + 1).astype(np.float64)
    weights = np.exp(-offsets * offsets / 8.0)
    weights = weights / weights.sum()
    return [float(weights[RADIUS + j]) for j in range(RADIUS + 1)]


def cosine_table(count):
    j = np.arange(count)[:, None].astype(np.float64)
    i = np.arange(count)[None, :].astype(np.float64)
    table = np.cos(np.pi * j * (i + 0.5) / count) * np.sqrt(2.0 / count)
    table[0] = np.sqrt(1.0 / count)
    return table


def two_parts(table):
    table = table.astype(np.float32)
    high = table.astype(ml_dtypes.bfloat16)
    low = (table - high.astype(np.float32)).astype(ml_dtypes.bfloat16)
    return np.ascontiguousarray(high), np.ascontiguousarray(low)


def inverse_eigen(count_az, count_rg):
    along_az = 2.0 - 2.0 * np.cos(np.pi * np.arange(count_az) / count_az)
    along_rg = 2.0 - 2.0 * np.cos(np.pi * np.arange(count_rg) / count_rg)
    return (1.0 / (DAMPING + along_az[:, None] + along_rg[None, :])).astype(np.float32)


def poly(coefficients, y):
    value = jnp.full_like(y, coefficients[-1])
    for c in coefficients[-2::-1]:
        value = value * y + c
    return value


def angle_turns(im, re):
    a, b = jnp.abs(im), jnp.abs(re)
    big, small = jnp.maximum(a, b), jnp.minimum(a, b)
    t = small / jnp.maximum(big, 1e-37)
    p = t * poly(ATAN, t * t)
    p = jnp.where(a > b, 0.25 - p, p)
    p = jnp.where(re < 0.0, 0.5 - p, p)
    return jnp.where(im < 0.0, -p, p)


def edge(phase_p, gain_p, phase_q, gain_q):
    delta = phase_q - phase_p
    delta = delta - jnp.round(delta)
    half = gain_p * gain_q * poly(COS, delta * delta)
    weight = half * half
    return weight, weight * delta


def encode_gain(value):
    return jnp.exp2(value * CODE_SPAN - 0.5 * CODE_SPAN).astype(jnp.bfloat16)


def decode_gain(code):
    return (jnp.log2(code.astype(jnp.float32)) + 0.5 * CODE_SPAN) * (1.0 / CODE_SPAN)


def encode_power(value, scale):
    share = jnp.minimum(jnp.abs(value) / jnp.maximum(scale, TINY), 1.0) * POWER_BASE
    for _ in range(4):
        share = share * share
    return jnp.where(value < 0.0, -share, share)


def decode_power(code, scale):
    share = jnp.abs(code)
    for _ in range(4):
        share = jnp.sqrt(share)
    share = share * (scale * (1.0 / POWER_BASE))
    return jnp.where(code < 0.0, -share, share)


def split(value):
    high = value.astype(jnp.bfloat16)
    return high, (value - high.astype(jnp.float32)).astype(jnp.bfloat16)


def dot3(a, b):
    f = functools.partial(jnp.dot, preferred_element_type=jnp.float32)
    return f(a[0], b[1]) + f(a[1], b[0]) + f(a[0], b[0])


def lanes_of(shape):
    return lax.broadcasted_iota(jnp.int32, shape, 1)


def call(body, outs, args, scratch, name, smem_first=True, flops=1000000, out_space=pltpu.VMEM):
    specs = [pl.BlockSpec(memory_space=pltpu.VMEM)] * len(args)
    if smem_first:
        specs[0] = pl.BlockSpec(memory_space=pltpu.SMEM)
    return pl.pallas_call(
        body,
        out_shape=[jax.ShapeDtypeStruct(s, d) for s, d in outs],
        in_specs=specs,
        out_specs=[pl.BlockSpec(memory_space=out_space)] * len(outs),
        scratch_shapes=scratch,
        compiler_params=pltpu.CompilerParams(vmem_limit_bytes=VMEM_LIMIT),
        cost_estimate=pl.CostEstimate(flops=flops, bytes_accessed=4000000, transcendentals=0),
        name=name,
    )(*args)


def interior(body, outs, args, scratch):
    return pl.pallas_call(
        body,
        out_shape=[jax.ShapeDtypeStruct(s, d) for s, d in outs],
        in_specs=[pl.BlockSpec(memory_space=pltpu.SMEM)] + [pl.BlockSpec(memory_space=pltpu.HBM)] * 2,
        out_specs=[pl.BlockSpec(memory_space=pltpu.VMEM)] * len(outs),
        scratch_shapes=scratch,
        compiler_params=pltpu.CompilerParams(vmem_limit_bytes=VMEM_LIMIT),
        cost_estimate=pl.CostEstimate(flops=8000000, bytes_accessed=4000000, transcendentals=0),
        name="interior",
    )(*args)


def phase_gain(smoothed):
    re, im, one, two = smoothed
    gain = jnp.sqrt(re * re + im * im) / (jnp.sqrt(one * two) + EPS)
    return angle_turns(im, re), jnp.sqrt(gain)


def products(ar, ai, br, bi, scale=None):
    ar, ai, br, bi = (v.astype(jnp.float32) for v in (ar, ai, br, bi))
    if scale is not None:
        ar, ai, br, bi = (v * scale for v in (ar, ai, br, bi))
    return (ar * br + ai * bi, ai * br - ar * bi, ar * ar + ai * ai, br * br + bi * bi)


def along_range(x):
    k = taps()
    n = x.shape[1]
    total = k[0] * x
    for j in range(1, RADIUS + 1):
        total = total + k[j] * (pltpu.roll(x, j, 1) + pltpu.roll(x, n - j, 1))
    return total


def along_azimuth(ref, f, row, rows, cs):
    k = taps()
    total = k[0] * ref[f, row : row + rows, cs]
    for j in range(1, RADIUS + 1):
        total = total + k[j] * (ref[f, row - j : row - j + rows, cs] + ref[f, row + j : row + j + rows, cs])
    return total


def end_weights(before):
    k = taps()
    sub = lax.broadcasted_iota(jnp.int32, (HALO, 1), 0)
    low = jnp.zeros((HALO, 1), jnp.float32)
    high = jnp.zeros((HALO, 1), jnp.float32)
    for j in range(RADIUS + 1):
        low = jnp.where(sub == (HALO - 1 - j if before else HALO - j), k[j], low)
        high = jnp.where(sub == (j - 1 if before else j), k[j], high)
    return low, high


def first_of_half(own, half, across):
    return (own & half) ^ (half if across else 0)


def window(lines, width, tile, columns, across, own, rows):
    half = columns // 2
    span = half * tile + 2 * LANES
    first_tile = first_of_half(own, half, across)
    start = pl.multiple_of(first_tile * tile, LANES)
    pixel = lanes_of((rows, span)) + (start - LANES)
    return first_tile, start, span, jnp.logical_and(pixel >= 0, pixel < width)


def interior_kernel(lines, width, tile, columns, across, ids, first, second, ranged, codes, rims, raw, prod, field, sems):
    half = columns // 2
    chunk = 16
    first_tile, start, span, in_image = window(lines, width, tile, columns, across, ids[1], 8)
    upper = jnp.where(first_tile == 0, 0, 1)
    source = pl.multiple_of(upper * (width // 2 - 2 * LANES), LANES)
    target = pl.multiple_of((1 - upper) * 2 * LANES, LANES)
    size = width // 2 + 2 * LANES
    blank = pl.multiple_of(upper * size, LANES)
    copies = []
    for i in range(lines // chunk):
        rs = pl.ds(i * chunk, chunk)
        for a, ref in enumerate((first, second)):
            copy = pltpu.make_async_copy(
                ref.at[:, rs, pl.ds(source, size)], raw.at[a, :, rs, pl.ds(target, size)], sems.at[2 * i + a]
            )
            copy.start()
            copies.append(copy)
    for a in range(2):
        for part in range(2):
            raw[a, part, :, pl.ds(blank, 2 * LANES)] = jnp.zeros((lines, 2 * LANES), jnp.bfloat16)
    for i in range(lines // chunk):
        copies[2 * i].wait()
        copies[2 * i + 1].wait()
        rs = slice(i * chunk, (i + 1) * chunk)
        for c in range(0, span + 2 * LANES, 512):
            cs = slice(c, c + 512)
            values = products(raw[0, 0, rs, cs], raw[0, 1, rs, cs], raw[1, 0, rs, cs], raw[1, 1, rs, cs])
            for f in range(4):
                prod[f, :, cs] = values[f]
        for f in range(4):
            for r in range(0, chunk, 8):
                total = along_range(prod[f, r : r + 8, :])[:, LANES : LANES + span]
                row = i * chunk + r
                ranged[f, row : row + 8, :] = jnp.where(in_image, total, 0.0)
    inner = lines - 2 * EDGE
    for c in range(0, span, LANES):
        cs = slice(c, c + LANES)
        for r in range(0, inner, 16):
            smoothed = [along_azimuth(ranged, f, EDGE + r, 16, cs) for f in range(4)]
            phase, gain = phase_gain(smoothed)
            field[0, r : r + 16, cs] = phase
            field[1, r : r + 16, cs] = gain
            codes[0, r : r + 16, cs], codes[1, r : r + 16, cs] = split(phase)
            codes[2, r : r + 16, cs] = encode_gain(gain)
    groups = lines // 8
    for t in range(half):
        rims[t] = rim_block(field, groups, range(EDGE // 8, (lines - EDGE) // 8), EDGE // 8, t * tile, tile, None)


def rim_block(field, groups, which, first_group, start, tile, block, hint=None):
    lane = lanes_of((8, LANES))
    if block is None:
        block = jnp.zeros((8, LANES), jnp.float32)
    for f in range(2):
        for side in range(2):
            offset = start if side == 0 else start + LANES + tile
            at = slice(offset, offset + LANES) if hint is None else pl.ds(hint(offset, LANES), LANES)
            for g in which:
                target = (f * 2 + side) * groups + g
                row = 8 * (g - first_group)
                x = field[f, row : row + 8, at]
                shift = (target - (LANES - 1 if side == 0 else 0)) % LANES
                if shift:
                    x = pltpu.roll(x, shift, 1)
                block = jnp.where(lane == target, x, block)
    return block


def border_kernel(lines, width, tile, columns, across, ids, ranged, codes, rims, from_pair, from_next, *rest):
    half = columns // 2
    outs, (prod, seg, field, ends) = rest[:half], rest[half:]
    own = ids[1]
    odd = ids[4]
    first_tile, start, span, in_image = window(lines, width, tile, columns, across, own, HALO)
    inside = (
        jnp.where(ids[2] == 0, 0.0, 1.0).astype(jnp.float32),
        jnp.where(ids[2] == ids[3] - 1, 0.0, 1.0).astype(jnp.float32),
    )
    zero = jnp.zeros((HALO, 2 * LANES), jnp.float32)
    own_rows = EDGE + HALO
    for e in range(2):
        flag = odd if e == 0 else 1 - odd
        keep = flag.astype(jnp.float32)
        for f in range(4):
            prod[f, :, 0 : 2 * LANES] = zero
            prod[f, :, 2 * LANES + width :] = zero
        for c in range(0, width, 512):
            cs = slice(c, c + 512)
            parts = [
                from_pair[i, :, cs].astype(jnp.float32) * keep + from_next[i, :, cs].astype(jnp.float32) * (1.0 - keep)
                for i in range(4)
            ]
            values = products(*parts, inside[e])
            for f in range(4):
                prod[f, :, 2 * LANES + c : 2 * LANES + c + 512] = values[f]
        for f in range(4):
            total = along_range(prod[f, :, pl.ds(start, span + 2 * LANES)])[:, LANES : LANES + span]
            total = jnp.where(in_image, total, 0.0)
            if e == 0:
                seg[e, f, 0:HALO, :] = total
                seg[e, f, HALO:, :] = ranged[f, 0:own_rows, :]
            else:
                seg[e, f, own_rows:, :] = total
                seg[e, f, 0:own_rows, :] = ranged[f, lines - own_rows :, :]
    for e in range(2):
        ref = seg.at[e]
        for c in range(0, span, LANES):
            cs = slice(c, c + LANES)
            smoothed = [along_azimuth(ref, f, HALO, EDGE, cs) for f in range(4)]
            phase, gain = phase_gain(smoothed)
            field[0, e * EDGE : (e + 1) * EDGE, cs] = phase
            field[1, e * EDGE : (e + 1) * EDGE, cs] = gain
        low, high = end_weights(e == 0)
        r = 0 if e == 0 else own_rows - HALO
        smoothed = [
            jnp.sum(low * ref[f, r : r + HALO, :] + high * ref[f, r + HALO : r + 2 * HALO, :], axis=0, keepdims=True)
            for f in range(4)
        ]
        phase, gain = phase_gain(smoothed)
        ends[e : e + 1, :] = phase
        ends[2 + e : 3 + e, :] = gain * inside[e]
    groups = lines // 8
    edge_groups = EDGE // 8
    inner = lines - 2 * EDGE
    for n, s in enumerate(range(half, columns) if across else range(half)):
        out = outs[n]
        target = own ^ s
        local = pl.multiple_of((target - first_tile) * tile, LANES)
        cs = pl.ds(pl.multiple_of(local + LANES, LANES), tile)
        for i in range(3):
            out[i * lines + EDGE : i * lines + EDGE + inner, :] = codes[i, :, cs]
        for e in range(2):
            row = 0 if e == 0 else lines - EDGE
            rs = slice(e * EDGE, (e + 1) * EDGE)
            out[row : row + EDGE, :], out[lines + row : lines + row + EDGE, :] = split(field[0, rs, cs])
            out[2 * lines + row : 2 * lines + row + EDGE, :] = encode_gain(field[1, rs, cs])
        block = rims[target - first_tile]
        block = rim_block(field, groups, range(edge_groups), 0, local, tile, block, pl.multiple_of)
        block = rim_block(
            field, groups, range(groups - edge_groups, groups), groups - 2 * edge_groups, local, tile, block,
            pl.multiple_of,
        )
        rows = []
        for i in range(4):
            for h in range(tile // LANES):
                rows.append(ends[i : i + 1, pl.ds(pl.multiple_of(local + (h + 1) * LANES, LANES), LANES)])
        block = jnp.concatenate([block, jnp.concatenate(rows, axis=0)], axis=1)
        out[3 * lines :, :] = jnp.concatenate(split(block), axis=0)


def strip_kernel(lines, width, tile, columns, exchange, ids, first, second, above, below, *rest):
    n_out = len(rest) - 3
    outs, (prod, ranged, field) = rest[:n_out], rest[n_out:]
    k = taps()
    own = ids[1]
    inside_above = jnp.where(ids[2] == 0, 0.0, 1.0).astype(jnp.float32)
    inside_below = jnp.where(ids[2] == ids[3] - 1, 0.0, 1.0).astype(jnp.float32)
    height = lines + 2 * HALO

    zero = jnp.zeros((height, LANES), jnp.float32)
    for f in range(4):
        prod[f, :, 0:LANES] = zero
        prod[f, :, LANES + width :] = zero
    step = min(width, 512)
    for c in range(0, width, step):
        at = slice(LANES + c, LANES + c + step)
        cs = slice(c, c + step)
        rows = min(lines, 16)
        for r in range(0, lines, rows):
            rs = slice(r, r + rows)
            values = products(first[0, rs, cs], first[1, rs, cs], second[0, rs, cs], second[1, rs, cs])
            for f in range(4):
                prod[f, HALO + r : HALO + r + rows, at] = values[f]
        for ref, r, scale in ((above, 0, inside_above), (below, HALO + lines, inside_below)):
            values = products(ref[0, :, cs], ref[1, :, cs], ref[2, :, cs], ref[3, :, cs], scale)
            for f in range(4):
                prod[f, r : r + HALO, at] = values[f]

    step = min(width, 1024)
    for f in range(4):
        for r in range(0, height, 8):
            for c in range(0, width, step):
                x = prod[f, r : r + 8, c : c + step + 2 * LANES]
                n = step + 2 * LANES
                total = k[0] * x
                for j in range(1, RADIUS + 1):
                    total = total + k[j] * (pltpu.roll(x, j, 1) + pltpu.roll(x, n - j, 1))
                ranged[f, r : r + 8, c : c + step] = total[:, LANES : LANES + step]

    for f in range(2):
        field[f, :, 0:LANES] = zero[:lines]
        field[f, :, LANES + width :] = zero[:lines]
    rows = min(lines, 32)
    sub = lax.broadcasted_iota(jnp.int32, (HALO, 1), 0)
    low = jnp.zeros((HALO, 1), jnp.float32)
    high = jnp.zeros((HALO, 1), jnp.float32)
    for j in range(RADIUS + 1):
        low = jnp.where(sub == HALO - 1 - j, k[j], low)
        high = jnp.where(sub == j - 1, k[j], high)
    top, bottom = [], []
    for c in range(0, width, LANES):
        cs = slice(c, c + LANES)
        for r in range(0, lines, rows):
            smoothed = []
            for f in range(4):
                b = HALO + r
                total = k[0] * ranged[f, b : b + rows, cs]
                for j in range(1, RADIUS + 1):
                    total = total + k[j] * (
                        ranged[f, b - j : b - j + rows, cs] + ranged[f, b + j : b + j + rows, cs]
                    )
                smoothed.append(total)
            phase, gain = phase_gain(smoothed)
            field[0, r : r + rows, LANES + c : 2 * LANES + c] = phase
            field[1, r : r + rows, LANES + c : 2 * LANES + c] = gain

    step = min(width, 1024)
    low = low + jnp.zeros((HALO, step), jnp.float32)
    high = high + jnp.zeros((HALO, step), jnp.float32)
    mirror_low = jnp.zeros((HALO, 1), jnp.float32)
    mirror_high = jnp.zeros((HALO, 1), jnp.float32)
    for j in range(RADIUS + 1):
        mirror_high = jnp.where(sub == j, k[j], mirror_high)
        mirror_low = jnp.where(sub == HALO - j, k[j], mirror_low)
    ends = []
    for c in range(0, width, step):
        cs = slice(c, c + step)
        up = [
            jnp.sum(low * ranged[f, 0:HALO, cs] + high * ranged[f, HALO : 2 * HALO, cs], axis=0, keepdims=True)
            for f in range(4)
        ]
        down = [
            jnp.sum(
                mirror_low * ranged[f, lines : lines + HALO, cs]
                + mirror_high * ranged[f, lines + HALO : lines + 2 * HALO, cs],
                axis=0,
                keepdims=True,
            )
            for f in range(4)
        ]
        up_phase, up_gain = phase_gain(up)
        down_phase, down_gain = phase_gain(down)
        ends.append((up_phase, down_phase, up_gain * inside_above, down_gain * inside_below))
    for i, (a, b, c_, d) in enumerate(ends):
        at = slice(i * step, (i + 1) * step)
        prod[0, 0:1, at] = a
        prod[0, 1:2, at] = b
        prod[0, 2:3, at] = c_
        prod[0, 3:4, at] = d

    groups = lines // 8
    lane = lanes_of((8, LANES))

    def pack(out, start, aligned):
        hint = pl.multiple_of if aligned else (lambda v, _: v)
        out[0:lines, :] = field[0, :, pl.ds(hint(start + LANES, LANES), tile)]
        out[lines : 2 * lines, :] = field[1, :, pl.ds(hint(start + LANES, LANES), tile)]
        block = jnp.zeros((8, LANES), jnp.float32)
        for f in range(2):
            for side in range(2):
                offset = start if side == 0 else start + LANES + tile
                for g in range(groups):
                    target = (f * 2 + side) * groups + g
                    x = field[f, 8 * g : 8 * g + 8, pl.ds(hint(offset, LANES), LANES)]
                    shift = (target - (LANES - 1 if side == 0 else 0)) % LANES
                    if shift:
                        x = pltpu.roll(x, shift, 1)
                    block = jnp.where(lane == target, x, block)
        base = 2 * lines
        out[base : base + 8, 0:LANES] = block
        for i in range(4):
            for h in range(tile // LANES):
                out[base + 2 * i + h : base + 2 * i + h + 1, LANES : 2 * LANES] = prod[
                    0, i : i + 1, pl.ds(hint(start + h * LANES, LANES), LANES)
                ]

    if exchange == "permute":
        for s in range(columns):
            pack(outs[s], (own ^ s) * tile, True)
    else:
        for s in range(columns):
            pack(outs[0].at[s], s * tile, False)


def precondition(field, tables, inverse):
    az, az_t, rg, rg_t = tables
    coef = dot3(az, split(field))
    coef = dot3(split(coef), rg_t)
    coef = coef * inverse[...]
    back = dot3(az_t, split(coef))
    return dot3(split(back), rg)


def table_pairs(tables):
    pairs = []
    for ref in tables:
        n = ref.shape[1]
        parts = [ref[i * n : (i + 1) * n, :] for i in range(4)]
        pairs += [(parts[0], parts[1]), (parts[2], parts[3])]
    return pairs


def line_groups(ref, tile_az, edge_lane):
    lane = lanes_of((8, LANES))
    first = (edge_lane // LANES) * LANES
    block = jnp.zeros((8, LANES), jnp.float32)
    for g in range(tile_az // 8):
        x = ref[8 * g : 8 * g + 8, first : first + LANES]
        shift = (g - edge_lane) % LANES
        if shift:
            x = pltpu.roll(x, shift, 1)
        block = jnp.where(lane == g, x, block)
    return block


def spread_groups(block, first_group, count, target_lane, base=0):
    parts = []
    for g in range(first_group, first_group + count):
        shift = (target_lane - (base + g)) % LANES
        parts.append(pltpu.roll(block, shift, 1) if shift else block)
    return jnp.concatenate(parts, axis=0) if count > 1 else parts[0]


def shifted_right(x, left):
    lane = lanes_of(x.shape)
    if left is None:
        return jnp.where(lane == 0, 0.0, pltpu.roll(x, 1, 1))
    wide = jnp.concatenate([left] * (x.shape[1] // LANES), axis=1)
    return jnp.where(lane == 0, wide, pltpu.roll(x, 1, 1))


def shifted_left(x, right):
    lane = lanes_of(x.shape)
    wide = jnp.concatenate([right] * (x.shape[1] // LANES), axis=1)
    return jnp.where(lane == x.shape[1] - 1, wide, pltpu.roll(x, x.shape[1] - 1, 1))


def divergence(tile_az, step, along_x, rim_x, along_y, r):
    rs = slice(r, r + step)
    x = along_x[rs, :]
    return (x - shifted_left(x, rim_x[rs, :])) + along_y[rs, :] - along_y[r + 1 : r + 1 + step, :]


def tile_kernel(lines, tile_az, tile, columns, exchange, ids, *rest):
    chunks = rest[: columns if exchange == "permute" else 1]
    rest = rest[len(chunks) :]
    tables, inverse = rest[:2], rest[2]
    residual, shaped, weight_x, rim_x, weight_y, row_pair, row_next, col_pair, col_next = rest[3:12]
    phase, gain, sides, ends, flux_x, flux_rim, flux_y = rest[12:]
    own = ids[1]
    pairs = table_pairs(tables)

    for s in range(columns):
        if exchange == "permute":
            src, strip = chunks[s], own ^ s
        else:
            src, strip = chunks[0].at[s], s
        row = strip * lines
        if exchange == "permute":
            row = pl.multiple_of(row, 8)
        at = pl.ds(pl.multiple_of(strip * 8, 8), 8) if exchange == "permute" else pl.ds(strip * 8, 8)
        if exchange == "permute":
            phase[pl.ds(HALO + row, lines), :] = src[0:lines, :].astype(jnp.float32) + src[
                lines : 2 * lines, :
            ].astype(jnp.float32)
            gain[pl.ds(HALO + row, lines), :] = decode_gain(src[2 * lines : 3 * lines, :])
            both = src[3 * lines :, :].astype(jnp.float32)
            block = both[0:8, :] + both[8:16, :]
        else:
            phase[pl.ds(HALO + row, lines), :] = src[0:lines, :]
            gain[pl.ds(HALO + row, lines), :] = src[lines : 2 * lines, :]
            block = src[2 * lines : 2 * lines + 8, :]
        sides[at, :] = block[:, 0:LANES]
        ends[at, :] = block[:, LANES : 2 * LANES]
    last = 8 * (columns - 1)
    for h in range(tile // LANES):
        cs = slice(h * LANES, (h + 1) * LANES)
        phase[HALO - 1 : HALO, cs] = ends[h : h + 1, :]
        gain[HALO - 1 : HALO, cs] = ends[4 + h : 5 + h, :]
        phase[HALO + tile_az : HALO + tile_az + 1, cs] = ends[last + 2 + h : last + 3 + h, :]
        gain[HALO + tile_az : HALO + tile_az + 1, cs] = ends[last + 6 + h : last + 7 + h, :]

    step = min(tile_az, 32)
    groups = lines // 8
    for r in range(0, tile_az, step):
        rs = slice(r, r + step)
        b = HALO + r
        p, g = phase[b : b + step, :], gain[b : b + step, :]
        halo = []
        for f in range(2):
            for side in range(2):
                parts = []
                for line_group in range(r // 8, (r + step) // 8):
                    strip, inner = divmod(line_group, groups)
                    block = sides[8 * strip : 8 * strip + 8, :]
                    source_lane = (f * 2 + side) * groups + inner
                    shift = ((0 if side == 0 else LANES - 1) - source_lane) % LANES
                    parts.append(pltpu.roll(block, shift, 1) if shift else block)
                halo.append(jnp.concatenate(parts, axis=0) if len(parts) > 1 else parts[0])
        w, f = edge(shifted_right(p, halo[0]), shifted_right(g, halo[2]), p, g)
        weight_x[rs, :] = w
        flux_x[rs, :] = f
        w, f = edge(p[:, tile - LANES :], g[:, tile - LANES :], halo[1], halo[3])
        rim_x[rs, :] = w
        flux_rim[rs, :] = f
        w, f = edge(phase[b - 1 : b - 1 + step, :], gain[b - 1 : b - 1 + step, :], p, g)
        weight_y[rs, :] = w
        flux_y[rs, :] = f
    b = HALO + tile_az
    w, f = edge(
        phase[b - 1 : b, :], gain[b - 1 : b, :], phase[b : b + 1, :], gain[b : b + 1, :]
    )
    weight_y[tile_az : tile_az + 8, :] = jnp.broadcast_to(w, (8, tile))
    flux_y[tile_az : tile_az + 8, :] = jnp.broadcast_to(f, (8, tile))

    for r in range(0, tile_az, step):
        residual[r : r + step, :] = TURN * divergence(tile_az, step, flux_x, flux_rim, flux_y, r)
    shaped[...] = precondition(residual[...], pairs, inverse)
    row_odd, col_odd = ids[5] == 1, ids[4] == 1
    top = jnp.concatenate([shaped[0:1, h : h + LANES] for h in range(0, tile, LANES)], axis=0)
    bottom = jnp.concatenate([shaped[tile_az - 1 : tile_az, h : h + LANES] for h in range(0, tile, LANES)], axis=0)
    row_pair[0:2, :] = jnp.where(row_odd, top, bottom)
    row_next[0:2, :] = jnp.where(row_odd, bottom, top)
    left = line_groups(shaped, tile_az, 0)
    right = line_groups(shaped, tile_az, tile - 1)
    col_pair[...] = jnp.where(col_odd, left, right)
    col_next[...] = jnp.where(col_odd, right, left)


def apply_operator(tile_az, tile, u, weight_x, rim_x, weight_y, flux_x, flux_rim, flux_y, left, right, out):
    step = min(tile_az, 32)
    for r in range(0, tile_az, step):
        rs = slice(r, r + step)
        b = HALO + r
        x = u[b : b + step, :]
        l = None if left is None else spread_groups(left, r // 8, step // 8, 0)
        flux_x[rs, :] = weight_x[rs, :] * (x - shifted_right(x, l))
        edge_x = x[:, tile - LANES :]
        if right is None:
            flux_rim[rs, :] = -rim_x[rs, :] * edge_x
        else:
            flux_rim[rs, :] = rim_x[rs, :] * (spread_groups(right, r // 8, step // 8, LANES - 1) - edge_x)
        flux_y[rs, :] = weight_y[rs, :] * (x - u[b - 1 : b - 1 + step, :])
    b = HALO + tile_az
    flux_y[tile_az : tile_az + 1, :] = weight_y[tile_az : tile_az + 1, :] * (u[b : b + 1, :] - u[b - 1 : b, :])
    for r in range(0, tile_az, step):
        out[r : r + step, :] = DAMPING * u[HALO + r : HALO + r + step, :] + divergence(
            tile_az, step, flux_x, flux_rim, flux_y, r
        )


def inner(a, b, tile_az, offset_a=0, offset_b=0):
    total = jnp.zeros((32, a.shape[1]), jnp.float32)
    for r in range(0, tile_az, 32):
        total = total + a[offset_a + r : offset_a + r + 32, :] * b[offset_b + r : offset_b + r + 32, :]
    return jnp.sum(jnp.sum(total, axis=0, keepdims=True), axis=1, keepdims=True)


def second_kernel(
    tile_az, tile, ids, residual, shaped, weight_x, rim_x, weight_y, row_pair, row_next, col_pair, col_next, *rest
):
    tables, inverse = rest[:2], rest[2]
    operated, shaped2, operated2, chunk, roots = rest[3:8]
    u, flux_x, flux_rim, flux_y = rest[8:]
    pairs = table_pairs(tables)
    row_odd, col_odd = ids[5] == 1, ids[4] == 1
    up = jnp.where(row_odd, row_pair[0:2, :], row_next[0:2, :])
    down = jnp.where(row_odd, row_next[0:2, :], row_pair[0:2, :])
    left = jnp.where(col_odd, col_pair[...], col_next[...])
    right = jnp.where(col_odd, col_next[...], col_pair[...])
    u[HALO : HALO + tile_az, :] = shaped[...]
    for h in range(tile // LANES):
        cs = slice(h * LANES, (h + 1) * LANES)
        u[HALO - 1 : HALO, cs] = up[h : h + 1, :]
        u[HALO + tile_az : HALO + tile_az + 1, cs] = down[h : h + 1, :]
    apply_operator(
        tile_az, tile, u, weight_x, rim_x, weight_y, flux_x, flux_rim, flux_y, left, right, operated
    )
    image = precondition(operated[...], pairs, inverse)
    shaped2[...] = image
    u[HALO : HALO + tile_az, :] = image
    apply_operator(
        tile_az, tile, u, weight_x, rim_x, weight_y, flux_x, flux_rim, flux_y, left, right, operated2
    )
    lane = lanes_of((1, LANES))
    sums = jnp.zeros((1, LANES), jnp.float32)
    for i, (a, b) in enumerate(
        (
            (residual, shaped),
            (shaped, operated),
            (residual, shaped2),
            (operated, shaped2),
            (shaped2, operated2),
        )
    ):
        sums = jnp.where(lane == i, inner(a, b, tile_az), sums)
    def rows_of(x):
        return jnp.concatenate([x[:, h : h + LANES] for h in range(0, tile, LANES)], axis=0)

    weight_t, weight_b = rows_of(weight_y[0:1, :]), rows_of(weight_y[tile_az : tile_az + 1, :])
    weight_l, weight_r = line_groups(weight_x, tile_az, 0), line_groups(rim_x, tile_az, LANES - 1)
    top = rows_of(image_row(shaped2, shaped, 0))
    bottom = rows_of(image_row(shaped2, shaped, tile_az - 1))
    left_rim = line_groups(shaped2, tile_az, 0) - line_groups(shaped, tile_az, 0)
    right_rim = line_groups(shaped2, tile_az, tile - 1) - line_groups(shaped, tile_az, tile - 1)
    known = jnp.sum(weight_t * up * top + weight_b * down * bottom, keepdims=True) + jnp.sum(
        weight_l * left * left_rim + weight_r * right * right_rim, keepdims=True
    )
    sums = jnp.where(lane == 4, sums - known, sums)
    half = tile_az // 8
    wide = lanes_of((8, LANES))
    root_sides = jnp.sqrt(jnp.where(wide < half, weight_l, pltpu.roll(weight_r, half, 1)))
    sides = root_sides * jnp.where(wide < half, left_rim, pltpu.roll(right_rim, half, 1))
    root_ends = jnp.sqrt(jnp.concatenate([weight_t, weight_b], axis=0))
    ends = root_ends * jnp.concatenate([top, bottom], axis=0)
    scale = jnp.maximum(jnp.max(jnp.abs(sides), keepdims=True), jnp.max(jnp.abs(ends), keepdims=True))
    scale = (scale * 1.01).astype(jnp.bfloat16).astype(jnp.float32)
    sums = jnp.where(lane == SCALE_LANE, scale, sums)
    high = sums.astype(jnp.bfloat16).astype(jnp.float32)
    middle = (sums - high).astype(jnp.bfloat16).astype(jnp.float32)
    rest_ = sums - high - middle
    sums = high + pltpu.roll(middle, 8, 1) + pltpu.roll(rest_, 16, 1)
    chunk[...] = jnp.concatenate(
        [encode_power(sides, scale), encode_power(ends, scale), jnp.broadcast_to(sums, (4, LANES))], axis=0
    ).astype(jnp.bfloat16)
    roots[...] = jnp.concatenate([root_sides, root_ends, root_ends], axis=0)


def image_row(a, b, row):
    return a[row : row + 1, :] - b[row : row + 1, :]


def last_kernel(
    tile_az, tile, rows, columns, ids, gathered, residual, shaped, operated, shaped2, operated2, roots,
    solution_hbm, residual_hbm, solution_out, residual_out, sems
):
    half = tile_az // 8
    lane = lanes_of((8, LANES))
    total = jnp.zeros((4, LANES), jnp.float32)
    cross_x = jnp.zeros((8, LANES), jnp.float32)
    cross_y = jnp.zeros((2, LANES), jnp.float32)
    values = {}

    def decoded(i):
        x = gathered[i].astype(jnp.float32)
        return jnp.concatenate([decode_power(x[0:12, :], x[12:13, SCALE_LANE : SCALE_LANE + 1]), x[12:16, :]], axis=0)

    def value_of(i):
        if i not in values:
            values[i] = decoded(i)
        return values[i]

    for r in range(rows):
        for c in range(columns):
            i = r * columns + c
            here = value_of(i)
            total = total + here[12:16, :]
            if c + 1 < columns:
                cross_x = cross_x + pltpu.roll(here[0:8, :], LANES - half, 1) * value_of(i + 1)[0:8, :]
            if r + 1 < rows:
                cross_y = cross_y + here[10:12, :] * value_of(i + columns)[8:10, :]
    cross = jnp.sum(jnp.where(lane < half, cross_x, 0.0), keepdims=True) + jnp.sum(cross_y, keepdims=True)
    wide = total[0:1, :]
    first_lane = lanes_of((1, LANES))
    pick = [
        jnp.sum(jnp.where(first_lane % 8 == i, jnp.where(first_lane < 24, wide, 0.0), 0.0), axis=1, keepdims=True)
        for i in range(5)
    ]
    dot0, curve0, mixed, cross_dot, curve2 = pick
    curve2 = curve2 - 2.0 * cross
    alpha = dot0 / curve0
    fresh = dot0 - alpha * (mixed + curve0) + alpha * alpha * cross_dot
    beta = fresh / dot0
    grown = 1.0 + beta
    curve1 = grown * grown * curve0 - 2.0 * alpha * grown * cross_dot + alpha * alpha * curve2
    step1 = fresh / curve1
    on_first = alpha + step1 * grown
    on_second = step1 * alpha

    row, col = ids[0], ids[1]
    here = row * columns + col

    def neighbour(ok, index):
        return jnp.where(ok, index, here), jnp.where(ok, 1.0, 0.0).astype(jnp.float32)

    up, up_ok = neighbour(row > 0, here - columns)
    down, down_ok = neighbour(row < rows - 1, here + columns)
    left, left_ok = neighbour(col > 0, here - 1)
    right, right_ok = neighbour(col < columns - 1, here + 1)
    near = [decoded(i) for i in (left, right, up, down)]
    from_left = pltpu.roll(near[0][0:8, :], LANES - half, 1) * left_ok
    from_right = pltpu.roll(near[1][0:8, :], half, 1) * right_ok
    top = jnp.concatenate([near[2][10 + h : 11 + h, :] for h in range(tile // LANES)], axis=1) * up_ok
    bottom = jnp.concatenate([near[3][8 + h : 9 + h, :] for h in range(tile // LANES)], axis=1) * down_ok
    top = top * jnp.concatenate([roots[8 + h : 9 + h, :] for h in range(tile // LANES)], axis=1)
    bottom = bottom * jnp.concatenate([roots[10 + h : 11 + h, :] for h in range(tile // LANES)], axis=1)
    from_left = from_left * roots[0:8, :]
    from_right = from_right * roots[0:8, :]
    step = min(tile_az, 64)
    copies = []
    for r in range(0, tile_az, step):
        rs = slice(r, r + step)
        solution_out[rs, :] = on_first * shaped[rs, :] - on_second * shaped2[rs, :]
        q = operated2[rs, :]
        wide = lanes_of((step, tile))
        l = jnp.concatenate([spread_groups(from_left, r // 8, step // 8, 0)] * (tile // LANES), axis=1)
        q = q - jnp.where(wide == 0, l, 0.0)
        l = jnp.concatenate([spread_groups(from_right, r // 8, step // 8, LANES - 1, half)] * (tile // LANES), axis=1)
        q = q - jnp.where(wide == tile - 1, l, 0.0)
        if r == 0 or r + step == tile_az:
            deep = lax.broadcasted_iota(jnp.int32, (step, tile), 0)
        if r == 0:
            q = q - jnp.where(deep == 0, jnp.broadcast_to(top, (step, tile)), 0.0)
        if r + step == tile_az:
            q = q - jnp.where(deep == step - 1, jnp.broadcast_to(bottom, (step, tile)), 0.0)
        residual_out[rs, :] = residual[rs, :] - on_first * operated[rs, :] + on_second * q
        for n, (src, dst) in enumerate(((solution_out, solution_hbm), (residual_out, residual_hbm))):
            copy = pltpu.make_async_copy(src.at[rs, :], dst.at[rs, :], sems.at[2 * (r // step) + n])
            copy.start()
            copies.append(copy)
    for copy in copies:
        copy.wait()


def swapped(value, axis, count, step):
    if step == 0:
        pairs = [(i, i ^ 1) for i in range(count)]
    else:
        pairs = [(i, (i + 1 if i % 2 else i - 1) % count) for i in range(count)]
    return lax.ppermute(value, axis, pairs)


def shards(rows, columns, first_slc, second_slc):
    lines, width = first_slc.shape[1:]
    tile = width // columns
    tile_az = lines * columns
    axes = ("row", "col")
    exchange = "permute" if lines >= 4 * EDGE and columns <= 8 else "all_to_all"
    row, col = lax.axis_index("row"), lax.axis_index("col")
    ids = jnp.stack([row, col, row * columns + col, jnp.int32(rows * columns), col % 2, row % 2]).astype(jnp.int32)
    f32, bf16 = jnp.float32, jnp.bfloat16

    head = jnp.concatenate([first_slc[:, :HALO], second_slc[:, :HALO]], 0)
    tail = jnp.concatenate([first_slc[:, -HALO:], second_slc[:, -HALO:]], 0)
    odd = col % 2 == 1
    from_pair = swapped(jnp.where(odd, head, tail), axes, rows * columns, 0)
    from_next = swapped(jnp.where(odd, tail, head), axes, rows * columns, 1)
    wide = width + 2 * LANES
    if exchange == "permute":
        half = columns // 2
        span = half * tile + 2 * LANES
        sent = [None] * columns
        sources = (first_slc, second_slc)
        for across in (True, False):
            ranged, codes, rims = interior(
                functools.partial(interior_kernel, lines, width, tile, columns, across),
                [((4, lines, span), f32), ((3, lines - 2 * EDGE, span), bf16), ((half, 8, LANES), f32)],
                (ids, *sources),
                [
                    pltpu.VMEM((2, 2, lines, span + 2 * LANES), bf16),
                    pltpu.VMEM((4, 16, span + 2 * LANES), f32),
                    pltpu.VMEM((2, lines - 2 * EDGE, span), f32),
                    pltpu.SemaphoreType.DMA((lines // 8,)),
                ],
            )
            part = call(
                functools.partial(border_kernel, lines, width, tile, columns, across),
                [((3 * lines + 16, tile), bf16)] * half,
                (ids, ranged, codes, rims, from_pair, from_next),
                [
                    pltpu.VMEM((4, HALO, width + 4 * LANES), f32),
                    pltpu.VMEM((2, 4, EDGE + 2 * HALO, span), f32),
                    pltpu.VMEM((2, 2 * EDGE, span), f32),
                    pltpu.VMEM((8, span), f32),
                ],
                "borders",
            )
            for i, value in enumerate(part):
                sent[i + (half if across else 0)] = value
            if across:
                *part, first_slc, second_slc = lax.optimization_barrier((*part, first_slc, second_slc))
                sources = (first_slc, second_slc)
                for i, value in enumerate(part):
                    sent[i + half] = value
        arrived = [sent[0]] + [
            lax.ppermute(sent[s], "col", [(i, i ^ s) for i in range(columns)]) for s in range(1, columns)
        ]
    else:
        above = jnp.where(odd, from_pair, from_next)
        below = jnp.where(odd, from_next, from_pair)
        height = lines + 2 * HALO
        sent = call(
            functools.partial(strip_kernel, lines, width, tile, columns, exchange),
            [((columns, 2 * lines + 8, tile), f32)],
            (ids, first_slc, second_slc, above, below),
            [pltpu.VMEM((4, height, wide), f32), pltpu.VMEM((4, height, width), f32), pltpu.VMEM((2, lines, wide), f32)],
            "strips",
        )
        arrived = [lax.all_to_all(sent[0], "col", 0, 0, tiled=True)]

    tables = []
    for table in (cosine_table(tile_az), cosine_table(tile)):
        parts = [*two_parts(table), *two_parts(table.T)]
        tables.append(jnp.asarray(np.concatenate(parts, axis=0)))
    inverse = jnp.asarray(inverse_eigen(tile_az, tile))

    whole = ((tile_az, tile), f32)
    block = ((8, LANES), f32)
    padded = pltpu.VMEM((tile_az + 2 * HALO, tile), f32)
    fluxes = [
        pltpu.VMEM((tile_az, tile), f32),
        pltpu.VMEM((tile_az, LANES), f32),
        pltpu.VMEM((tile_az + 8, tile), f32),
    ]
    residual, shaped, weight_x, rim_x, weight_y, row_pair, row_next, col_pair, col_next = call(
        functools.partial(tile_kernel, lines, tile_az, tile, columns, exchange),
        [whole, whole, whole, ((tile_az, LANES), f32), ((tile_az + 8, tile), f32), block, block, block, block],
        (ids, *arrived, *tables, inverse),
        [padded, padded, pltpu.VMEM((8 * columns, LANES), f32), pltpu.VMEM((8 * columns, LANES), f32), *fluxes],
        "tiles",
    )
    rims = (
        swapped(row_pair, "row", rows, 0),
        swapped(row_next, "row", rows, 1),
        swapped(col_pair, "col", columns, 0),
        swapped(col_next, "col", columns, 1),
    )
    operated, shaped2, operated2, chunk, roots = call(
        functools.partial(second_kernel, tile_az, tile),
        [whole, whole, whole, ((16, LANES), bf16), ((16, LANES), f32)],
        (ids, residual, shaped, weight_x, rim_x, weight_y, *rims, *tables, inverse),
        [padded, *fluxes],
        "operator",
    )
    spread = jnp.broadcast_to(chunk[None], (rows * columns, 16, LANES))
    gathered = lax.all_to_all(spread, axes, 0, 0, tiled=True)
    return tuple(
        call(
            functools.partial(last_kernel, tile_az, tile, rows, columns),
            [whole, whole],
            (ids, gathered, residual, shaped, operated, shaped2, operated2, roots),
            [
                pltpu.VMEM((tile_az, tile), f32),
                pltpu.VMEM((tile_az, tile), f32),
                pltpu.SemaphoreType.DMA((2 * (tile_az // min(tile_az, 64)),)),
            ],
            "finish",
            out_space=pltpu.HBM,
        )
    )


def solution(mesh):
    placed = P(None, ("row", "col"), None)
    return jax.shard_map(
        functools.partial(shards, mesh.shape["row"], mesh.shape["col"]),
        mesh=mesh,
        in_specs=(placed, placed),
        out_specs=(P("row", "col"), P("row", "col")),
        check_vma=False,
    )
```

```python
import functools
import math

import jax
import jax.numpy as jnp
import ml_dtypes
import numpy as np
from jax import lax
from jax.experimental import pallas as pl
from jax.experimental.pallas import tpu as pltpu
from jax.sharding import PartitionSpec as P

EPS = 1e-05
DAMPING = 0.0001
RADIUS = 4
LANES = 128
HALO = 8
EDGE = 16
TURN = 2.0 * math.pi
CODE_SPAN = 248.0
POWER_BASE = 2.0**7.5
TINY = 1e-30
SCALE_LANE = 5
VMEM_LIMIT = 40 * 1024 * 1024

ATAN = (
    0.1591549409219458,
    -0.05305126669892651,
    0.03181993346630217,
    -0.022611352052724496,
    0.016957432021882463,
    -0.011990188139443825,
    0.0068498925926071,
    -0.002591499099089036,
    0.00046210915702298266,
)
COS = (
    0.9999999997806517,
    -4.934802137228286,
    4.0587091643402005,
    -1.3352120566397616,
    0.23493755882899706,
    -0.024396716411350872,
)


def taps():
    offsets = np.arange(-RADIUS, RADIUS + 1).astype(np.float64)
    weights = np.exp(-offsets * offsets / 8.0)
    weights = weights / weights.sum()
    return [float(weights[RADIUS + j]) for j in range(RADIUS + 1)]


def cosine_table(count):
    j = np.arange(count)[:, None].astype(np.float64)
    i = np.arange(count)[None, :].astype(np.float64)
    table = np.cos(np.pi * j * (i + 0.5) / count) * np.sqrt(2.0 / count)
    table[0] = np.sqrt(1.0 / count)
    return table


def two_parts(table):
    table = table.astype(np.float32)
    high = table.astype(ml_dtypes.bfloat16)
    low = (table - high.astype(np.float32)).astype(ml_dtypes.bfloat16)
    return np.ascontiguousarray(high), np.ascontiguousarray(low)


def inverse_eigen(count_az, count_rg):
    along_az = 2.0 - 2.0 * np.cos(np.pi * np.arange(count_az) / count_az)
    along_rg = 2.0 - 2.0 * np.cos(np.pi * np.arange(count_rg) / count_rg)
    return (1.0 / (DAMPING + along_az[:, None] + along_rg[None, :])).astype(np.float32)


def poly(coefficients, y):
    value = jnp.full_like(y, coefficients[-1])
    for c in coefficients[-2::-1]:
        value = value * y + c
    return value


def angle_turns(im, re):
    a, b = jnp.abs(im), jnp.abs(re)
    big, small = jnp.maximum(a, b), jnp.minimum(a, b)
    t = small / jnp.maximum(big, 1e-37)
    p = t * poly(ATAN, t * t)
    p = jnp.where(a > b, 0.25 - p, p)
    p = jnp.where(re < 0.0, 0.5 - p, p)
    return jnp.where(im < 0.0, -p, p)


def edge(phase_p, gain_p, phase_q, gain_q):
    delta = phase_q - phase_p
    delta = delta - jnp.round(delta)
    half = gain_p * gain_q * poly(COS, delta * delta)
    weight = half * half
    return weight, weight * delta


def encode_gain(value):
    return jnp.exp2(value * CODE_SPAN - 0.5 * CODE_SPAN).astype(jnp.bfloat16)


def decode_gain(code):
    return (jnp.log2(code.astype(jnp.float32)) + 0.5 * CODE_SPAN) * (1.0 / CODE_SPAN)


def encode_power(value, scale):
    share = jnp.minimum(jnp.abs(value) / jnp.maximum(scale, TINY), 1.0) * POWER_BASE
    for _ in range(4):
        share = share * share
    return jnp.where(value < 0.0, -share, share)


def decode_power(code, scale):
    share = jnp.exp2(jnp.log2(jnp.abs(code)) * (1.0 / 16.0)) * (scale * (1.0 / POWER_BASE))
    return jnp.where(code < 0.0, -share, share)


def split(value):
    high = value.astype(jnp.bfloat16)
    return high, (value - high.astype(jnp.float32)).astype(jnp.bfloat16)


def dot3(a, b):
    f = functools.partial(jnp.dot, preferred_element_type=jnp.float32)
    return f(a[0], b[1]) + f(a[1], b[0]) + f(a[0], b[0])


def lanes_of(shape):
    return lax.broadcasted_iota(jnp.int32, shape, 1)


def call(body, outs, args, scratch, name, smem_first=True, flops=1000000, out_space=pltpu.VMEM):
    specs = [pl.BlockSpec(memory_space=pltpu.VMEM)] * len(args)
    if smem_first:
        specs[0] = pl.BlockSpec(memory_space=pltpu.SMEM)
    return pl.pallas_call(
        body,
        out_shape=[jax.ShapeDtypeStruct(s, d) for s, d in outs],
        in_specs=specs,
        out_specs=[pl.BlockSpec(memory_space=out_space)] * len(outs),
        scratch_shapes=scratch,
        compiler_params=pltpu.CompilerParams(vmem_limit_bytes=VMEM_LIMIT),
        cost_estimate=pl.CostEstimate(flops=flops, bytes_accessed=4000000, transcendentals=0),
        name=name,
    )(*args)


def interior(body, outs, args, scratch):
    return pl.pallas_call(
        body,
        out_shape=[jax.ShapeDtypeStruct(s, d) for s, d in outs],
        in_specs=[pl.BlockSpec(memory_space=pltpu.SMEM)] + [pl.BlockSpec(memory_space=pltpu.HBM)] * 2
        + [pl.BlockSpec(memory_space=pltpu.VMEM)],
        out_specs=[pl.BlockSpec(memory_space=pltpu.VMEM)] * len(outs),
        scratch_shapes=scratch,
        compiler_params=pltpu.CompilerParams(vmem_limit_bytes=VMEM_LIMIT),
        cost_estimate=pl.CostEstimate(flops=8000000, bytes_accessed=4000000, transcendentals=0),
        name="interior",
    )(*args)


def phase_gain(smoothed):
    re, im, one, two = smoothed
    gain = jnp.sqrt(re * re + im * im) / (jnp.sqrt(one * two) + EPS)
    return angle_turns(im, re), jnp.sqrt(gain)


def products(ar, ai, br, bi, scale=None):
    ar, ai, br, bi = (v.astype(jnp.float32) for v in (ar, ai, br, bi))
    if scale is not None:
        ar, ai, br, bi = (v * scale for v in (ar, ai, br, bi))
    return (ar * br + ai * bi, ai * br - ar * bi, ar * ar + ai * ai, br * br + bi * bi)


def along_range(x):
    k = taps()
    n = x.shape[1]
    total = k[0] * x
    for j in range(1, RADIUS + 1):
        total = total + k[j] * (pltpu.roll(x, j, 1) + pltpu.roll(x, n - j, 1))
    return total


def along_azimuth(ref, f, row, rows, cs):
    k = taps()
    total = k[0] * ref[f, row : row + rows, cs]
    for j in range(1, RADIUS + 1):
        total = total + k[j] * (ref[f, row - j : row - j + rows, cs] + ref[f, row + j : row + j + rows, cs])
    return total


def end_weights(before):
    k = taps()
    sub = lax.broadcasted_iota(jnp.int32, (HALO, 1), 0)
    low = jnp.zeros((HALO, 1), jnp.float32)
    high = jnp.zeros((HALO, 1), jnp.float32)
    for j in range(RADIUS + 1):
        low = jnp.where(sub == (HALO - 1 - j if before else HALO - j), k[j], low)
        high = jnp.where(sub == (j - 1 if before else j), k[j], high)
    return low, high


def first_of_half(own, half, across):
    return (own & half) ^ (half if across else 0)


def window(lines, width, tile, columns, across, own, rows):
    half = columns // 2
    span = half * tile + 2 * LANES
    first_tile = first_of_half(own, half, across)
    start = pl.multiple_of(first_tile * tile, LANES)
    pixel = lanes_of((rows, span)) + (start - LANES)
    return first_tile, start, span, jnp.logical_and(pixel >= 0, pixel < width)


def range_table(tile_pair, out):
    k = taps()
    margin = (tile_pair - out) // 2
    table = np.zeros((tile_pair, out))
    for n in range(out):
        for j in range(-RADIUS, RADIUS + 1):
            table[n + margin + j, n] = k[abs(j)]
    return table


def interior_kernel(
    lines, width, tile, columns, across, ids, first, second, table, ranged, field, codes, rims, raw, high, low, sems
):
    half = columns // 2
    chunk = 16
    first_tile, start, span, _ = window(lines, width, tile, columns, across, ids[1], 8)
    upper = jnp.where(first_tile == 0, 0, 1)
    source = pl.multiple_of(upper * (width // 2 - 2 * LANES), LANES)
    target = pl.multiple_of((1 - upper) * 2 * LANES, LANES)
    size = width // 2 + 2 * LANES
    blank = pl.multiple_of(upper * size, LANES)
    copies = []
    for i in range(lines // chunk):
        rs = pl.ds(i * chunk, chunk)
        for a, ref in enumerate((first, second)):
            copy = pltpu.make_async_copy(
                ref.at[:, rs, pl.ds(source, size)], raw.at[a, :, rs, pl.ds(target, size)], sems.at[2 * i + a]
            )
            copy.start()
            copies.append(copy)
    for a in range(2):
        for part in range(2):
            raw[a, part, :, pl.ds(blank, 2 * LANES)] = jnp.zeros((lines, 2 * LANES), jnp.bfloat16)
    for i in range(lines // chunk):
        copies[2 * i].wait()
        copies[2 * i + 1].wait()
        rs = slice(i * chunk, (i + 1) * chunk)
        for c in range(0, span + 2 * LANES, 2 * LANES):
            cs = slice(c, c + 2 * LANES)
            values = products(raw[0, 0, rs, cs], raw[0, 1, rs, cs], raw[1, 0, rs, cs], raw[1, 1, rs, cs])
            for f in range(4):
                row = f * lines + i * chunk
                high[row : row + chunk, cs], low[row : row + chunk, cs] = split(values[f])
    block = 2 * LANES
    weights = table[0 : 2 * block, :], table[2 * block :, :]
    for c in range(0, span, block):
        cs = slice(c, c + 2 * block)
        total = dot3((high[:, cs], low[:, cs]), weights)
        if c == 0 or c + block == span:
            pixel = lanes_of(total.shape) + (start - LANES + c)
            total = jnp.where(jnp.logical_and(pixel >= 0, pixel < width), total, 0.0)
        for f in range(4):
            ranged[f, :, c : c + block] = total[f * lines : (f + 1) * lines, :]
    for c in range(0, span, LANES):
        cs = slice(c, c + LANES)
        steps = [(HALO, HALO)] + [(r, 16) for r in range(EDGE, lines - EDGE, 16)] + [(lines - EDGE, HALO)]
        for r, rows in steps:
            smoothed = [along_azimuth(ranged, f, r, rows, cs) for f in range(4)]
            phase, gain = phase_gain(smoothed)
            field[0, r - HALO : r - HALO + rows, cs] = phase
            field[1, r - HALO : r - HALO + rows, cs] = gain
            if rows == 16:
                at = slice(r - EDGE, r - EDGE + rows)
                codes[0, at, cs], codes[1, at, cs] = split(phase)
                codes[2, at, cs] = encode_gain(gain)
    groups = lines // 8
    for t in range(half):
        rims[t] = rim_block(field, groups, range(1, groups - 1), 1, t * tile, tile, None)


def rim_block(field, groups, which, first_group, start, tile, block, hint=None):
    lane = lanes_of((8, LANES))
    if block is None:
        block = jnp.zeros((8, LANES), jnp.float32)
    for f in range(2):
        for side in range(2):
            offset = start if side == 0 else start + LANES + tile
            at = slice(offset, offset + LANES) if hint is None else pl.ds(hint(offset, LANES), LANES)
            for g in which:
                target = (f * 2 + side) * groups + g
                row = 8 * (g - first_group)
                x = field[f, row : row + 8, at]
                shift = (target - (LANES - 1 if side == 0 else 0)) % LANES
                if shift:
                    x = pltpu.roll(x, shift, 1)
                block = jnp.where(lane == target, x, block)
    return block


def border_kernel(lines, width, tile, columns, across, ids, ranged, inside_field, codes, rims, from_pair, from_next, *rest):
    half = columns // 2
    outs, (prod, seg, field, ends) = rest[:half], rest[half:]
    own = ids[1]
    odd = ids[4]
    first_tile, start, span, in_image = window(lines, width, tile, columns, across, own, HALO)
    inside = (
        jnp.where(ids[2] == 0, 0.0, 1.0).astype(jnp.float32),
        jnp.where(ids[2] == ids[3] - 1, 0.0, 1.0).astype(jnp.float32),
    )
    zero = jnp.zeros((HALO, 2 * LANES), jnp.float32)
    own_rows = 2 * HALO
    for e in range(2):
        flag = odd if e == 0 else 1 - odd
        keep = flag.astype(jnp.float32)
        for f in range(4):
            prod[f, :, 0 : 2 * LANES] = zero
            prod[f, :, 2 * LANES + width :] = zero
        for c in range(0, width, 512):
            cs = slice(c, c + 512)
            parts = [
                from_pair[i, :, cs].astype(jnp.float32) * keep + from_next[i, :, cs].astype(jnp.float32) * (1.0 - keep)
                for i in range(4)
            ]
            values = products(*parts, inside[e])
            for f in range(4):
                prod[f, :, 2 * LANES + c : 2 * LANES + c + 512] = values[f]
        for f in range(4):
            total = along_range(prod[f, :, pl.ds(start, span + 2 * LANES)])[:, LANES : LANES + span]
            total = jnp.where(in_image, total, 0.0)
            if e == 0:
                seg[e, f, 0:HALO, :] = total
                seg[e, f, HALO:, :] = ranged[f, 0:own_rows, :]
            else:
                seg[e, f, own_rows:, :] = total
                seg[e, f, 0:own_rows, :] = ranged[f, lines - own_rows :, :]
    for e in range(2):
        ref = seg.at[e]
        for c in range(0, span, LANES):
            cs = slice(c, c + LANES)
            smoothed = [along_azimuth(ref, f, HALO, HALO, cs) for f in range(4)]
            phase, gain = phase_gain(smoothed)
            field[0, e * HALO : (e + 1) * HALO, cs] = phase
            field[1, e * HALO : (e + 1) * HALO, cs] = gain
        low, high = end_weights(e == 0)
        r = 0 if e == 0 else own_rows - HALO
        smoothed = [
            jnp.sum(low * ref[f, r : r + HALO, :] + high * ref[f, r + HALO : r + 2 * HALO, :], axis=0, keepdims=True)
            for f in range(4)
        ]
        phase, gain = phase_gain(smoothed)
        ends[e : e + 1, :] = phase
        ends[2 + e : 3 + e, :] = gain * inside[e]
    groups = lines // 8
    inner = lines - 2 * EDGE
    for n, s in enumerate(range(half, columns) if across else range(half)):
        out = outs[n]
        target = own ^ s
        local = pl.multiple_of((target - first_tile) * tile, LANES)
        cs = pl.ds(pl.multiple_of(local + LANES, LANES), tile)
        for i in range(3):
            out[i * lines + EDGE : i * lines + EDGE + inner, :] = codes[i, :, cs]
        for e in range(2):
            row = 0 if e == 0 else lines - EDGE
            rs = slice(e * HALO, (e + 1) * HALO)
            inner_rows = slice(0, HALO) if e == 0 else slice(lines - 3 * HALO, lines - 2 * HALO)
            pairs = [(field[i, rs, cs], inside_field[i, inner_rows, cs]) for i in range(2)]
            phase, gain = (jnp.concatenate(p if e == 0 else p[::-1], axis=0) for p in pairs)
            out[row : row + EDGE, :], out[lines + row : lines + row + EDGE, :] = split(phase)
            out[2 * lines + row : 2 * lines + row + EDGE, :] = encode_gain(gain)
        block = rims[target - first_tile]
        block = rim_block(field, groups, (0,), 0, local, tile, block, pl.multiple_of)
        block = rim_block(field, groups, (groups - 1,), groups - 2, local, tile, block, pl.multiple_of)
        rows = []
        for i in range(4):
            for h in range(tile // LANES):
                rows.append(ends[i : i + 1, pl.ds(pl.multiple_of(local + (h + 1) * LANES, LANES), LANES)])
        block = jnp.concatenate([block, jnp.concatenate(rows, axis=0)], axis=1)
        out[3 * lines :, :] = jnp.concatenate(split(block), axis=0)


def strip_kernel(lines, width, tile, columns, exchange, ids, first, second, above, below, *rest):
    n_out = len(rest) - 3
    outs, (prod, ranged, field) = rest[:n_out], rest[n_out:]
    k = taps()
    own = ids[1]
    inside_above = jnp.where(ids[2] == 0, 0.0, 1.0).astype(jnp.float32)
    inside_below = jnp.where(ids[2] == ids[3] - 1, 0.0, 1.0).astype(jnp.float32)
    height = lines + 2 * HALO

    zero = jnp.zeros((height, LANES), jnp.float32)
    for f in range(4):
        prod[f, :, 0:LANES] = zero
        prod[f, :, LANES + width :] = zero
    step = min(width, 512)
    for c in range(0, width, step):
        at = slice(LANES + c, LANES + c + step)
        cs = slice(c, c + step)
        rows = min(lines, 16)
        for r in range(0, lines, rows):
            rs = slice(r, r + rows)
            values = products(first[0, rs, cs], first[1, rs, cs], second[0, rs, cs], second[1, rs, cs])
            for f in range(4):
                prod[f, HALO + r : HALO + r + rows, at] = values[f]
        for ref, r, scale in ((above, 0, inside_above), (below, HALO + lines, inside_below)):
            values = products(ref[0, :, cs], ref[1, :, cs], ref[2, :, cs], ref[3, :, cs], scale)
            for f in range(4):
                prod[f, r : r + HALO, at] = values[f]

    step = min(width, 1024)
    for f in range(4):
        for r in range(0, height, 8):
            for c in range(0, width, step):
                x = prod[f, r : r + 8, c : c + step + 2 * LANES]
                n = step + 2 * LANES
                total = k[0] * x
                for j in range(1, RADIUS + 1):
                    total = total + k[j] * (pltpu.roll(x, j, 1) + pltpu.roll(x, n - j, 1))
                ranged[f, r : r + 8, c : c + step] = total[:, LANES : LANES + step]

    for f in range(2):
        field[f, :, 0:LANES] = zero[:lines]
        field[f, :, LANES + width :] = zero[:lines]
    rows = min(lines, 32)
    sub = lax.broadcasted_iota(jnp.int32, (HALO, 1), 0)
    low = jnp.zeros((HALO, 1), jnp.float32)
    high = jnp.zeros((HALO, 1), jnp.float32)
    for j in range(RADIUS + 1):
        low = jnp.where(sub == HALO - 1 - j, k[j], low)
        high = jnp.where(sub == j - 1, k[j], high)
    top, bottom = [], []
    for c in range(0, width, LANES):
        cs = slice(c, c + LANES)
        for r in range(0, lines, rows):
            smoothed = []
            for f in range(4):
                b = HALO + r
                total = k[0] * ranged[f, b : b + rows, cs]
                for j in range(1, RADIUS + 1):
                    total = total + k[j] * (
                        ranged[f, b - j : b - j + rows, cs] + ranged[f, b + j : b + j + rows, cs]
                    )
                smoothed.append(total)
            phase, gain = phase_gain(smoothed)
            field[0, r : r + rows, LANES + c : 2 * LANES + c] = phase
            field[1, r : r + rows, LANES + c : 2 * LANES + c] = gain

    step = min(width, 1024)
    low = low + jnp.zeros((HALO, step), jnp.float32)
    high = high + jnp.zeros((HALO, step), jnp.float32)
    mirror_low = jnp.zeros((HALO, 1), jnp.float32)
    mirror_high = jnp.zeros((HALO, 1), jnp.float32)
    for j in range(RADIUS + 1):
        mirror_high = jnp.where(sub == j, k[j], mirror_high)
        mirror_low = jnp.where(sub == HALO - j, k[j], mirror_low)
    ends = []
    for c in range(0, width, step):
        cs = slice(c, c + step)
        up = [
            jnp.sum(low * ranged[f, 0:HALO, cs] + high * ranged[f, HALO : 2 * HALO, cs], axis=0, keepdims=True)
            for f in range(4)
        ]
        down = [
            jnp.sum(
                mirror_low * ranged[f, lines : lines + HALO, cs]
                + mirror_high * ranged[f, lines + HALO : lines + 2 * HALO, cs],
                axis=0,
                keepdims=True,
            )
            for f in range(4)
        ]
        up_phase, up_gain = phase_gain(up)
        down_phase, down_gain = phase_gain(down)
        ends.append((up_phase, down_phase, up_gain * inside_above, down_gain * inside_below))
    for i, (a, b, c_, d) in enumerate(ends):
        at = slice(i * step, (i + 1) * step)
        prod[0, 0:1, at] = a
        prod[0, 1:2, at] = b
        prod[0, 2:3, at] = c_
        prod[0, 3:4, at] = d

    groups = lines // 8
    lane = lanes_of((8, LANES))

    def pack(out, start, aligned):
        hint = pl.multiple_of if aligned else (lambda v, _: v)
        out[0:lines, :] = field[0, :, pl.ds(hint(start + LANES, LANES), tile)]
        out[lines : 2 * lines, :] = field[1, :, pl.ds(hint(start + LANES, LANES), tile)]
        block = jnp.zeros((8, LANES), jnp.float32)
        for f in range(2):
            for side in range(2):
                offset = start if side == 0 else start + LANES + tile
                for g in range(groups):
                    target = (f * 2 + side) * groups + g
                    x = field[f, 8 * g : 8 * g + 8, pl.ds(hint(offset, LANES), LANES)]
                    shift = (target - (LANES - 1 if side == 0 else 0)) % LANES
                    if shift:
                        x = pltpu.roll(x, shift, 1)
                    block = jnp.where(lane == target, x, block)
        base = 2 * lines
        out[base : base + 8, 0:LANES] = block
        for i in range(4):
            for h in range(tile // LANES):
                out[base + 2 * i + h : base + 2 * i + h + 1, LANES : 2 * LANES] = prod[
                    0, i : i + 1, pl.ds(hint(start + h * LANES, LANES), LANES)
                ]

    if exchange == "permute":
        for s in range(columns):
            pack(outs[s], (own ^ s) * tile, True)
    else:
        for s in range(columns):
            pack(outs[0].at[s], s * tile, False)


def precondition(field, tables, inverse):
    az, az_t, rg, rg_t = tables
    coef = dot3(az, split(field))
    coef = dot3(split(coef), rg_t)
    coef = coef * inverse[...]
    back = dot3(az_t, split(coef))
    return dot3(split(back), rg)


def table_pairs(tables):
    pairs = []
    for ref in tables:
        n = ref.shape[1]
        parts = [ref[i * n : (i + 1) * n, :] for i in range(4)]
        pairs += [(parts[0], parts[1]), (parts[2], parts[3])]
    return pairs


def line_groups(ref, tile_az, edge_lane):
    lane = lanes_of((8, LANES))
    first = (edge_lane // LANES) * LANES
    block = jnp.zeros((8, LANES), jnp.float32)
    for g in range(tile_az // 8):
        x = ref[8 * g : 8 * g + 8, first : first + LANES]
        shift = (g - edge_lane) % LANES
        if shift:
            x = pltpu.roll(x, shift, 1)
        block = jnp.where(lane == g, x, block)
    return block


def spread_groups(block, first_group, count, target_lane, base=0):
    parts = []
    for g in range(first_group, first_group + count):
        shift = (target_lane - (base + g)) % LANES
        parts.append(pltpu.roll(block, shift, 1) if shift else block)
    return jnp.concatenate(parts, axis=0) if count > 1 else parts[0]


def shifted_right(x, left):
    lane = lanes_of(x.shape)
    if left is None:
        return jnp.where(lane == 0, 0.0, pltpu.roll(x, 1, 1))
    wide = jnp.concatenate([left] * (x.shape[1] // LANES), axis=1)
    return jnp.where(lane == 0, wide, pltpu.roll(x, 1, 1))


def shifted_left(x, right):
    lane = lanes_of(x.shape)
    wide = jnp.concatenate([right] * (x.shape[1] // LANES), axis=1)
    return jnp.where(lane == x.shape[1] - 1, wide, pltpu.roll(x, x.shape[1] - 1, 1))


def divergence(tile_az, step, along_x, rim_x, along_y, r):
    rs = slice(r, r + step)
    x = along_x[rs, :]
    return (x - shifted_left(x, rim_x[rs, :])) + along_y[rs, :] - along_y[r + 1 : r + 1 + step, :]


def edges_of(lines, count, tile, coded, sources, scratch, outs):
    phase, gain, sides, ends = scratch
    weight_x, flux_x, rim_x, flux_rim, weight_y, flux_y, weight_end, flux_end = outs
    height = count * lines
    for src, strip in sources:
        if coded:
            row, at = pl.multiple_of(strip * lines, 8), pl.ds(pl.multiple_of(strip * 8, 8), 8)
            phase[pl.ds(HALO + row, lines), :] = src[0:lines, :].astype(jnp.float32) + src[
                lines : 2 * lines, :
            ].astype(jnp.float32)
            gain[pl.ds(HALO + row, lines), :] = decode_gain(src[2 * lines : 3 * lines, :])
            both = src[3 * lines :, :].astype(jnp.float32)
            block = both[0:8, :] + both[8:16, :]
        else:
            row, at = strip * lines, pl.ds(strip * 8, 8)
            phase[pl.ds(HALO + row, lines), :] = src[0:lines, :]
            gain[pl.ds(HALO + row, lines), :] = src[lines : 2 * lines, :]
            block = src[2 * lines : 2 * lines + 8, :]
        sides[at, :] = block[:, 0:LANES]
        ends[at, :] = block[:, LANES : 2 * LANES]
    last = 8 * (count - 1)
    for h in range(tile // LANES):
        cs = slice(h * LANES, (h + 1) * LANES)
        phase[HALO - 1 : HALO, cs] = ends[h : h + 1, :]
        gain[HALO - 1 : HALO, cs] = ends[4 + h : 5 + h, :]
        phase[HALO + height : HALO + height + 1, cs] = ends[last + 2 + h : last + 3 + h, :]
        gain[HALO + height : HALO + height + 1, cs] = ends[last + 6 + h : last + 7 + h, :]

    step = min(height, 32)
    groups = lines // 8
    for r in range(0, height, step):
        rs = slice(r, r + step)
        b = HALO + r
        p, g = phase[b : b + step, :], gain[b : b + step, :]
        halo = []
        for f in range(2):
            for side in range(2):
                parts = []
                for line_group in range(r // 8, (r + step) // 8):
                    strip, inner = divmod(line_group, groups)
                    block = sides[8 * strip : 8 * strip + 8, :]
                    source_lane = (f * 2 + side) * groups + inner
                    shift = ((0 if side == 0 else LANES - 1) - source_lane) % LANES
                    parts.append(pltpu.roll(block, shift, 1) if shift else block)
                halo.append(jnp.concatenate(parts, axis=0) if len(parts) > 1 else parts[0])
        weight_x[rs, :], flux_x[rs, :] = edge(shifted_right(p, halo[0]), shifted_right(g, halo[2]), p, g)
        rim_x[rs, :], flux_rim[rs, :] = edge(p[:, tile - LANES :], g[:, tile - LANES :], halo[1], halo[3])
        weight_y[rs, :], flux_y[rs, :] = edge(phase[b - 1 : b - 1 + step, :], gain[b - 1 : b - 1 + step, :], p, g)
    b = HALO + height
    w, f = edge(phase[b - 1 : b, :], gain[b - 1 : b, :], phase[b : b + 1, :], gain[b : b + 1, :])
    weight_end[...] = jnp.broadcast_to(w, (8, tile))
    flux_end[...] = jnp.broadcast_to(f, (8, tile))


def far_kernel(lines, tile, columns, ids, *rest):
    half = columns // 2
    own = ids[1]
    sources = [(rest[n], (own ^ n) & (half - 1)) for n in range(half)]
    edges_of(lines, half, tile, True, sources, rest[half + 8 :], rest[half : half + 8])


def tile_kernel(lines, tile_az, tile, columns, exchange, ids, *rest):
    coded = exchange == "permute"
    half = columns // 2
    own = ids[1]
    count = half if coded else columns
    if coded:
        sources = [(rest[s], (own ^ s) & (half - 1)) for s in range(half)]
        far, rest = rest[half : half + 8], rest[half + 8 :]
    else:
        sources = [(rest[0].at[s], s) for s in range(columns)]
        rest = rest[1:]
    tables, inverse = rest[:2], rest[2]
    residual, shaped, weight_x, rim_x, weight_y, row_pair, row_next, col_pair, col_next = rest[3:12]
    phase, gain, sides, ends, flux_x, flux_rim, flux_y, weight_end, flux_end = rest[12:]
    pairs = table_pairs(tables)
    height = count * lines
    whole = (weight_x, flux_x, rim_x, flux_rim, weight_y, flux_y)
    if coded:
        lower = (own & half) // half
        at = pl.ds(pl.multiple_of(lower * height, 8), height)
        outs = [ref.at[at, :] for ref in whole]
    else:
        outs = [ref.at[pl.ds(0, height), :] for ref in whole]
    edges_of(
        lines, count, tile, coded, sources, (phase, gain, sides, ends), (*outs, weight_end, flux_end)
    )
    w, f = weight_end[...], flux_end[...]
    if coded:
        at = pl.ds(pl.multiple_of((1 - lower) * height, 8), height)
        for source, ref in zip(far, whole):
            ref[at, :] = source[...]
        w, f = jnp.where(lower == 1, w, far[6][...]), jnp.where(lower == 1, f, far[7][...])
    weight_y[tile_az : tile_az + 8, :] = w
    flux_y[tile_az : tile_az + 8, :] = f

    step = min(tile_az, 32)
    for r in range(0, tile_az, step):
        residual[r : r + step, :] = TURN * divergence(tile_az, step, flux_x, flux_rim, flux_y, r)
    shaped[...] = precondition(residual[...], pairs, inverse)
    row_odd, col_odd = ids[5] == 1, ids[4] == 1
    top = jnp.concatenate([shaped[0:1, h : h + LANES] for h in range(0, tile, LANES)], axis=0)
    bottom = jnp.concatenate([shaped[tile_az - 1 : tile_az, h : h + LANES] for h in range(0, tile, LANES)], axis=0)
    row_pair[0:2, :] = jnp.where(row_odd, top, bottom)
    row_next[0:2, :] = jnp.where(row_odd, bottom, top)
    left = line_groups(shaped, tile_az, 0)
    right = line_groups(shaped, tile_az, tile - 1)
    col_pair[...] = jnp.where(col_odd, left, right)
    col_next[...] = jnp.where(col_odd, right, left)


def apply_operator(tile_az, tile, u, weight_x, rim_x, weight_y, flux_x, flux_rim, flux_y, left, right, out):
    step = min(tile_az, 32)
    for r in range(0, tile_az, step):
        rs = slice(r, r + step)
        b = HALO + r
        x = u[b : b + step, :]
        l = None if left is None else spread_groups(left, r // 8, step // 8, 0)
        flux_x[rs, :] = weight_x[rs, :] * (x - shifted_right(x, l))
        edge_x = x[:, tile - LANES :]
        if right is None:
            flux_rim[rs, :] = -rim_x[rs, :] * edge_x
        else:
            flux_rim[rs, :] = rim_x[rs, :] * (spread_groups(right, r // 8, step // 8, LANES - 1) - edge_x)
        flux_y[rs, :] = weight_y[rs, :] * (x - u[b - 1 : b - 1 + step, :])
    b = HALO + tile_az
    flux_y[tile_az : tile_az + 1, :] = weight_y[tile_az : tile_az + 1, :] * (u[b : b + 1, :] - u[b - 1 : b, :])
    for r in range(0, tile_az, step):
        out[r : r + step, :] = DAMPING * u[HALO + r : HALO + r + step, :] + divergence(
            tile_az, step, flux_x, flux_rim, flux_y, r
        )


def inner(a, b, tile_az, offset_a=0, offset_b=0):
    total = jnp.zeros((32, a.shape[1]), jnp.float32)
    for r in range(0, tile_az, 32):
        total = total + a[offset_a + r : offset_a + r + 32, :] * b[offset_b + r : offset_b + r + 32, :]
    return jnp.sum(jnp.sum(total, axis=0, keepdims=True), axis=1, keepdims=True)


def second_kernel(
    tile_az, tile, ids, residual, shaped, weight_x, rim_x, weight_y, row_pair, row_next, col_pair, col_next, *rest
):
    tables, inverse = rest[:2], rest[2]
    operated, shaped2, operated2, chunk, roots = rest[3:8]
    u, flux_x, flux_rim, flux_y = rest[8:]
    pairs = table_pairs(tables)
    row_odd, col_odd = ids[5] == 1, ids[4] == 1
    up = jnp.where(row_odd, row_pair[0:2, :], row_next[0:2, :])
    down = jnp.where(row_odd, row_next[0:2, :], row_pair[0:2, :])
    left = jnp.where(col_odd, col_pair[...], col_next[...])
    right = jnp.where(col_odd, col_next[...], col_pair[...])
    u[HALO : HALO + tile_az, :] = shaped[...]
    for h in range(tile // LANES):
        cs = slice(h * LANES, (h + 1) * LANES)
        u[HALO - 1 : HALO, cs] = up[h : h + 1, :]
        u[HALO + tile_az : HALO + tile_az + 1, cs] = down[h : h + 1, :]
    apply_operator(
        tile_az, tile, u, weight_x, rim_x, weight_y, flux_x, flux_rim, flux_y, left, right, operated
    )
    image = precondition(operated[...], pairs, inverse)
    shaped2[...] = image
    u[HALO : HALO + tile_az, :] = image
    apply_operator(
        tile_az, tile, u, weight_x, rim_x, weight_y, flux_x, flux_rim, flux_y, left, right, operated2
    )
    lane = lanes_of((1, LANES))
    sums = jnp.zeros((1, LANES), jnp.float32)
    for i, (a, b) in enumerate(
        (
            (residual, shaped),
            (shaped, operated),
            (residual, shaped2),
            (operated, shaped2),
            (shaped2, operated2),
        )
    ):
        sums = jnp.where(lane == i, inner(a, b, tile_az), sums)
    def rows_of(x):
        return jnp.concatenate([x[:, h : h + LANES] for h in range(0, tile, LANES)], axis=0)

    weight_t, weight_b = rows_of(weight_y[0:1, :]), rows_of(weight_y[tile_az : tile_az + 1, :])
    weight_l, weight_r = line_groups(weight_x, tile_az, 0), line_groups(rim_x, tile_az, LANES - 1)
    top = rows_of(image_row(shaped2, shaped, 0))
    bottom = rows_of(image_row(shaped2, shaped, tile_az - 1))
    left_rim = line_groups(shaped2, tile_az, 0) - line_groups(shaped, tile_az, 0)
    right_rim = line_groups(shaped2, tile_az, tile - 1) - line_groups(shaped, tile_az, tile - 1)
    known = jnp.sum(weight_t * up * top + weight_b * down * bottom, keepdims=True) + jnp.sum(
        weight_l * left * left_rim + weight_r * right * right_rim, keepdims=True
    )
    sums = jnp.where(lane == 4, sums - known, sums)
    half = tile_az // 8
    wide = lanes_of((8, LANES))
    root_sides = jnp.sqrt(jnp.where(wide < half, weight_l, pltpu.roll(weight_r, half, 1)))
    sides = root_sides * jnp.where(wide < half, left_rim, pltpu.roll(right_rim, half, 1))
    root_ends = jnp.sqrt(jnp.concatenate([weight_t, weight_b], axis=0))
    ends = root_ends * jnp.concatenate([top, bottom], axis=0)
    scale = jnp.maximum(jnp.max(jnp.abs(sides), keepdims=True), jnp.max(jnp.abs(ends), keepdims=True))
    scale = (scale * 1.01).astype(jnp.bfloat16).astype(jnp.float32)
    sums = jnp.where(lane == SCALE_LANE, scale, sums)
    high = sums.astype(jnp.bfloat16).astype(jnp.float32)
    middle = (sums - high).astype(jnp.bfloat16).astype(jnp.float32)
    rest_ = sums - high - middle
    sums = high + pltpu.roll(middle, 8, 1) + pltpu.roll(rest_, 16, 1)
    chunk[...] = jnp.concatenate(
        [encode_power(sides, scale), encode_power(ends, scale), jnp.broadcast_to(sums, (4, LANES))], axis=0
    ).astype(jnp.bfloat16)
    roots[...] = jnp.concatenate([root_sides, root_ends, root_ends], axis=0)


def image_row(a, b, row):
    return a[row : row + 1, :] - b[row : row + 1, :]


def last_kernel(
    tile_az, tile, rows, columns, ids, gathered, residual, shaped, operated, shaped2, operated2, roots,
    solution_hbm, residual_hbm, solution_out, residual_out, sems
):
    half = tile_az // 8
    lane = lanes_of((8, LANES))
    total = jnp.zeros((4, LANES), jnp.float32)
    cross_x = jnp.zeros((8, LANES), jnp.float32)
    cross_y = jnp.zeros((2, LANES), jnp.float32)
    values = {}

    def decoded(i):
        x = gathered[i].astype(jnp.float32)
        return jnp.concatenate([decode_power(x[0:12, :], x[12:13, SCALE_LANE : SCALE_LANE + 1]), x[12:16, :]], axis=0)

    def value_of(i):
        if i not in values:
            values[i] = decoded(i)
        return values[i]

    for r in range(rows):
        for c in range(columns):
            i = r * columns + c
            here = value_of(i)
            total = total + here[12:16, :]
            if c + 1 < columns:
                cross_x = cross_x + pltpu.roll(here[0:8, :], LANES - half, 1) * value_of(i + 1)[0:8, :]
            if r + 1 < rows:
                cross_y = cross_y + here[10:12, :] * value_of(i + columns)[8:10, :]
    cross = jnp.sum(jnp.where(lane < half, cross_x, 0.0), keepdims=True) + jnp.sum(cross_y, keepdims=True)
    wide = total[0:1, :]
    first_lane = lanes_of((1, LANES))
    pick = [
        jnp.sum(jnp.where(first_lane % 8 == i, jnp.where(first_lane < 24, wide, 0.0), 0.0), axis=1, keepdims=True)
        for i in range(5)
    ]
    dot0, curve0, mixed, cross_dot, curve2 = pick
    curve2 = curve2 - 2.0 * cross
    alpha = dot0 / curve0
    fresh = dot0 - alpha * (mixed + curve0) + alpha * alpha * cross_dot
    beta = fresh / dot0
    grown = 1.0 + beta
    curve1 = grown * grown * curve0 - 2.0 * alpha * grown * cross_dot + alpha * alpha * curve2
    step1 = fresh / curve1
    on_first = alpha + step1 * grown
    on_second = step1 * alpha

    row, col = ids[0], ids[1]
    here = row * columns + col

    def neighbour(ok, index):
        return jnp.where(ok, index, here), jnp.where(ok, 1.0, 0.0).astype(jnp.float32)

    up, up_ok = neighbour(row > 0, here - columns)
    down, down_ok = neighbour(row < rows - 1, here + columns)
    left, left_ok = neighbour(col > 0, here - 1)
    right, right_ok = neighbour(col < columns - 1, here + 1)
    near = [decoded(i) for i in (left, right, up, down)]
    from_left = pltpu.roll(near[0][0:8, :], LANES - half, 1) * left_ok
    from_right = pltpu.roll(near[1][0:8, :], half, 1) * right_ok
    top = jnp.concatenate([near[2][10 + h : 11 + h, :] for h in range(tile // LANES)], axis=1) * up_ok
    bottom = jnp.concatenate([near[3][8 + h : 9 + h, :] for h in range(tile // LANES)], axis=1) * down_ok
    top = top * jnp.concatenate([roots[8 + h : 9 + h, :] for h in range(tile // LANES)], axis=1)
    bottom = bottom * jnp.concatenate([roots[10 + h : 11 + h, :] for h in range(tile // LANES)], axis=1)
    from_left = from_left * roots[0:8, :]
    from_right = from_right * roots[0:8, :]
    step = min(tile_az, 64)
    copies = []
    for r in range(0, tile_az, step):
        rs = slice(r, r + step)
        solution_out[rs, :] = on_first * shaped[rs, :] - on_second * shaped2[rs, :]
        q = operated2[rs, :]
        wide = lanes_of((step, tile))
        l = jnp.concatenate([spread_groups(from_left, r // 8, step // 8, 0)] * (tile // LANES), axis=1)
        q = q - jnp.where(wide == 0, l, 0.0)
        l = jnp.concatenate([spread_groups(from_right, r // 8, step // 8, LANES - 1, half)] * (tile // LANES), axis=1)
        q = q - jnp.where(wide == tile - 1, l, 0.0)
        if r == 0 or r + step == tile_az:
            deep = lax.broadcasted_iota(jnp.int32, (step, tile), 0)
        if r == 0:
            q = q - jnp.where(deep == 0, jnp.broadcast_to(top, (step, tile)), 0.0)
        if r + step == tile_az:
            q = q - jnp.where(deep == step - 1, jnp.broadcast_to(bottom, (step, tile)), 0.0)
        residual_out[rs, :] = residual[rs, :] - on_first * operated[rs, :] + on_second * q
        for n, (src, dst) in enumerate(((solution_out, solution_hbm), (residual_out, residual_hbm))):
            copy = pltpu.make_async_copy(src.at[rs, :], dst.at[rs, :], sems.at[2 * (r // step) + n])
            copy.start()
            copies.append(copy)
    for copy in copies:
        copy.wait()


def swapped(value, axis, count, step):
    if step == 0:
        pairs = [(i, i ^ 1) for i in range(count)]
    else:
        pairs = [(i, (i + 1 if i % 2 else i - 1) % count) for i in range(count)]
    return lax.ppermute(value, axis, pairs)


def shards(rows, columns, first_slc, second_slc):
    lines, width = first_slc.shape[1:]
    tile = width // columns
    tile_az = lines * columns
    axes = ("row", "col")
    exchange = "permute" if lines >= 4 * EDGE and columns <= 8 else "all_to_all"
    row, col = lax.axis_index("row"), lax.axis_index("col")
    ids = jnp.stack([row, col, row * columns + col, jnp.int32(rows * columns), col % 2, row % 2]).astype(jnp.int32)
    f32, bf16 = jnp.float32, jnp.bfloat16

    head = jnp.concatenate([first_slc[:, :HALO], second_slc[:, :HALO]], 0)
    tail = jnp.concatenate([first_slc[:, -HALO:], second_slc[:, -HALO:]], 0)
    odd = col % 2 == 1
    from_pair = swapped(jnp.where(odd, head, tail), axes, rows * columns, 0)
    from_next = swapped(jnp.where(odd, tail, head), axes, rows * columns, 1)
    wide = width + 2 * LANES
    if exchange == "permute":
        half = columns // 2
        span = half * tile + 2 * LANES
        smoothing = jnp.asarray(np.concatenate(two_parts(range_table(4 * LANES, 2 * LANES)), axis=0))
        sent = [None] * columns
        sources = (first_slc, second_slc)
        for across in (True, False):
            ranged, inner, codes, rims = interior(
                functools.partial(interior_kernel, lines, width, tile, columns, across),
                [
                    ((4, lines, span), f32),
                    ((2, lines - 2 * HALO, span), f32),
                    ((3, lines - 2 * EDGE, span), bf16),
                    ((half, 8, LANES), f32),
                ],
                (ids, *sources, smoothing),
                [
                    pltpu.VMEM((2, 2, lines, span + 2 * LANES), bf16),
                    pltpu.VMEM((4 * lines, span + 2 * LANES), bf16),
                    pltpu.VMEM((4 * lines, span + 2 * LANES), bf16),
                    pltpu.SemaphoreType.DMA((lines // 8,)),
                ],
            )
            part = call(
                functools.partial(border_kernel, lines, width, tile, columns, across),
                [((3 * lines + 16, tile), bf16)] * half,
                (ids, ranged, inner, codes, rims, from_pair, from_next),
                [
                    pltpu.VMEM((4, HALO, width + 4 * LANES), f32),
                    pltpu.VMEM((2, 4, 3 * HALO, span), f32),
                    pltpu.VMEM((2, 2 * HALO, span), f32),
                    pltpu.VMEM((8, span), f32),
                ],
                "borders",
            )
            for i, value in enumerate(part):
                sent[i + (half if across else 0)] = value
            if across:
                *part, first_slc, second_slc = lax.optimization_barrier((*part, first_slc, second_slc))
                sources = (first_slc, second_slc)
                for i, value in enumerate(part):
                    sent[i + half] = value
        arrived = [sent[0]] + [
            lax.ppermute(sent[s], "col", [(i, i ^ s) for i in range(columns)]) for s in range(1, columns)
        ]
    else:
        above = jnp.where(odd, from_pair, from_next)
        below = jnp.where(odd, from_next, from_pair)
        height = lines + 2 * HALO
        sent = call(
            functools.partial(strip_kernel, lines, width, tile, columns, exchange),
            [((columns, 2 * lines + 8, tile), f32)],
            (ids, first_slc, second_slc, above, below),
            [pltpu.VMEM((4, height, wide), f32), pltpu.VMEM((4, height, width), f32), pltpu.VMEM((2, lines, wide), f32)],
            "strips",
        )
        arrived = [lax.all_to_all(sent[0], "col", 0, 0, tiled=True)]

    tables = []
    for table in (cosine_table(tile_az), cosine_table(tile)):
        parts = [*two_parts(table), *two_parts(table.T)]
        tables.append(jnp.asarray(np.concatenate(parts, axis=0)))
    inverse = jnp.asarray(inverse_eigen(tile_az, tile))

    whole = ((tile_az, tile), f32)
    block = ((8, LANES), f32)
    padded = pltpu.VMEM((tile_az + 2 * HALO, tile), f32)
    fluxes = [
        pltpu.VMEM((tile_az, tile), f32),
        pltpu.VMEM((tile_az, LANES), f32),
        pltpu.VMEM((tile_az + 8, tile), f32),
    ]
    edge_rows = tile_az
    if exchange == "permute":
        edge_rows = half * lines
        part = ((edge_rows, tile), f32)
        side = ((edge_rows, LANES), f32)
        last = ((8, tile), f32)
        far = call(
            functools.partial(far_kernel, lines, tile, columns),
            [part, part, side, side, part, part, last, last],
            (ids, *arrived[half:]),
            [
                pltpu.VMEM((edge_rows + 2 * HALO, tile), f32),
                pltpu.VMEM((edge_rows + 2 * HALO, tile), f32),
                pltpu.VMEM((8 * half, LANES), f32),
                pltpu.VMEM((8 * half, LANES), f32),
            ],
            "far",
        )
        arrived = [*arrived[:half], *far]
    gathered_lines = pltpu.VMEM((edge_rows + 2 * HALO, tile), f32)
    residual, shaped, weight_x, rim_x, weight_y, row_pair, row_next, col_pair, col_next = call(
        functools.partial(tile_kernel, lines, tile_az, tile, columns, exchange),
        [whole, whole, whole, ((tile_az, LANES), f32), ((tile_az + 8, tile), f32), block, block, block, block],
        (ids, *arrived, *tables, inverse),
        [
            gathered_lines,
            gathered_lines,
            pltpu.VMEM((8 * columns, LANES), f32),
            pltpu.VMEM((8 * columns, LANES), f32),
            *fluxes,
            pltpu.VMEM((8, tile), f32),
            pltpu.VMEM((8, tile), f32),
        ],
        "tiles",
    )
    rims = (
        swapped(row_pair, "row", rows, 0),
        swapped(row_next, "row", rows, 1),
        swapped(col_pair, "col", columns, 0),
        swapped(col_next, "col", columns, 1),
    )
    operated, shaped2, operated2, chunk, roots = call(
        functools.partial(second_kernel, tile_az, tile),
        [whole, whole, whole, ((16, LANES), bf16), ((16, LANES), f32)],
        (ids, residual, shaped, weight_x, rim_x, weight_y, *rims, *tables, inverse),
        [padded, *fluxes],
        "operator",
    )
    spread = jnp.broadcast_to(chunk[None], (rows * columns, 16, LANES))
    gathered = lax.all_to_all(spread, axes, 0, 0, tiled=True)
    return tuple(
        call(
            functools.partial(last_kernel, tile_az, tile, rows, columns),
            [whole, whole],
            (ids, gathered, residual, shaped, operated, shaped2, operated2, roots),
            [
                pltpu.VMEM((tile_az, tile), f32),
                pltpu.VMEM((tile_az, tile), f32),
                pltpu.SemaphoreType.DMA((2 * (tile_az // min(tile_az, 64)),)),
            ],
            "finish",
            out_space=pltpu.HBM,
        )
    )


def solution(mesh):
    placed = P(None, ("row", "col"), None)
    return jax.shard_map(
        functools.partial(shards, mesh.shape["row"], mesh.shape["col"]),
        mesh=mesh,
        in_specs=(placed, placed),
        out_specs=(P("row", "col"), P("row", "col")),
        check_vma=False,
    )
```

```python
import functools
import math

import jax
import jax.numpy as jnp
import ml_dtypes
import numpy as np
from jax import lax
from jax.experimental import pallas as pl
from jax.experimental.pallas import tpu as pltpu
from jax.sharding import PartitionSpec as P

EPS = 1e-05
DAMPING = 0.0001
RADIUS = 4
LANES = 128
HALO = 8
EDGE = 16
TURN = 2.0 * math.pi
CODE_SPAN = 248.0
POWER_BASE = 2.0**7.5
TINY = 1e-30
SCALE_LANE = 5
VMEM_LIMIT = 40 * 1024 * 1024

ATAN = (
    0.1591549409219458,
    -0.05305126669892651,
    0.03181993346630217,
    -0.022611352052724496,
    0.016957432021882463,
    -0.011990188139443825,
    0.0068498925926071,
    -0.002591499099089036,
    0.00046210915702298266,
)
COS = (
    0.9999999997806517,
    -4.934802137228286,
    4.0587091643402005,
    -1.3352120566397616,
    0.23493755882899706,
    -0.024396716411350872,
)


def taps():
    offsets = np.arange(-RADIUS, RADIUS + 1).astype(np.float64)
    weights = np.exp(-offsets * offsets / 8.0)
    weights = weights / weights.sum()
    return [float(weights[RADIUS + j]) for j in range(RADIUS + 1)]


def cosine_table(count):
    j = np.arange(count)[:, None].astype(np.float64)
    i = np.arange(count)[None, :].astype(np.float64)
    table = np.cos(np.pi * j * (i + 0.5) / count) * np.sqrt(2.0 / count)
    table[0] = np.sqrt(1.0 / count)
    return table


def two_parts(table):
    table = table.astype(np.float32)
    high = table.astype(ml_dtypes.bfloat16)
    low = (table - high.astype(np.float32)).astype(ml_dtypes.bfloat16)
    return np.ascontiguousarray(high), np.ascontiguousarray(low)


def inverse_eigen(count_az, count_rg):
    along_az = 2.0 - 2.0 * np.cos(np.pi * np.arange(count_az) / count_az)
    along_rg = 2.0 - 2.0 * np.cos(np.pi * np.arange(count_rg) / count_rg)
    return (1.0 / (DAMPING + along_az[:, None] + along_rg[None, :])).astype(np.float32)


def poly(coefficients, y):
    value = jnp.full_like(y, coefficients[-1])
    for c in coefficients[-2::-1]:
        value = value * y + c
    return value


def angle_turns(im, re):
    a, b = jnp.abs(im), jnp.abs(re)
    big, small = jnp.maximum(a, b), jnp.minimum(a, b)
    t = small / jnp.maximum(big, 1e-37)
    p = t * poly(ATAN, t * t)
    p = jnp.where(a > b, 0.25 - p, p)
    p = jnp.where(re < 0.0, 0.5 - p, p)
    return jnp.where(im < 0.0, -p, p)


def edge(phase_p, gain_p, phase_q, gain_q):
    delta = phase_q - phase_p
    delta = delta - jnp.round(delta)
    half = gain_p * gain_q * poly(COS, delta * delta)
    weight = half * half
    return weight, weight * delta


def encode_gain(value):
    return jnp.exp2(value * CODE_SPAN - 0.5 * CODE_SPAN).astype(jnp.bfloat16)


def decode_gain(code):
    return (jnp.log2(code.astype(jnp.float32)) + 0.5 * CODE_SPAN) * (1.0 / CODE_SPAN)


def encode_power(value, scale):
    share = jnp.minimum(jnp.abs(value) / jnp.maximum(scale, TINY), 1.0) * POWER_BASE
    for _ in range(4):
        share = share * share
    return jnp.where(value < 0.0, -share, share)


def decode_power(code, scale):
    share = jnp.exp2(jnp.log2(jnp.abs(code)) * (1.0 / 16.0)) * (scale * (1.0 / POWER_BASE))
    return jnp.where(code < 0.0, -share, share)


def split(value):
    high = value.astype(jnp.bfloat16)
    return high, (value - high.astype(jnp.float32)).astype(jnp.bfloat16)


def dot3(a, b):
    f = functools.partial(jnp.dot, preferred_element_type=jnp.float32)
    return f(a[0], b[1]) + f(a[1], b[0]) + f(a[0], b[0])


def lanes_of(shape):
    return lax.broadcasted_iota(jnp.int32, shape, 1)


def call(body, outs, args, scratch, name, smem_first=True, flops=1000000, out_space=pltpu.VMEM):
    specs = [pl.BlockSpec(memory_space=pltpu.VMEM)] * len(args)
    if smem_first:
        specs[0] = pl.BlockSpec(memory_space=pltpu.SMEM)
    return pl.pallas_call(
        body,
        out_shape=[jax.ShapeDtypeStruct(s, d) for s, d in outs],
        in_specs=specs,
        out_specs=[pl.BlockSpec(memory_space=out_space)] * len(outs),
        scratch_shapes=scratch,
        compiler_params=pltpu.CompilerParams(vmem_limit_bytes=VMEM_LIMIT),
        cost_estimate=pl.CostEstimate(flops=flops, bytes_accessed=4000000, transcendentals=0),
        name=name,
    )(*args)


def interior(body, outs, args, scratch):
    return pl.pallas_call(
        body,
        out_shape=[jax.ShapeDtypeStruct(s, d) for s, d in outs],
        in_specs=[pl.BlockSpec(memory_space=pltpu.SMEM)] + [pl.BlockSpec(memory_space=pltpu.HBM)] * 2
        + [pl.BlockSpec(memory_space=pltpu.VMEM)],
        out_specs=[pl.BlockSpec(memory_space=pltpu.VMEM)] * len(outs),
        scratch_shapes=scratch,
        compiler_params=pltpu.CompilerParams(vmem_limit_bytes=VMEM_LIMIT),
        cost_estimate=pl.CostEstimate(flops=8000000, bytes_accessed=4000000, transcendentals=0),
        name="interior",
    )(*args)


def phase_gain(smoothed):
    re, im, one, two = smoothed
    gain = jnp.sqrt(re * re + im * im) / (jnp.sqrt(one * two) + EPS)
    return angle_turns(im, re), jnp.sqrt(gain)


def products(ar, ai, br, bi, scale=None):
    ar, ai, br, bi = (v.astype(jnp.float32) for v in (ar, ai, br, bi))
    if scale is not None:
        ar, ai, br, bi = (v * scale for v in (ar, ai, br, bi))
    return (ar * br + ai * bi, ai * br - ar * bi, ar * ar + ai * ai, br * br + bi * bi)


def along_range(x):
    k = taps()
    n = x.shape[1]
    total = k[0] * x
    for j in range(1, RADIUS + 1):
        total = total + k[j] * (pltpu.roll(x, j, 1) + pltpu.roll(x, n - j, 1))
    return total


def along_azimuth(ref, f, row, rows, cs):
    k = taps()
    total = k[0] * ref[f, row : row + rows, cs]
    for j in range(1, RADIUS + 1):
        total = total + k[j] * (ref[f, row - j : row - j + rows, cs] + ref[f, row + j : row + j + rows, cs])
    return total


def end_weights(before):
    k = taps()
    sub = lax.broadcasted_iota(jnp.int32, (HALO, 1), 0)
    low = jnp.zeros((HALO, 1), jnp.float32)
    high = jnp.zeros((HALO, 1), jnp.float32)
    for j in range(RADIUS + 1):
        low = jnp.where(sub == (HALO - 1 - j if before else HALO - j), k[j], low)
        high = jnp.where(sub == (j - 1 if before else j), k[j], high)
    return low, high


def first_of_half(own, half, across):
    return (own & half) ^ (half if across else 0)


def window(lines, width, tile, columns, across, own, rows):
    half = columns // 2
    span = half * tile + 2 * LANES
    first_tile = first_of_half(own, half, across)
    start = pl.multiple_of(first_tile * tile, LANES)
    pixel = lanes_of((rows, span)) + (start - LANES)
    return first_tile, start, span, jnp.logical_and(pixel >= 0, pixel < width)


def range_table(tile_pair, out):
    k = taps()
    margin = (tile_pair - out) // 2
    table = np.zeros((tile_pair, out))
    for n in range(out):
        for j in range(-RADIUS, RADIUS + 1):
            table[n + margin + j, n] = k[abs(j)]
    return table


def interior_kernel(
    lines, width, tile, columns, across, ids, first, second, table, ranged, field, codes, rims, raw, high, low, sems
):
    half = columns // 2
    chunk = 16
    first_tile, start, span, _ = window(lines, width, tile, columns, across, ids[1], 8)
    upper = jnp.where(first_tile == 0, 0, 1)
    source = pl.multiple_of(upper * (width // 2 - 2 * LANES), LANES)
    target = pl.multiple_of((1 - upper) * 2 * LANES, LANES)
    size = width // 2 + 2 * LANES
    blank = pl.multiple_of(upper * size, LANES)
    copies = []
    for i in range(lines // chunk):
        rs = pl.ds(i * chunk, chunk)
        for a, ref in enumerate((first, second)):
            copy = pltpu.make_async_copy(
                ref.at[:, rs, pl.ds(source, size)], raw.at[a, :, rs, pl.ds(target, size)], sems.at[2 * i + a]
            )
            copy.start()
            copies.append(copy)
    for a in range(2):
        for part in range(2):
            raw[a, part, :, pl.ds(blank, 2 * LANES)] = jnp.zeros((lines, 2 * LANES), jnp.bfloat16)
    for i in range(lines // chunk):
        copies[2 * i].wait()
        copies[2 * i + 1].wait()
        rs = slice(i * chunk, (i + 1) * chunk)
        for c in range(0, span + 2 * LANES, 2 * LANES):
            cs = slice(c, c + 2 * LANES)
            values = products(raw[0, 0, rs, cs], raw[0, 1, rs, cs], raw[1, 0, rs, cs], raw[1, 1, rs, cs])
            for f in range(4):
                row = f * lines + i * chunk
                high[row : row + chunk, cs], low[row : row + chunk, cs] = split(values[f])
    block = 2 * LANES
    weights = table[0 : 2 * block, :], table[2 * block :, :]
    for c in range(0, span, block):
        cs = slice(c, c + 2 * block)
        total = dot3((high[:, cs], low[:, cs]), weights)
        if c == 0 or c + block == span:
            pixel = lanes_of(total.shape) + (start - LANES + c)
            total = jnp.where(jnp.logical_and(pixel >= 0, pixel < width), total, 0.0)
        for f in range(4):
            ranged[f, :, c : c + block] = total[f * lines : (f + 1) * lines, :]
    for c in range(0, span, LANES):
        cs = slice(c, c + LANES)
        steps = [(HALO, HALO)] + [(r, 16) for r in range(EDGE, lines - EDGE, 16)] + [(lines - EDGE, HALO)]
        for r, rows in steps:
            smoothed = [along_azimuth(ranged, f, r, rows, cs) for f in range(4)]
            phase, gain = phase_gain(smoothed)
            field[0, r - HALO : r - HALO + rows, cs] = phase
            field[1, r - HALO : r - HALO + rows, cs] = gain
            if rows == 16:
                at = slice(r - EDGE, r - EDGE + rows)
                codes[0, at, cs], codes[1, at, cs] = split(phase)
                codes[2, at, cs] = encode_gain(gain)
    groups = lines // 8
    for t in range(half):
        rims[t] = rim_block(field, groups, range(1, groups - 1), 1, t * tile, tile, None)


def rim_block(field, groups, which, first_group, start, tile, block, hint=None):
    lane = lanes_of((8, LANES))
    if block is None:
        block = jnp.zeros((8, LANES), jnp.float32)
    for f in range(2):
        for side in range(2):
            offset = start if side == 0 else start + LANES + tile
            at = slice(offset, offset + LANES) if hint is None else pl.ds(hint(offset, LANES), LANES)
            for g in which:
                target = (f * 2 + side) * groups + g
                row = 8 * (g - first_group)
                x = field[f, row : row + 8, at]
                shift = (target - (LANES - 1 if side == 0 else 0)) % LANES
                if shift:
                    x = pltpu.roll(x, shift, 1)
                block = jnp.where(lane == target, x, block)
    return block


def border_kernel(lines, width, tile, columns, across, ids, ranged, inside_field, codes, rims, from_pair, from_next, *rest):
    half = columns // 2
    outs, (prod, seg, field, ends) = rest[:half], rest[half:]
    own = ids[1]
    odd = ids[4]
    first_tile, start, span, in_image = window(lines, width, tile, columns, across, own, HALO)
    inside = (
        jnp.where(ids[2] == 0, 0.0, 1.0).astype(jnp.float32),
        jnp.where(ids[2] == ids[3] - 1, 0.0, 1.0).astype(jnp.float32),
    )
    zero = jnp.zeros((HALO, 2 * LANES), jnp.float32)
    own_rows = 2 * HALO
    for e in range(2):
        flag = odd if e == 0 else 1 - odd
        keep = flag.astype(jnp.float32)
        for f in range(4):
            prod[f, :, 0 : 2 * LANES] = zero
            prod[f, :, 2 * LANES + width :] = zero
        for c in range(0, width, 512):
            cs = slice(c, c + 512)
            parts = [
                from_pair[i, :, cs].astype(jnp.float32) * keep + from_next[i, :, cs].astype(jnp.float32) * (1.0 - keep)
                for i in range(4)
            ]
            values = products(*parts, inside[e])
            for f in range(4):
                prod[f, :, 2 * LANES + c : 2 * LANES + c + 512] = values[f]
        for f in range(4):
            total = along_range(prod[f, :, pl.ds(start, span + 2 * LANES)])[:, LANES : LANES + span]
            total = jnp.where(in_image, total, 0.0)
            if e == 0:
                seg[e, f, 0:HALO, :] = total
                seg[e, f, HALO:, :] = ranged[f, 0:own_rows, :]
            else:
                seg[e, f, own_rows:, :] = total
                seg[e, f, 0:own_rows, :] = ranged[f, lines - own_rows :, :]
    border = []
    for e in range(2):
        ref = seg.at[e]
        for c in range(0, span, LANES):
            cs = slice(c, c + LANES)
            smoothed = [along_azimuth(ref, f, HALO, HALO, cs) for f in range(4)]
            phase, gain = phase_gain(smoothed)
            field[0, e * HALO : (e + 1) * HALO, cs] = phase
            field[1, e * HALO : (e + 1) * HALO, cs] = gain
        low, high = end_weights(e == 0)
        r = 0 if e == 0 else own_rows - HALO
        border.append(
            [
                jnp.sum(low * ref[f, r : r + HALO, :] + high * ref[f, r + HALO : r + 2 * HALO, :], axis=0, keepdims=True)
                for f in range(4)
            ]
        )
    phase, gain = phase_gain([jnp.concatenate(pair, axis=0) for pair in zip(*border)])
    ends[0:2, :] = phase
    ends[2:4, :] = gain
    for e in range(2):
        ends[2 + e : 3 + e, :] = ends[2 + e : 3 + e, :] * inside[e]
    groups = lines // 8
    inner = lines - 2 * EDGE
    for n, s in enumerate(range(half, columns) if across else range(half)):
        out = outs[n]
        target = own ^ s
        local = pl.multiple_of((target - first_tile) * tile, LANES)
        cs = pl.ds(pl.multiple_of(local + LANES, LANES), tile)
        for i in range(3):
            out[i * lines + EDGE : i * lines + EDGE + inner, :] = codes[i, :, cs]
        for e in range(2):
            row = 0 if e == 0 else lines - EDGE
            rs = slice(e * HALO, (e + 1) * HALO)
            inner_rows = slice(0, HALO) if e == 0 else slice(lines - 3 * HALO, lines - 2 * HALO)
            pairs = [(field[i, rs, cs], inside_field[i, inner_rows, cs]) for i in range(2)]
            phase, gain = (jnp.concatenate(p if e == 0 else p[::-1], axis=0) for p in pairs)
            out[row : row + EDGE, :], out[lines + row : lines + row + EDGE, :] = split(phase)
            out[2 * lines + row : 2 * lines + row + EDGE, :] = encode_gain(gain)
        block = rims[target - first_tile]
        block = rim_block(field, groups, (0,), 0, local, tile, block, pl.multiple_of)
        block = rim_block(field, groups, (groups - 1,), groups - 2, local, tile, block, pl.multiple_of)
        rows = []
        for i in range(4):
            for h in range(tile // LANES):
                rows.append(ends[i : i + 1, pl.ds(pl.multiple_of(local + (h + 1) * LANES, LANES), LANES)])
        block = jnp.concatenate([block, jnp.concatenate(rows, axis=0)], axis=1)
        out[3 * lines :, :] = jnp.concatenate(split(block), axis=0)


def strip_kernel(lines, width, tile, columns, exchange, ids, first, second, above, below, *rest):
    n_out = len(rest) - 3
    outs, (prod, ranged, field) = rest[:n_out], rest[n_out:]
    k = taps()
    own = ids[1]
    inside_above = jnp.where(ids[2] == 0, 0.0, 1.0).astype(jnp.float32)
    inside_below = jnp.where(ids[2] == ids[3] - 1, 0.0, 1.0).astype(jnp.float32)
    height = lines + 2 * HALO

    zero = jnp.zeros((height, LANES), jnp.float32)
    for f in range(4):
        prod[f, :, 0:LANES] = zero
        prod[f, :, LANES + width :] = zero
    step = min(width, 512)
    for c in range(0, width, step):
        at = slice(LANES + c, LANES + c + step)
        cs = slice(c, c + step)
        rows = min(lines, 16)
        for r in range(0, lines, rows):
            rs = slice(r, r + rows)
            values = products(first[0, rs, cs], first[1, rs, cs], second[0, rs, cs], second[1, rs, cs])
            for f in range(4):
                prod[f, HALO + r : HALO + r + rows, at] = values[f]
        for ref, r, scale in ((above, 0, inside_above), (below, HALO + lines, inside_below)):
            values = products(ref[0, :, cs], ref[1, :, cs], ref[2, :, cs], ref[3, :, cs], scale)
            for f in range(4):
                prod[f, r : r + HALO, at] = values[f]

    step = min(width, 1024)
    for f in range(4):
        for r in range(0, height, 8):
            for c in range(0, width, step):
                x = prod[f, r : r + 8, c : c + step + 2 * LANES]
                n = step + 2 * LANES
                total = k[0] * x
                for j in range(1, RADIUS + 1):
                    total = total + k[j] * (pltpu.roll(x, j, 1) + pltpu.roll(x, n - j, 1))
                ranged[f, r : r + 8, c : c + step] = total[:, LANES : LANES + step]

    for f in range(2):
        field[f, :, 0:LANES] = zero[:lines]
        field[f, :, LANES + width :] = zero[:lines]
    rows = min(lines, 32)
    sub = lax.broadcasted_iota(jnp.int32, (HALO, 1), 0)
    low = jnp.zeros((HALO, 1), jnp.float32)
    high = jnp.zeros((HALO, 1), jnp.float32)
    for j in range(RADIUS + 1):
        low = jnp.where(sub == HALO - 1 - j, k[j], low)
        high = jnp.where(sub == j - 1, k[j], high)
    top, bottom = [], []
    for c in range(0, width, LANES):
        cs = slice(c, c + LANES)
        for r in range(0, lines, rows):
            smoothed = []
            for f in range(4):
                b = HALO + r
                total = k[0] * ranged[f, b : b + rows, cs]
                for j in range(1, RADIUS + 1):
                    total = total + k[j] * (
                        ranged[f, b - j : b - j + rows, cs] + ranged[f, b + j : b + j + rows, cs]
                    )
                smoothed.append(total)
            phase, gain = phase_gain(smoothed)
            field[0, r : r + rows, LANES + c : 2 * LANES + c] = phase
            field[1, r : r + rows, LANES + c : 2 * LANES + c] = gain

    step = min(width, 1024)
    low = low + jnp.zeros((HALO, step), jnp.float32)
    high = high + jnp.zeros((HALO, step), jnp.float32)
    mirror_low = jnp.zeros((HALO, 1), jnp.float32)
    mirror_high = jnp.zeros((HALO, 1), jnp.float32)
    for j in range(RADIUS + 1):
        mirror_high = jnp.where(sub == j, k[j], mirror_high)
        mirror_low = jnp.where(sub == HALO - j, k[j], mirror_low)
    ends = []
    for c in range(0, width, step):
        cs = slice(c, c + step)
        up = [
            jnp.sum(low * ranged[f, 0:HALO, cs] + high * ranged[f, HALO : 2 * HALO, cs], axis=0, keepdims=True)
            for f in range(4)
        ]
        down = [
            jnp.sum(
                mirror_low * ranged[f, lines : lines + HALO, cs]
                + mirror_high * ranged[f, lines + HALO : lines + 2 * HALO, cs],
                axis=0,
                keepdims=True,
            )
            for f in range(4)
        ]
        up_phase, up_gain = phase_gain(up)
        down_phase, down_gain = phase_gain(down)
        ends.append((up_phase, down_phase, up_gain * inside_above, down_gain * inside_below))
    for i, (a, b, c_, d) in enumerate(ends):
        at = slice(i * step, (i + 1) * step)
        prod[0, 0:1, at] = a
        prod[0, 1:2, at] = b
        prod[0, 2:3, at] = c_
        prod[0, 3:4, at] = d

    groups = lines // 8
    lane = lanes_of((8, LANES))

    def pack(out, start, aligned):
        hint = pl.multiple_of if aligned else (lambda v, _: v)
        out[0:lines, :] = field[0, :, pl.ds(hint(start + LANES, LANES), tile)]
        out[lines : 2 * lines, :] = field[1, :, pl.ds(hint(start + LANES, LANES), tile)]
        block = jnp.zeros((8, LANES), jnp.float32)
        for f in range(2):
            for side in range(2):
                offset = start if side == 0 else start + LANES + tile
                for g in range(groups):
                    target = (f * 2 + side) * groups + g
                    x = field[f, 8 * g : 8 * g + 8, pl.ds(hint(offset, LANES), LANES)]
                    shift = (target - (LANES - 1 if side == 0 else 0)) % LANES
                    if shift:
                        x = pltpu.roll(x, shift, 1)
                    block = jnp.where(lane == target, x, block)
        base = 2 * lines
        out[base : base + 8, 0:LANES] = block
        for i in range(4):
            for h in range(tile // LANES):
                out[base + 2 * i + h : base + 2 * i + h + 1, LANES : 2 * LANES] = prod[
                    0, i : i + 1, pl.ds(hint(start + h * LANES, LANES), LANES)
                ]

    if exchange == "permute":
        for s in range(columns):
            pack(outs[s], (own ^ s) * tile, True)
    else:
        for s in range(columns):
            pack(outs[0].at[s], s * tile, False)


def precondition(field, tables, inverse):
    az, az_t, rg, rg_t = tables
    coef = dot3(az, split(field))
    coef = dot3(split(coef), rg_t)
    coef = coef * inverse[...]
    back = dot3(az_t, split(coef))
    return dot3(split(back), rg)


def table_pairs(tables):
    pairs = []
    for ref in tables:
        n = ref.shape[1]
        parts = [ref[i * n : (i + 1) * n, :] for i in range(4)]
        pairs += [(parts[0], parts[1]), (parts[2], parts[3])]
    return pairs


def line_groups(ref, tile_az, edge_lane):
    lane = lanes_of((8, LANES))
    first = (edge_lane // LANES) * LANES
    block = jnp.zeros((8, LANES), jnp.float32)
    for g in range(tile_az // 8):
        x = ref[8 * g : 8 * g + 8, first : first + LANES]
        shift = (g - edge_lane) % LANES
        if shift:
            x = pltpu.roll(x, shift, 1)
        block = jnp.where(lane == g, x, block)
    return block


def spread_groups(block, first_group, count, target_lane, base=0):
    parts = []
    for g in range(first_group, first_group + count):
        shift = (target_lane - (base + g)) % LANES
        parts.append(pltpu.roll(block, shift, 1) if shift else block)
    return jnp.concatenate(parts, axis=0) if count > 1 else parts[0]


def shifted_right(x, left):
    lane = lanes_of(x.shape)
    if left is None:
        return jnp.where(lane == 0, 0.0, pltpu.roll(x, 1, 1))
    wide = jnp.concatenate([left] * (x.shape[1] // LANES), axis=1)
    return jnp.where(lane == 0, wide, pltpu.roll(x, 1, 1))


def shifted_left(x, right):
    lane = lanes_of(x.shape)
    wide = jnp.concatenate([right] * (x.shape[1] // LANES), axis=1)
    return jnp.where(lane == x.shape[1] - 1, wide, pltpu.roll(x, x.shape[1] - 1, 1))


def divergence(tile_az, step, along_x, rim_x, along_y, r):
    rs = slice(r, r + step)
    x = along_x[rs, :]
    return (x - shifted_left(x, rim_x[rs, :])) + along_y[rs, :] - along_y[r + 1 : r + 1 + step, :]


def edges_of(lines, count, tile, coded, sources, scratch, outs):
    phase, gain, sides, ends = scratch
    weight_x, flux_x, rim_x, flux_rim, weight_y, flux_y, weight_end, flux_end = outs
    height = count * lines
    for src, strip in sources:
        if coded:
            row, at = pl.multiple_of(strip * lines, 8), pl.ds(pl.multiple_of(strip * 8, 8), 8)
            phase[pl.ds(HALO + row, lines), :] = src[0:lines, :].astype(jnp.float32) + src[
                lines : 2 * lines, :
            ].astype(jnp.float32)
            gain[pl.ds(HALO + row, lines), :] = decode_gain(src[2 * lines : 3 * lines, :])
            both = src[3 * lines :, :].astype(jnp.float32)
            block = both[0:8, :] + both[8:16, :]
        else:
            row, at = strip * lines, pl.ds(strip * 8, 8)
            phase[pl.ds(HALO + row, lines), :] = src[0:lines, :]
            gain[pl.ds(HALO + row, lines), :] = src[lines : 2 * lines, :]
            block = src[2 * lines : 2 * lines + 8, :]
        sides[at, :] = block[:, 0:LANES]
        ends[at, :] = block[:, LANES : 2 * LANES]
    last = 8 * (count - 1)
    for h in range(tile // LANES):
        cs = slice(h * LANES, (h + 1) * LANES)
        phase[HALO - 1 : HALO, cs] = ends[h : h + 1, :]
        gain[HALO - 1 : HALO, cs] = ends[4 + h : 5 + h, :]
        phase[HALO + height : HALO + height + 1, cs] = ends[last + 2 + h : last + 3 + h, :]
        gain[HALO + height : HALO + height + 1, cs] = ends[last + 6 + h : last + 7 + h, :]

    step = min(height, 32)
    groups = lines // 8
    for r in range(0, height, step):
        rs = slice(r, r + step)
        b = HALO + r
        p, g = phase[b : b + step, :], gain[b : b + step, :]
        halo = []
        for f in range(2):
            for side in range(2):
                parts = []
                for line_group in range(r // 8, (r + step) // 8):
                    strip, inner = divmod(line_group, groups)
                    block = sides[8 * strip : 8 * strip + 8, :]
                    source_lane = (f * 2 + side) * groups + inner
                    shift = ((0 if side == 0 else LANES - 1) - source_lane) % LANES
                    parts.append(pltpu.roll(block, shift, 1) if shift else block)
                halo.append(jnp.concatenate(parts, axis=0) if len(parts) > 1 else parts[0])
        weight_x[rs, :], flux_x[rs, :] = edge(shifted_right(p, halo[0]), shifted_right(g, halo[2]), p, g)
        rim_x[rs, :], flux_rim[rs, :] = edge(p[:, tile - LANES :], g[:, tile - LANES :], halo[1], halo[3])
        weight_y[rs, :], flux_y[rs, :] = edge(phase[b - 1 : b - 1 + step, :], gain[b - 1 : b - 1 + step, :], p, g)
    b = HALO + height
    w, f = edge(phase[b - 1 : b, :], gain[b - 1 : b, :], phase[b : b + 1, :], gain[b : b + 1, :])
    weight_end[...] = jnp.broadcast_to(w, (8, tile))
    flux_end[...] = jnp.broadcast_to(f, (8, tile))


def far_kernel(lines, tile, columns, ids, *rest):
    half = columns // 2
    own = ids[1]
    sources = [(rest[n], (own ^ n) & (half - 1)) for n in range(half)]
    edges_of(lines, half, tile, True, sources, rest[half + 8 :], rest[half : half + 8])


def tile_kernel(lines, tile_az, tile, columns, exchange, ids, *rest):
    coded = exchange == "permute"
    half = columns // 2
    own = ids[1]
    count = half if coded else columns
    if coded:
        sources = [(rest[s], (own ^ s) & (half - 1)) for s in range(half)]
        far, rest = rest[half : half + 8], rest[half + 8 :]
    else:
        sources = [(rest[0].at[s], s) for s in range(columns)]
        rest = rest[1:]
    tables, inverse = rest[:2], rest[2]
    residual, shaped, weight_x, rim_x, weight_y, row_pair, row_next, col_pair, col_next = rest[3:12]
    phase, gain, sides, ends, flux_x, flux_rim, flux_y, weight_end, flux_end = rest[12:]
    pairs = table_pairs(tables)
    height = count * lines
    whole = (weight_x, flux_x, rim_x, flux_rim, weight_y, flux_y)
    if coded:
        lower = (own & half) // half
        at = pl.ds(pl.multiple_of(lower * height, 8), height)
        outs = [ref.at[at, :] for ref in whole]
    else:
        outs = [ref.at[pl.ds(0, height), :] for ref in whole]
    edges_of(
        lines, count, tile, coded, sources, (phase, gain, sides, ends), (*outs, weight_end, flux_end)
    )
    w, f = weight_end[...], flux_end[...]
    if coded:
        at = pl.ds(pl.multiple_of((1 - lower) * height, 8), height)
        for source, ref in zip(far, whole):
            ref[at, :] = source[...]
        w, f = jnp.where(lower == 1, w, far[6][...]), jnp.where(lower == 1, f, far[7][...])
    weight_y[tile_az : tile_az + 8, :] = w
    flux_y[tile_az : tile_az + 8, :] = f

    step = min(tile_az, 32)
    for r in range(0, tile_az, step):
        residual[r : r + step, :] = TURN * divergence(tile_az, step, flux_x, flux_rim, flux_y, r)
    shaped[...] = precondition(residual[...], pairs, inverse)
    row_odd, col_odd = ids[5] == 1, ids[4] == 1
    top = jnp.concatenate([shaped[0:1, h : h + LANES] for h in range(0, tile, LANES)], axis=0)
    bottom = jnp.concatenate([shaped[tile_az - 1 : tile_az, h : h + LANES] for h in range(0, tile, LANES)], axis=0)
    row_pair[0:2, :] = jnp.where(row_odd, top, bottom)
    row_next[0:2, :] = jnp.where(row_odd, bottom, top)
    left = line_groups(shaped, tile_az, 0)
    right = line_groups(shaped, tile_az, tile - 1)
    col_pair[...] = jnp.where(col_odd, left, right)
    col_next[...] = jnp.where(col_odd, right, left)


def apply_operator(tile_az, tile, u, weight_x, rim_x, weight_y, flux_x, flux_rim, flux_y, left, right, out):
    step = min(tile_az, 32)
    for r in range(0, tile_az, step):
        rs = slice(r, r + step)
        b = HALO + r
        x = u[b : b + step, :]
        l = None if left is None else spread_groups(left, r // 8, step // 8, 0)
        flux_x[rs, :] = weight_x[rs, :] * (x - shifted_right(x, l))
        edge_x = x[:, tile - LANES :]
        if right is None:
            flux_rim[rs, :] = -rim_x[rs, :] * edge_x
        else:
            flux_rim[rs, :] = rim_x[rs, :] * (spread_groups(right, r // 8, step // 8, LANES - 1) - edge_x)
        flux_y[rs, :] = weight_y[rs, :] * (x - u[b - 1 : b - 1 + step, :])
    b = HALO + tile_az
    flux_y[tile_az : tile_az + 1, :] = weight_y[tile_az : tile_az + 1, :] * (u[b : b + 1, :] - u[b - 1 : b, :])
    for r in range(0, tile_az, step):
        out[r : r + step, :] = DAMPING * u[HALO + r : HALO + r + step, :] + divergence(
            tile_az, step, flux_x, flux_rim, flux_y, r
        )


def inner(a, b, tile_az, offset_a=0, offset_b=0):
    total = jnp.zeros((32, a.shape[1]), jnp.float32)
    for r in range(0, tile_az, 32):
        total = total + a[offset_a + r : offset_a + r + 32, :] * b[offset_b + r : offset_b + r + 32, :]
    return jnp.sum(jnp.sum(total, axis=0, keepdims=True), axis=1, keepdims=True)


def second_kernel(
    tile_az, tile, ids, residual, shaped, weight_x, rim_x, weight_y, col_next, col_pair, row_next, row_pair, *rest
):
    tables, inverse = rest[:2], rest[2]
    operated, shaped2, operated2, chunk, roots = rest[3:8]
    u, flux_x, flux_rim, flux_y = rest[8:]
    pairs = table_pairs(tables)
    row_odd, col_odd = ids[5] == 1, ids[4] == 1
    up = jnp.where(row_odd, row_pair[0:2, :], row_next[0:2, :])
    down = jnp.where(row_odd, row_next[0:2, :], row_pair[0:2, :])
    left = jnp.where(col_odd, col_pair[...], col_next[...])
    right = jnp.where(col_odd, col_next[...], col_pair[...])
    u[HALO : HALO + tile_az, :] = shaped[...]
    for h in range(tile // LANES):
        cs = slice(h * LANES, (h + 1) * LANES)
        u[HALO - 1 : HALO, cs] = up[h : h + 1, :]
        u[HALO + tile_az : HALO + tile_az + 1, cs] = down[h : h + 1, :]
    apply_operator(
        tile_az, tile, u, weight_x, rim_x, weight_y, flux_x, flux_rim, flux_y, left, right, operated
    )
    image = precondition(operated[...], pairs, inverse)
    shaped2[...] = image
    u[HALO : HALO + tile_az, :] = image
    apply_operator(
        tile_az, tile, u, weight_x, rim_x, weight_y, flux_x, flux_rim, flux_y, left, right, operated2
    )
    lane = lanes_of((1, LANES))
    sums = jnp.zeros((1, LANES), jnp.float32)
    for i, (a, b) in enumerate(
        (
            (residual, shaped),
            (shaped, operated),
            (residual, shaped2),
            (operated, shaped2),
            (shaped2, operated2),
        )
    ):
        sums = jnp.where(lane == i, inner(a, b, tile_az), sums)
    def rows_of(x):
        return jnp.concatenate([x[:, h : h + LANES] for h in range(0, tile, LANES)], axis=0)

    weight_t, weight_b = rows_of(weight_y[0:1, :]), rows_of(weight_y[tile_az : tile_az + 1, :])
    weight_l, weight_r = line_groups(weight_x, tile_az, 0), line_groups(rim_x, tile_az, LANES - 1)
    top = rows_of(image_row(shaped2, shaped, 0))
    bottom = rows_of(image_row(shaped2, shaped, tile_az - 1))
    left_rim = line_groups(shaped2, tile_az, 0) - line_groups(shaped, tile_az, 0)
    right_rim = line_groups(shaped2, tile_az, tile - 1) - line_groups(shaped, tile_az, tile - 1)
    known = jnp.sum(weight_t * up * top + weight_b * down * bottom, keepdims=True) + jnp.sum(
        weight_l * left * left_rim + weight_r * right * right_rim, keepdims=True
    )
    sums = jnp.where(lane == 4, sums - known, sums)
    half = tile_az // 8
    wide = lanes_of((8, LANES))
    root_sides = jnp.sqrt(jnp.where(wide < half, weight_l, pltpu.roll(weight_r, half, 1)))
    sides = root_sides * jnp.where(wide < half, left_rim, pltpu.roll(right_rim, half, 1))
    root_ends = jnp.sqrt(jnp.concatenate([weight_t, weight_b], axis=0))
    ends = root_ends * jnp.concatenate([top, bottom], axis=0)
    scale = jnp.maximum(jnp.max(jnp.abs(sides), keepdims=True), jnp.max(jnp.abs(ends), keepdims=True))
    scale = (scale * 1.01).astype(jnp.bfloat16).astype(jnp.float32)
    sums = jnp.where(lane == SCALE_LANE, scale, sums)
    high = sums.astype(jnp.bfloat16).astype(jnp.float32)
    middle = (sums - high).astype(jnp.bfloat16).astype(jnp.float32)
    rest_ = sums - high - middle
    sums = high + pltpu.roll(middle, 8, 1) + pltpu.roll(rest_, 16, 1)
    chunk[...] = jnp.concatenate(
        [encode_power(sides, scale), encode_power(ends, scale), jnp.broadcast_to(sums, (4, LANES))], axis=0
    ).astype(jnp.bfloat16)
    roots[...] = jnp.concatenate([root_sides, root_ends, root_ends], axis=0)


def image_row(a, b, row):
    return a[row : row + 1, :] - b[row : row + 1, :]


def last_kernel(
    tile_az, tile, rows, columns, ids, gathered, residual, shaped, operated, shaped2, operated2, roots,
    solution_hbm, residual_hbm, solution_out, residual_out, sems
):
    half = tile_az // 8
    lane = lanes_of((8, LANES))
    total = jnp.zeros((4, LANES), jnp.float32)
    cross_x = jnp.zeros((8, LANES), jnp.float32)
    cross_y = jnp.zeros((2, LANES), jnp.float32)
    values = {}

    def decoded(i):
        x = gathered[i].astype(jnp.float32)
        return jnp.concatenate([decode_power(x[0:12, :], x[12:13, SCALE_LANE : SCALE_LANE + 1]), x[12:16, :]], axis=0)

    def value_of(i):
        if i not in values:
            values[i] = decoded(i)
        return values[i]

    for r in range(rows):
        for c in range(columns):
            i = r * columns + c
            here = value_of(i)
            total = total + here[12:16, :]
            if c + 1 < columns:
                cross_x = cross_x + pltpu.roll(here[0:8, :], LANES - half, 1) * value_of(i + 1)[0:8, :]
            if r + 1 < rows:
                cross_y = cross_y + here[10:12, :] * value_of(i + columns)[8:10, :]
    cross = jnp.sum(jnp.where(lane < half, cross_x, 0.0), keepdims=True) + jnp.sum(cross_y, keepdims=True)
    wide = total[0:1, :]
    first_lane = lanes_of((1, LANES))
    pick = [
        jnp.sum(jnp.where(first_lane % 8 == i, jnp.where(first_lane < 24, wide, 0.0), 0.0), axis=1, keepdims=True)
        for i in range(5)
    ]
    dot0, curve0, mixed, cross_dot, curve2 = pick
    curve2 = curve2 - 2.0 * cross
    alpha = dot0 / curve0
    fresh = dot0 - alpha * (mixed + curve0) + alpha * alpha * cross_dot
    beta = fresh / dot0
    grown = 1.0 + beta
    curve1 = grown * grown * curve0 - 2.0 * alpha * grown * cross_dot + alpha * alpha * curve2
    step1 = fresh / curve1
    on_first = alpha + step1 * grown
    on_second = step1 * alpha

    row, col = ids[0], ids[1]
    here = row * columns + col

    def neighbour(ok, index):
        return jnp.where(ok, index, here), jnp.where(ok, 1.0, 0.0).astype(jnp.float32)

    up, up_ok = neighbour(row > 0, here - columns)
    down, down_ok = neighbour(row < rows - 1, here + columns)
    left, left_ok = neighbour(col > 0, here - 1)
    right, right_ok = neighbour(col < columns - 1, here + 1)
    near = [decoded(i) for i in (left, right, up, down)]
    from_left = pltpu.roll(near[0][0:8, :], LANES - half, 1) * left_ok
    from_right = pltpu.roll(near[1][0:8, :], half, 1) * right_ok
    top = jnp.concatenate([near[2][10 + h : 11 + h, :] for h in range(tile // LANES)], axis=1) * up_ok
    bottom = jnp.concatenate([near[3][8 + h : 9 + h, :] for h in range(tile // LANES)], axis=1) * down_ok
    top = top * jnp.concatenate([roots[8 + h : 9 + h, :] for h in range(tile // LANES)], axis=1)
    bottom = bottom * jnp.concatenate([roots[10 + h : 11 + h, :] for h in range(tile // LANES)], axis=1)
    from_left = from_left * roots[0:8, :]
    from_right = from_right * roots[0:8, :]
    step = min(tile_az, 64)
    copies = []
    for r in range(0, tile_az, step):
        rs = slice(r, r + step)
        solution_out[rs, :] = on_first * shaped[rs, :] - on_second * shaped2[rs, :]
        q = operated2[rs, :]
        wide = lanes_of((step, tile))
        l = jnp.concatenate([spread_groups(from_left, r // 8, step // 8, 0)] * (tile // LANES), axis=1)
        q = q - jnp.where(wide == 0, l, 0.0)
        l = jnp.concatenate([spread_groups(from_right, r // 8, step // 8, LANES - 1, half)] * (tile // LANES), axis=1)
        q = q - jnp.where(wide == tile - 1, l, 0.0)
        if r == 0 or r + step == tile_az:
            deep = lax.broadcasted_iota(jnp.int32, (step, tile), 0)
        if r == 0:
            q = q - jnp.where(deep == 0, jnp.broadcast_to(top, (step, tile)), 0.0)
        if r + step == tile_az:
            q = q - jnp.where(deep == step - 1, jnp.broadcast_to(bottom, (step, tile)), 0.0)
        residual_out[rs, :] = residual[rs, :] - on_first * operated[rs, :] + on_second * q
        for n, (src, dst) in enumerate(((solution_out, solution_hbm), (residual_out, residual_hbm))):
            copy = pltpu.make_async_copy(src.at[rs, :], dst.at[rs, :], sems.at[2 * (r // step) + n])
            copy.start()
            copies.append(copy)
    for copy in copies:
        copy.wait()


def swapped(value, axis, count, step):
    if step == 0:
        pairs = [(i, i ^ 1) for i in range(count)]
    else:
        pairs = [(i, (i + 1 if i % 2 else i - 1) % count) for i in range(count)]
    return lax.ppermute(value, axis, pairs)


def shards(rows, columns, first_slc, second_slc):
    lines, width = first_slc.shape[1:]
    tile = width // columns
    tile_az = lines * columns
    axes = ("row", "col")
    exchange = "permute" if lines >= 4 * EDGE and columns <= 8 else "all_to_all"
    row, col = lax.axis_index("row"), lax.axis_index("col")
    ids = jnp.stack([row, col, row * columns + col, jnp.int32(rows * columns), col % 2, row % 2]).astype(jnp.int32)
    f32, bf16 = jnp.float32, jnp.bfloat16

    head = jnp.concatenate([first_slc[:, :HALO], second_slc[:, :HALO]], 0)
    tail = jnp.concatenate([first_slc[:, -HALO:], second_slc[:, -HALO:]], 0)
    odd = col % 2 == 1
    from_pair = swapped(jnp.where(odd, head, tail), axes, rows * columns, 0)
    from_next = swapped(jnp.where(odd, tail, head), axes, rows * columns, 1)
    wide = width + 2 * LANES
    if exchange == "permute":
        half = columns // 2
        span = half * tile + 2 * LANES
        smoothing = jnp.asarray(np.concatenate(two_parts(range_table(4 * LANES, 2 * LANES)), axis=0))
        sent = [None] * columns
        sources = (first_slc, second_slc)
        for across in (True, False):
            ranged, inner, codes, rims = interior(
                functools.partial(interior_kernel, lines, width, tile, columns, across),
                [
                    ((4, lines, span), f32),
                    ((2, lines - 2 * HALO, span), f32),
                    ((3, lines - 2 * EDGE, span), bf16),
                    ((half, 8, LANES), f32),
                ],
                (ids, *sources, smoothing),
                [
                    pltpu.VMEM((2, 2, lines, span + 2 * LANES), bf16),
                    pltpu.VMEM((4 * lines, span + 2 * LANES), bf16),
                    pltpu.VMEM((4 * lines, span + 2 * LANES), bf16),
                    pltpu.SemaphoreType.DMA((lines // 8,)),
                ],
            )
            part = call(
                functools.partial(border_kernel, lines, width, tile, columns, across),
                [((3 * lines + 16, tile), bf16)] * half,
                (ids, ranged, inner, codes, rims, from_pair, from_next),
                [
                    pltpu.VMEM((4, HALO, width + 4 * LANES), f32),
                    pltpu.VMEM((2, 4, 3 * HALO, span), f32),
                    pltpu.VMEM((2, 2 * HALO, span), f32),
                    pltpu.VMEM((8, span), f32),
                ],
                "borders",
            )
            for i, value in enumerate(part):
                sent[i + (half if across else 0)] = value
            if across:
                *part, first_slc, second_slc = lax.optimization_barrier((*part, first_slc, second_slc))
                sources = (first_slc, second_slc)
                for i, value in enumerate(part):
                    sent[i + half] = value
        arrived = [sent[0]] + [
            lax.ppermute(sent[s], "col", [(i, i ^ s) for i in range(columns)]) for s in range(1, columns)
        ]
    else:
        above = jnp.where(odd, from_pair, from_next)
        below = jnp.where(odd, from_next, from_pair)
        height = lines + 2 * HALO
        sent = call(
            functools.partial(strip_kernel, lines, width, tile, columns, exchange),
            [((columns, 2 * lines + 8, tile), f32)],
            (ids, first_slc, second_slc, above, below),
            [pltpu.VMEM((4, height, wide), f32), pltpu.VMEM((4, height, width), f32), pltpu.VMEM((2, lines, wide), f32)],
            "strips",
        )
        arrived = [lax.all_to_all(sent[0], "col", 0, 0, tiled=True)]

    tables = []
    for table in (cosine_table(tile_az), cosine_table(tile)):
        parts = [*two_parts(table), *two_parts(table.T)]
        tables.append(jnp.asarray(np.concatenate(parts, axis=0)))
    inverse = jnp.asarray(inverse_eigen(tile_az, tile))

    whole = ((tile_az, tile), f32)
    block = ((8, LANES), f32)
    padded = pltpu.VMEM((tile_az + 2 * HALO, tile), f32)
    fluxes = [
        pltpu.VMEM((tile_az, tile), f32),
        pltpu.VMEM((tile_az, LANES), f32),
        pltpu.VMEM((tile_az + 8, tile), f32),
    ]
    edge_rows = tile_az
    if exchange == "permute":
        edge_rows = half * lines
        part = ((edge_rows, tile), f32)
        side = ((edge_rows, LANES), f32)
        last = ((8, tile), f32)
        far = call(
            functools.partial(far_kernel, lines, tile, columns),
            [part, part, side, side, part, part, last, last],
            (ids, *arrived[half:]),
            [
                pltpu.VMEM((edge_rows + 2 * HALO, tile), f32),
                pltpu.VMEM((edge_rows + 2 * HALO, tile), f32),
                pltpu.VMEM((8 * half, LANES), f32),
                pltpu.VMEM((8 * half, LANES), f32),
            ],
            "far",
        )
        arrived = [*arrived[:half], *far]
    gathered_lines = pltpu.VMEM((edge_rows + 2 * HALO, tile), f32)
    residual, shaped, weight_x, rim_x, weight_y, row_pair, row_next, col_pair, col_next = call(
        functools.partial(tile_kernel, lines, tile_az, tile, columns, exchange),
        [whole, whole, whole, ((tile_az, LANES), f32), ((tile_az + 8, tile), f32), block, block, block, block],
        (ids, *arrived, *tables, inverse),
        [
            gathered_lines,
            gathered_lines,
            pltpu.VMEM((8 * columns, LANES), f32),
            pltpu.VMEM((8 * columns, LANES), f32),
            *fluxes,
            pltpu.VMEM((8, tile), f32),
            pltpu.VMEM((8, tile), f32),
        ],
        "tiles",
    )
    col_next = swapped(col_next, "col", columns, 1)
    col_pair = swapped(col_pair, "col", columns, 0)
    row_next = swapped(row_next, "row", rows, 1)
    row_pair = swapped(row_pair, "row", rows, 0)
    rims = (col_next, col_pair, row_next, row_pair)
    operated, shaped2, operated2, chunk, roots = call(
        functools.partial(second_kernel, tile_az, tile),
        [whole, whole, whole, ((16, LANES), bf16), ((16, LANES), f32)],
        (ids, residual, shaped, weight_x, rim_x, weight_y, *rims, *tables, inverse),
        [padded, *fluxes],
        "operator",
    )
    spread = jnp.broadcast_to(chunk[None], (rows * columns, 16, LANES))
    gathered = lax.all_to_all(spread, axes, 0, 0, tiled=True)
    return tuple(
        call(
            functools.partial(last_kernel, tile_az, tile, rows, columns),
            [whole, whole],
            (ids, gathered, residual, shaped, operated, shaped2, operated2, roots),
            [
                pltpu.VMEM((tile_az, tile), f32),
                pltpu.VMEM((tile_az, tile), f32),
                pltpu.SemaphoreType.DMA((2 * (tile_az // min(tile_az, 64)),)),
            ],
            "finish",
            out_space=pltpu.HBM,
        )
    )


def solution(mesh):
    placed = P(None, ("row", "col"), None)
    return jax.shard_map(
        functools.partial(shards, mesh.shape["row"], mesh.shape["col"]),
        mesh=mesh,
        in_specs=(placed, placed),
        out_specs=(P("row", "col"), P("row", "col")),
        check_vma=False,
    )
```

```python
import functools
import math

import jax
import jax.numpy as jnp
import ml_dtypes
import numpy as np
from jax import lax
from jax.experimental import pallas as pl
from jax.experimental.pallas import tpu as pltpu
from jax.sharding import PartitionSpec as P

EPS = 1e-05
DAMPING = 0.0001
RADIUS = 4
LANES = 128
HALO = 8
EDGE = 16
TURN = 2.0 * math.pi
CODE_SPAN = 248.0
POWER_BASE = 2.0**7.5
TINY = 1e-30
SCALE_LANE = 5
VMEM_LIMIT = 40 * 1024 * 1024

ATAN = (
    0.1591549409219458,
    -0.05305126669892651,
    0.03181993346630217,
    -0.022611352052724496,
    0.016957432021882463,
    -0.011990188139443825,
    0.0068498925926071,
    -0.002591499099089036,
    0.00046210915702298266,
)
COS = (
    0.9999999997806517,
    -4.934802137228286,
    4.0587091643402005,
    -1.3352120566397616,
    0.23493755882899706,
    -0.024396716411350872,
)


def taps():
    offsets = np.arange(-RADIUS, RADIUS + 1).astype(np.float64)
    weights = np.exp(-offsets * offsets / 8.0)
    weights = weights / weights.sum()
    return [float(weights[RADIUS + j]) for j in range(RADIUS + 1)]


def cosine_table(count):
    j = np.arange(count)[:, None].astype(np.float64)
    i = np.arange(count)[None, :].astype(np.float64)
    table = np.cos(np.pi * j * (i + 0.5) / count) * np.sqrt(2.0 / count)
    table[0] = np.sqrt(1.0 / count)
    return table


def two_parts(table):
    table = table.astype(np.float32)
    high = table.astype(ml_dtypes.bfloat16)
    low = (table - high.astype(np.float32)).astype(ml_dtypes.bfloat16)
    return np.ascontiguousarray(high), np.ascontiguousarray(low)


def inverse_eigen(count_az, count_rg):
    along_az = 2.0 - 2.0 * np.cos(np.pi * np.arange(count_az) / count_az)
    along_rg = 2.0 - 2.0 * np.cos(np.pi * np.arange(count_rg) / count_rg)
    return (1.0 / (DAMPING + along_az[:, None] + along_rg[None, :])).astype(np.float32)


def poly(coefficients, y):
    value = jnp.full_like(y, coefficients[-1])
    for c in coefficients[-2::-1]:
        value = value * y + c
    return value


def angle_turns(im, re):
    a, b = jnp.abs(im), jnp.abs(re)
    big, small = jnp.maximum(a, b), jnp.minimum(a, b)
    t = small / jnp.maximum(big, 1e-37)
    p = t * poly(ATAN, t * t)
    p = jnp.where(a > b, 0.25 - p, p)
    p = jnp.where(re < 0.0, 0.5 - p, p)
    return jnp.where(im < 0.0, -p, p)


def edge(phase_p, gain_p, phase_q, gain_q):
    delta = phase_q - phase_p
    delta = delta - jnp.round(delta)
    half = gain_p * gain_q * poly(COS, delta * delta)
    weight = half * half
    return weight, weight * delta


def encode_gain(value):
    return jnp.exp2(value * CODE_SPAN - 0.5 * CODE_SPAN).astype(jnp.bfloat16)


def decode_gain(code):
    return (jnp.log2(code.astype(jnp.float32)) + 0.5 * CODE_SPAN) * (1.0 / CODE_SPAN)


def encode_power(value, scale):
    share = jnp.minimum(jnp.abs(value) / jnp.maximum(scale, TINY), 1.0) * POWER_BASE
    for _ in range(4):
        share = share * share
    return jnp.where(value < 0.0, -share, share)


def decode_power(code, scale):
    share = jnp.exp2(jnp.log2(jnp.abs(code)) * (1.0 / 16.0)) * (scale * (1.0 / POWER_BASE))
    return jnp.where(code < 0.0, -share, share)


def split(value):
    high = value.astype(jnp.bfloat16)
    return high, (value - high.astype(jnp.float32)).astype(jnp.bfloat16)


def dot3(a, b):
    f = functools.partial(jnp.dot, preferred_element_type=jnp.float32)
    return f(a[0], b[1]) + f(a[1], b[0]) + f(a[0], b[0])


def lanes_of(shape):
    return lax.broadcasted_iota(jnp.int32, shape, 1)


def call(body, outs, args, scratch, name, smem_first=True, flops=1000000, out_space=pltpu.VMEM):
    specs = [pl.BlockSpec(memory_space=pltpu.VMEM)] * len(args)
    if smem_first:
        specs[0] = pl.BlockSpec(memory_space=pltpu.SMEM)
    return pl.pallas_call(
        body,
        out_shape=[jax.ShapeDtypeStruct(s, d) for s, d in outs],
        in_specs=specs,
        out_specs=[pl.BlockSpec(memory_space=out_space)] * len(outs),
        scratch_shapes=scratch,
        compiler_params=pltpu.CompilerParams(vmem_limit_bytes=VMEM_LIMIT),
        cost_estimate=pl.CostEstimate(flops=flops, bytes_accessed=4000000, transcendentals=0),
        name=name,
    )(*args)


def interior(body, outs, args, scratch):
    return pl.pallas_call(
        body,
        out_shape=[jax.ShapeDtypeStruct(s, d) for s, d in outs],
        in_specs=[pl.BlockSpec(memory_space=pltpu.SMEM)] + [pl.BlockSpec(memory_space=pltpu.HBM)] * 2
        + [pl.BlockSpec(memory_space=pltpu.VMEM)],
        out_specs=[pl.BlockSpec(memory_space=pltpu.VMEM)] * len(outs),
        scratch_shapes=scratch,
        compiler_params=pltpu.CompilerParams(vmem_limit_bytes=VMEM_LIMIT),
        cost_estimate=pl.CostEstimate(flops=8000000, bytes_accessed=4000000, transcendentals=0),
        name="interior",
    )(*args)


def phase_gain(smoothed):
    re, im, one, two = smoothed
    gain = jnp.sqrt(re * re + im * im) / (jnp.sqrt(one * two) + EPS)
    return angle_turns(im, re), jnp.sqrt(gain)


def products(ar, ai, br, bi, scale=None):
    ar, ai, br, bi = (v.astype(jnp.float32) for v in (ar, ai, br, bi))
    if scale is not None:
        ar, ai, br, bi = (v * scale for v in (ar, ai, br, bi))
    return (ar * br + ai * bi, ai * br - ar * bi, ar * ar + ai * ai, br * br + bi * bi)


def along_range(x):
    k = taps()
    n = x.shape[1]
    total = k[0] * x
    for j in range(1, RADIUS + 1):
        total = total + k[j] * (pltpu.roll(x, j, 1) + pltpu.roll(x, n - j, 1))
    return total


def along_azimuth(ref, f, row, rows, cs):
    k = taps()
    total = k[0] * ref[f, row : row + rows, cs]
    for j in range(1, RADIUS + 1):
        total = total + k[j] * (ref[f, row - j : row - j + rows, cs] + ref[f, row + j : row + j + rows, cs])
    return total


def end_weights(before):
    k = taps()
    sub = lax.broadcasted_iota(jnp.int32, (HALO, 1), 0)
    low = jnp.zeros((HALO, 1), jnp.float32)
    high = jnp.zeros((HALO, 1), jnp.float32)
    for j in range(RADIUS + 1):
        low = jnp.where(sub == (HALO - 1 - j if before else HALO - j), k[j], low)
        high = jnp.where(sub == (j - 1 if before else j), k[j], high)
    return low, high


def first_of_half(own, half, across):
    return (own & half) ^ (half if across else 0)


def window(lines, width, tile, columns, across, own, rows):
    half = columns // 2
    span = half * tile + 2 * LANES
    first_tile = first_of_half(own, half, across)
    start = pl.multiple_of(first_tile * tile, LANES)
    pixel = lanes_of((rows, span)) + (start - LANES)
    return first_tile, start, span, jnp.logical_and(pixel >= 0, pixel < width)


def range_table(tile_pair, out):
    k = taps()
    margin = (tile_pair - out) // 2
    table = np.zeros((tile_pair, out))
    for n in range(out):
        for j in range(-RADIUS, RADIUS + 1):
            table[n + margin + j, n] = k[abs(j)]
    return table


def interior_kernel(
    lines, width, tile, columns, across, ids, first, second, table, ranged, field, codes, rims, raw, high, low, sems
):
    half = columns // 2
    chunk = 16
    first_tile, start, span, _ = window(lines, width, tile, columns, across, ids[1], 8)
    upper = jnp.where(first_tile == 0, 0, 1)
    source = pl.multiple_of(upper * (width // 2 - 2 * LANES), LANES)
    target = pl.multiple_of((1 - upper) * 2 * LANES, LANES)
    size = width // 2 + 2 * LANES
    blank = pl.multiple_of(upper * size, LANES)
    copies = []
    for i in range(lines // chunk):
        rs = pl.ds(i * chunk, chunk)
        for a, ref in enumerate((first, second)):
            copy = pltpu.make_async_copy(
                ref.at[:, rs, pl.ds(source, size)], raw.at[a, :, rs, pl.ds(target, size)], sems.at[2 * i + a]
            )
            copy.start()
            copies.append(copy)
    for a in range(2):
        for part in range(2):
            raw[a, part, :, pl.ds(blank, 2 * LANES)] = jnp.zeros((lines, 2 * LANES), jnp.bfloat16)
    for i in range(lines // chunk):
        copies[2 * i].wait()
        copies[2 * i + 1].wait()
        rs = slice(i * chunk, (i + 1) * chunk)
        for c in range(0, span + 2 * LANES, 2 * LANES):
            cs = slice(c, c + 2 * LANES)
            values = products(raw[0, 0, rs, cs], raw[0, 1, rs, cs], raw[1, 0, rs, cs], raw[1, 1, rs, cs])
            for f in range(4):
                row = f * lines + i * chunk
                high[row : row + chunk, cs], low[row : row + chunk, cs] = split(values[f])
    block = 2 * LANES
    weights = table[0 : 2 * block, :], table[2 * block :, :]
    for c in range(0, span, block):
        cs = slice(c, c + 2 * block)
        total = dot3((high[:, cs], low[:, cs]), weights)
        if c == 0 or c + block == span:
            pixel = lanes_of(total.shape) + (start - LANES + c)
            total = jnp.where(jnp.logical_and(pixel >= 0, pixel < width), total, 0.0)
        for f in range(4):
            ranged[f, :, c : c + block] = total[f * lines : (f + 1) * lines, :]
    for c in range(0, span, LANES):
        cs = slice(c, c + LANES)
        steps = [(HALO, HALO)] + [(r, 16) for r in range(EDGE, lines - EDGE, 16)] + [(lines - EDGE, HALO)]
        for r, rows in steps:
            smoothed = [along_azimuth(ranged, f, r, rows, cs) for f in range(4)]
            phase, gain = phase_gain(smoothed)
            field[0, r - HALO : r - HALO + rows, cs] = phase
            field[1, r - HALO : r - HALO + rows, cs] = gain
            if rows == 16:
                at = slice(r - EDGE, r - EDGE + rows)
                codes[0, at, cs], codes[1, at, cs] = split(phase)
                codes[2, at, cs] = encode_gain(gain)
    groups = lines // 8
    for t in range(half):
        rims[t] = rim_block(field, groups, range(1, groups - 1), 1, t * tile, tile, None)


def rim_block(field, groups, which, first_group, start, tile, block, hint=None):
    lane = lanes_of((8, LANES))
    if block is None:
        block = jnp.zeros((8, LANES), jnp.float32)
    for f in range(2):
        for side in range(2):
            offset = start if side == 0 else start + LANES + tile
            at = slice(offset, offset + LANES) if hint is None else pl.ds(hint(offset, LANES), LANES)
            for g in which:
                target = (f * 2 + side) * groups + g
                row = 8 * (g - first_group)
                x = field[f, row : row + 8, at]
                shift = (target - (LANES - 1 if side == 0 else 0)) % LANES
                if shift:
                    x = pltpu.roll(x, shift, 1)
                block = jnp.where(lane == target, x, block)
    return block


def border_kernel(lines, width, tile, columns, across, ids, ranged, inside_field, codes, rims, from_pair, from_next, *rest):
    half = columns // 2
    outs, (prod, seg, field, ends) = rest[:half], rest[half:]
    own = ids[1]
    odd = ids[4]
    first_tile, start, span, in_image = window(lines, width, tile, columns, across, own, HALO)
    inside = (
        jnp.where(ids[2] == 0, 0.0, 1.0).astype(jnp.float32),
        jnp.where(ids[2] == ids[3] - 1, 0.0, 1.0).astype(jnp.float32),
    )
    zero = jnp.zeros((HALO, 2 * LANES), jnp.float32)
    own_rows = 2 * HALO
    for e in range(2):
        flag = odd if e == 0 else 1 - odd
        keep = flag.astype(jnp.float32)
        for f in range(4):
            prod[f, :, 0 : 2 * LANES] = zero
            prod[f, :, 2 * LANES + width :] = zero
        for c in range(0, width, 512):
            cs = slice(c, c + 512)
            parts = [
                from_pair[i, :, cs].astype(jnp.float32) * keep + from_next[i, :, cs].astype(jnp.float32) * (1.0 - keep)
                for i in range(4)
            ]
            values = products(*parts, inside[e])
            for f in range(4):
                prod[f, :, 2 * LANES + c : 2 * LANES + c + 512] = values[f]
        for f in range(4):
            total = along_range(prod[f, :, pl.ds(start, span + 2 * LANES)])[:, LANES : LANES + span]
            total = jnp.where(in_image, total, 0.0)
            if e == 0:
                seg[e, f, 0:HALO, :] = total
                seg[e, f, HALO:, :] = ranged[f, 0:own_rows, :]
            else:
                seg[e, f, own_rows:, :] = total
                seg[e, f, 0:own_rows, :] = ranged[f, lines - own_rows :, :]
    border = []
    for e in range(2):
        ref = seg.at[e]
        for c in range(0, span, LANES):
            cs = slice(c, c + LANES)
            smoothed = [along_azimuth(ref, f, HALO, HALO, cs) for f in range(4)]
            phase, gain = phase_gain(smoothed)
            field[0, e * HALO : (e + 1) * HALO, cs] = phase
            field[1, e * HALO : (e + 1) * HALO, cs] = gain
        low, high = end_weights(e == 0)
        r = 0 if e == 0 else own_rows - HALO
        border.append(
            [
                jnp.sum(low * ref[f, r : r + HALO, :] + high * ref[f, r + HALO : r + 2 * HALO, :], axis=0, keepdims=True)
                for f in range(4)
            ]
        )
    phase, gain = phase_gain([jnp.concatenate(pair, axis=0) for pair in zip(*border)])
    ends[0:2, :] = phase
    ends[2:4, :] = gain
    for e in range(2):
        ends[2 + e : 3 + e, :] = ends[2 + e : 3 + e, :] * inside[e]
    groups = lines // 8
    inner = lines - 2 * EDGE
    for n, s in enumerate(range(half, columns) if across else range(half)):
        out = outs[n]
        target = own ^ s
        local = pl.multiple_of((target - first_tile) * tile, LANES)
        cs = pl.ds(pl.multiple_of(local + LANES, LANES), tile)
        for i in range(3):
            out[i * lines + EDGE : i * lines + EDGE + inner, :] = codes[i, :, cs]
        for e in range(2):
            row = 0 if e == 0 else lines - EDGE
            rs = slice(e * HALO, (e + 1) * HALO)
            inner_rows = slice(0, HALO) if e == 0 else slice(lines - 3 * HALO, lines - 2 * HALO)
            pairs = [(field[i, rs, cs], inside_field[i, inner_rows, cs]) for i in range(2)]
            phase, gain = (jnp.concatenate(p if e == 0 else p[::-1], axis=0) for p in pairs)
            out[row : row + EDGE, :], out[lines + row : lines + row + EDGE, :] = split(phase)
            out[2 * lines + row : 2 * lines + row + EDGE, :] = encode_gain(gain)
        block = rims[target - first_tile]
        block = rim_block(field, groups, (0,), 0, local, tile, block, pl.multiple_of)
        block = rim_block(field, groups, (groups - 1,), groups - 2, local, tile, block, pl.multiple_of)
        rows = []
        for i in range(4):
            for h in range(tile // LANES):
                rows.append(ends[i : i + 1, pl.ds(pl.multiple_of(local + (h + 1) * LANES, LANES), LANES)])
        block = jnp.concatenate([block, jnp.concatenate(rows, axis=0)], axis=1)
        out[3 * lines :, :] = jnp.concatenate(split(block), axis=0)


def strip_kernel(lines, width, tile, columns, exchange, ids, first, second, above, below, *rest):
    n_out = len(rest) - 3
    outs, (prod, ranged, field) = rest[:n_out], rest[n_out:]
    k = taps()
    own = ids[1]
    inside_above = jnp.where(ids[2] == 0, 0.0, 1.0).astype(jnp.float32)
    inside_below = jnp.where(ids[2] == ids[3] - 1, 0.0, 1.0).astype(jnp.float32)
    height = lines + 2 * HALO

    zero = jnp.zeros((height, LANES), jnp.float32)
    for f in range(4):
        prod[f, :, 0:LANES] = zero
        prod[f, :, LANES + width :] = zero
    step = min(width, 512)
    for c in range(0, width, step):
        at = slice(LANES + c, LANES + c + step)
        cs = slice(c, c + step)
        rows = min(lines, 16)
        for r in range(0, lines, rows):
            rs = slice(r, r + rows)
            values = products(first[0, rs, cs], first[1, rs, cs], second[0, rs, cs], second[1, rs, cs])
            for f in range(4):
                prod[f, HALO + r : HALO + r + rows, at] = values[f]
        for ref, r, scale in ((above, 0, inside_above), (below, HALO + lines, inside_below)):
            values = products(ref[0, :, cs], ref[1, :, cs], ref[2, :, cs], ref[3, :, cs], scale)
            for f in range(4):
                prod[f, r : r + HALO, at] = values[f]

    step = min(width, 1024)
    for f in range(4):
        for r in range(0, height, 8):
            for c in range(0, width, step):
                x = prod[f, r : r + 8, c : c + step + 2 * LANES]
                n = step + 2 * LANES
                total = k[0] * x
                for j in range(1, RADIUS + 1):
                    total = total + k[j] * (pltpu.roll(x, j, 1) + pltpu.roll(x, n - j, 1))
                ranged[f, r : r + 8, c : c + step] = total[:, LANES : LANES + step]

    for f in range(2):
        field[f, :, 0:LANES] = zero[:lines]
        field[f, :, LANES + width :] = zero[:lines]
    rows = min(lines, 32)
    sub = lax.broadcasted_iota(jnp.int32, (HALO, 1), 0)
    low = jnp.zeros((HALO, 1), jnp.float32)
    high = jnp.zeros((HALO, 1), jnp.float32)
    for j in range(RADIUS + 1):
        low = jnp.where(sub == HALO - 1 - j, k[j], low)
        high = jnp.where(sub == j - 1, k[j], high)
    top, bottom = [], []
    for c in range(0, width, LANES):
        cs = slice(c, c + LANES)
        for r in range(0, lines, rows):
            smoothed = []
            for f in range(4):
                b = HALO + r
                total = k[0] * ranged[f, b : b + rows, cs]
                for j in range(1, RADIUS + 1):
                    total = total + k[j] * (
                        ranged[f, b - j : b - j + rows, cs] + ranged[f, b + j : b + j + rows, cs]
                    )
                smoothed.append(total)
            phase, gain = phase_gain(smoothed)
            field[0, r : r + rows, LANES + c : 2 * LANES + c] = phase
            field[1, r : r + rows, LANES + c : 2 * LANES + c] = gain

    step = min(width, 1024)
    low = low + jnp.zeros((HALO, step), jnp.float32)
    high = high + jnp.zeros((HALO, step), jnp.float32)
    mirror_low = jnp.zeros((HALO, 1), jnp.float32)
    mirror_high = jnp.zeros((HALO, 1), jnp.float32)
    for j in range(RADIUS + 1):
        mirror_high = jnp.where(sub == j, k[j], mirror_high)
        mirror_low = jnp.where(sub == HALO - j, k[j], mirror_low)
    ends = []
    for c in range(0, width, step):
        cs = slice(c, c + step)
        up = [
            jnp.sum(low * ranged[f, 0:HALO, cs] + high * ranged[f, HALO : 2 * HALO, cs], axis=0, keepdims=True)
            for f in range(4)
        ]
        down = [
            jnp.sum(
                mirror_low * ranged[f, lines : lines + HALO, cs]
                + mirror_high * ranged[f, lines + HALO : lines + 2 * HALO, cs],
                axis=0,
                keepdims=True,
            )
            for f in range(4)
        ]
        up_phase, up_gain = phase_gain(up)
        down_phase, down_gain = phase_gain(down)
        ends.append((up_phase, down_phase, up_gain * inside_above, down_gain * inside_below))
    for i, (a, b, c_, d) in enumerate(ends):
        at = slice(i * step, (i + 1) * step)
        prod[0, 0:1, at] = a
        prod[0, 1:2, at] = b
        prod[0, 2:3, at] = c_
        prod[0, 3:4, at] = d

    groups = lines // 8
    lane = lanes_of((8, LANES))

    def pack(out, start, aligned):
        hint = pl.multiple_of if aligned else (lambda v, _: v)
        out[0:lines, :] = field[0, :, pl.ds(hint(start + LANES, LANES), tile)]
        out[lines : 2 * lines, :] = field[1, :, pl.ds(hint(start + LANES, LANES), tile)]
        block = jnp.zeros((8, LANES), jnp.float32)
        for f in range(2):
            for side in range(2):
                offset = start if side == 0 else start + LANES + tile
                for g in range(groups):
                    target = (f * 2 + side) * groups + g
                    x = field[f, 8 * g : 8 * g + 8, pl.ds(hint(offset, LANES), LANES)]
                    shift = (target - (LANES - 1 if side == 0 else 0)) % LANES
                    if shift:
                        x = pltpu.roll(x, shift, 1)
                    block = jnp.where(lane == target, x, block)
        base = 2 * lines
        out[base : base + 8, 0:LANES] = block
        for i in range(4):
            for h in range(tile // LANES):
                out[base + 2 * i + h : base + 2 * i + h + 1, LANES : 2 * LANES] = prod[
                    0, i : i + 1, pl.ds(hint(start + h * LANES, LANES), LANES)
                ]

    if exchange == "permute":
        for s in range(columns):
            pack(outs[s], (own ^ s) * tile, True)
    else:
        for s in range(columns):
            pack(outs[0].at[s], s * tile, False)


def precondition(field, tables, inverse):
    az, az_t, rg, rg_t = tables
    coef = dot3(az, split(field))
    coef = dot3(split(coef), rg_t)
    coef = coef * inverse[...]
    back = dot3(az_t, split(coef))
    return dot3(split(back), rg)


def table_pairs(tables):
    pairs = []
    for ref in tables:
        n = ref.shape[1]
        parts = [ref[i * n : (i + 1) * n, :] for i in range(4)]
        pairs += [(parts[0], parts[1]), (parts[2], parts[3])]
    return pairs


def line_groups(ref, tile_az, edge_lane):
    lane = lanes_of((8, LANES))
    first = (edge_lane // LANES) * LANES
    block = jnp.zeros((8, LANES), jnp.float32)
    for g in range(tile_az // 8):
        x = ref[8 * g : 8 * g + 8, first : first + LANES]
        shift = (g - edge_lane) % LANES
        if shift:
            x = pltpu.roll(x, shift, 1)
        block = jnp.where(lane == g, x, block)
    return block


def spread_groups(block, first_group, count, target_lane, base=0):
    parts = []
    for g in range(first_group, first_group + count):
        shift = (target_lane - (base + g)) % LANES
        parts.append(pltpu.roll(block, shift, 1) if shift else block)
    return jnp.concatenate(parts, axis=0) if count > 1 else parts[0]


def shifted_right(x, left):
    lane = lanes_of(x.shape)
    if left is None:
        return jnp.where(lane == 0, 0.0, pltpu.roll(x, 1, 1))
    wide = jnp.concatenate([left] * (x.shape[1] // LANES), axis=1)
    return jnp.where(lane == 0, wide, pltpu.roll(x, 1, 1))


def shifted_left(x, right):
    lane = lanes_of(x.shape)
    wide = jnp.concatenate([right] * (x.shape[1] // LANES), axis=1)
    return jnp.where(lane == x.shape[1] - 1, wide, pltpu.roll(x, x.shape[1] - 1, 1))


def divergence(tile_az, step, along_x, rim_x, along_y, r):
    rs = slice(r, r + step)
    x = along_x[rs, :]
    return (x - shifted_left(x, rim_x[rs, :])) + along_y[rs, :] - along_y[r + 1 : r + 1 + step, :]


def edges_of(lines, count, tile, coded, sources, scratch, outs):
    phase, gain, sides, ends = scratch
    weight_x, flux_x, rim_x, flux_rim, weight_y, flux_y, weight_end, flux_end = outs
    height = count * lines
    for src, strip in sources:
        if coded:
            row, at = pl.multiple_of(strip * lines, 8), pl.ds(pl.multiple_of(strip * 8, 8), 8)
            phase[pl.ds(HALO + row, lines), :] = src[0:lines, :].astype(jnp.float32) + src[
                lines : 2 * lines, :
            ].astype(jnp.float32)
            gain[pl.ds(HALO + row, lines), :] = decode_gain(src[2 * lines : 3 * lines, :])
            both = src[3 * lines :, :].astype(jnp.float32)
            block = both[0:8, :] + both[8:16, :]
        else:
            row, at = strip * lines, pl.ds(strip * 8, 8)
            phase[pl.ds(HALO + row, lines), :] = src[0:lines, :]
            gain[pl.ds(HALO + row, lines), :] = src[lines : 2 * lines, :]
            block = src[2 * lines : 2 * lines + 8, :]
        sides[at, :] = block[:, 0:LANES]
        ends[at, :] = block[:, LANES : 2 * LANES]
    last = 8 * (count - 1)
    for h in range(tile // LANES):
        cs = slice(h * LANES, (h + 1) * LANES)
        phase[HALO - 1 : HALO, cs] = ends[h : h + 1, :]
        gain[HALO - 1 : HALO, cs] = ends[4 + h : 5 + h, :]
        phase[HALO + height : HALO + height + 1, cs] = ends[last + 2 + h : last + 3 + h, :]
        gain[HALO + height : HALO + height + 1, cs] = ends[last + 6 + h : last + 7 + h, :]

    step = min(height, 32)
    groups = lines // 8
    for r in range(0, height, step):
        rs = slice(r, r + step)
        b = HALO + r
        p, g = phase[b : b + step, :], gain[b : b + step, :]
        halo = []
        for f in range(2):
            for side in range(2):
                parts = []
                for line_group in range(r // 8, (r + step) // 8):
                    strip, inner = divmod(line_group, groups)
                    block = sides[8 * strip : 8 * strip + 8, :]
                    source_lane = (f * 2 + side) * groups + inner
                    shift = ((0 if side == 0 else LANES - 1) - source_lane) % LANES
                    parts.append(pltpu.roll(block, shift, 1) if shift else block)
                halo.append(jnp.concatenate(parts, axis=0) if len(parts) > 1 else parts[0])
        weight_x[rs, :], flux_x[rs, :] = edge(shifted_right(p, halo[0]), shifted_right(g, halo[2]), p, g)
        rim_x[rs, :], flux_rim[rs, :] = edge(p[:, tile - LANES :], g[:, tile - LANES :], halo[1], halo[3])
        weight_y[rs, :], flux_y[rs, :] = edge(phase[b - 1 : b - 1 + step, :], gain[b - 1 : b - 1 + step, :], p, g)
    b = HALO + height
    w, f = edge(phase[b - 1 : b, :], gain[b - 1 : b, :], phase[b : b + 1, :], gain[b : b + 1, :])
    weight_end[...] = jnp.broadcast_to(w, (8, tile))
    flux_end[...] = jnp.broadcast_to(f, (8, tile))


def far_kernel(lines, tile, columns, ids, *rest):
    half = columns // 2
    own = ids[1]
    sources = [(rest[n], (own ^ n) & (half - 1)) for n in range(half)]
    edges_of(lines, half, tile, True, sources, rest[half + 8 :], rest[half : half + 8])


def tile_kernel(lines, tile_az, tile, columns, exchange, ids, *rest):
    coded = exchange == "permute"
    half = columns // 2
    own = ids[1]
    count = half if coded else columns
    if coded:
        sources = [(rest[half - 1 - s], (own ^ s) & (half - 1)) for s in range(half)]
        far, rest = rest[half : half + 8], rest[half + 8 :]
    else:
        sources = [(rest[0].at[s], s) for s in range(columns)]
        rest = rest[1:]
    tables, inverse = rest[:2], rest[2]
    residual, shaped, weight_x, rim_x, weight_y, row_pair, row_next, col_pair, col_next = rest[3:12]
    phase, gain, sides, ends, flux_x, flux_rim, flux_y, weight_end, flux_end = rest[12:]
    pairs = table_pairs(tables)
    height = count * lines
    whole = (weight_x, flux_x, rim_x, flux_rim, weight_y, flux_y)
    if coded:
        lower = (own & half) // half
        at = pl.ds(pl.multiple_of(lower * height, 8), height)
        outs = [ref.at[at, :] for ref in whole]
    else:
        outs = [ref.at[pl.ds(0, height), :] for ref in whole]
    edges_of(
        lines, count, tile, coded, sources, (phase, gain, sides, ends), (*outs, weight_end, flux_end)
    )
    w, f = weight_end[...], flux_end[...]
    if coded:
        at = pl.ds(pl.multiple_of((1 - lower) * height, 8), height)
        for source, ref in zip(far, whole):
            ref[at, :] = source[...]
        w, f = jnp.where(lower == 1, w, far[6][...]), jnp.where(lower == 1, f, far[7][...])
    weight_y[tile_az : tile_az + 8, :] = w
    flux_y[tile_az : tile_az + 8, :] = f

    step = min(tile_az, 32)
    for r in range(0, tile_az, step):
        residual[r : r + step, :] = TURN * divergence(tile_az, step, flux_x, flux_rim, flux_y, r)
    shaped[...] = precondition(residual[...], pairs, inverse)
    row_odd, col_odd = ids[5] == 1, ids[4] == 1
    top = jnp.concatenate([shaped[0:1, h : h + LANES] for h in range(0, tile, LANES)], axis=0)
    bottom = jnp.concatenate([shaped[tile_az - 1 : tile_az, h : h + LANES] for h in range(0, tile, LANES)], axis=0)
    row_pair[0:2, :] = jnp.where(row_odd, top, bottom)
    row_next[0:2, :] = jnp.where(row_odd, bottom, top)
    left = line_groups(shaped, tile_az, 0)
    right = line_groups(shaped, tile_az, tile - 1)
    col_pair[...] = jnp.where(col_odd, left, right)
    col_next[...] = jnp.where(col_odd, right, left)


def apply_operator(tile_az, tile, u, weight_x, rim_x, weight_y, flux_x, flux_rim, flux_y, left, right, out):
    step = min(tile_az, 32)
    for r in range(0, tile_az, step):
        rs = slice(r, r + step)
        b = HALO + r
        x = u[b : b + step, :]
        l = None if left is None else spread_groups(left, r // 8, step // 8, 0)
        flux_x[rs, :] = weight_x[rs, :] * (x - shifted_right(x, l))
        edge_x = x[:, tile - LANES :]
        if right is None:
            flux_rim[rs, :] = -rim_x[rs, :] * edge_x
        else:
            flux_rim[rs, :] = rim_x[rs, :] * (spread_groups(right, r // 8, step // 8, LANES - 1) - edge_x)
        flux_y[rs, :] = weight_y[rs, :] * (x - u[b - 1 : b - 1 + step, :])
    b = HALO + tile_az
    flux_y[tile_az : tile_az + 1, :] = weight_y[tile_az : tile_az + 1, :] * (u[b : b + 1, :] - u[b - 1 : b, :])
    for r in range(0, tile_az, step):
        out[r : r + step, :] = DAMPING * u[HALO + r : HALO + r + step, :] + divergence(
            tile_az, step, flux_x, flux_rim, flux_y, r
        )


def inner(a, b, tile_az, offset_a=0, offset_b=0):
    total = jnp.zeros((32, a.shape[1]), jnp.float32)
    for r in range(0, tile_az, 32):
        total = total + a[offset_a + r : offset_a + r + 32, :] * b[offset_b + r : offset_b + r + 32, :]
    return jnp.sum(jnp.sum(total, axis=0, keepdims=True), axis=1, keepdims=True)


def second_kernel(
    tile_az, tile, ids, residual, shaped, weight_x, rim_x, weight_y, col_next, col_pair, row_next, row_pair, *rest
):
    tables, inverse = rest[:2], rest[2]
    operated, shaped2, operated2, chunk, roots = rest[3:8]
    u, flux_x, flux_rim, flux_y = rest[8:]
    pairs = table_pairs(tables)
    row_odd, col_odd = ids[5] == 1, ids[4] == 1
    up = jnp.where(row_odd, row_pair[0:2, :], row_next[0:2, :])
    down = jnp.where(row_odd, row_next[0:2, :], row_pair[0:2, :])
    left = jnp.where(col_odd, col_pair[...], col_next[...])
    right = jnp.where(col_odd, col_next[...], col_pair[...])
    u[HALO : HALO + tile_az, :] = shaped[...]
    for h in range(tile // LANES):
        cs = slice(h * LANES, (h + 1) * LANES)
        u[HALO - 1 : HALO, cs] = up[h : h + 1, :]
        u[HALO + tile_az : HALO + tile_az + 1, cs] = down[h : h + 1, :]
    apply_operator(
        tile_az, tile, u, weight_x, rim_x, weight_y, flux_x, flux_rim, flux_y, left, right, operated
    )
    image = precondition(operated[...], pairs, inverse)
    shaped2[...] = image
    u[HALO : HALO + tile_az, :] = image
    apply_operator(
        tile_az, tile, u, weight_x, rim_x, weight_y, flux_x, flux_rim, flux_y, left, right, operated2
    )
    lane = lanes_of((1, LANES))
    sums = jnp.zeros((1, LANES), jnp.float32)
    for i, (a, b) in enumerate(
        (
            (residual, shaped),
            (shaped, operated),
            (residual, shaped2),
            (operated, shaped2),
            (shaped2, operated2),
        )
    ):
        sums = jnp.where(lane == i, inner(a, b, tile_az), sums)
    def rows_of(x):
        return jnp.concatenate([x[:, h : h + LANES] for h in range(0, tile, LANES)], axis=0)

    weight_t, weight_b = rows_of(weight_y[0:1, :]), rows_of(weight_y[tile_az : tile_az + 1, :])
    weight_l, weight_r = line_groups(weight_x, tile_az, 0), line_groups(rim_x, tile_az, LANES - 1)
    top = rows_of(image_row(shaped2, shaped, 0))
    bottom = rows_of(image_row(shaped2, shaped, tile_az - 1))
    left_rim = line_groups(shaped2, tile_az, 0) - line_groups(shaped, tile_az, 0)
    right_rim = line_groups(shaped2, tile_az, tile - 1) - line_groups(shaped, tile_az, tile - 1)
    known = jnp.sum(weight_t * up * top + weight_b * down * bottom, keepdims=True) + jnp.sum(
        weight_l * left * left_rim + weight_r * right * right_rim, keepdims=True
    )
    sums = jnp.where(lane == 4, sums - known, sums)
    half = tile_az // 8
    wide = lanes_of((8, LANES))
    root_sides = jnp.sqrt(jnp.where(wide < half, weight_l, pltpu.roll(weight_r, half, 1)))
    sides = root_sides * jnp.where(wide < half, left_rim, pltpu.roll(right_rim, half, 1))
    root_ends = jnp.sqrt(jnp.concatenate([weight_t, weight_b], axis=0))
    ends = root_ends * jnp.concatenate([top, bottom], axis=0)
    scale = jnp.maximum(jnp.max(jnp.abs(sides), keepdims=True), jnp.max(jnp.abs(ends), keepdims=True))
    scale = (scale * 1.01).astype(jnp.bfloat16).astype(jnp.float32)
    sums = jnp.where(lane == SCALE_LANE, scale, sums)
    high = sums.astype(jnp.bfloat16).astype(jnp.float32)
    middle = (sums - high).astype(jnp.bfloat16).astype(jnp.float32)
    rest_ = sums - high - middle
    sums = high + pltpu.roll(middle, 8, 1) + pltpu.roll(rest_, 16, 1)
    chunk[...] = jnp.concatenate(
        [encode_power(sides, scale), encode_power(ends, scale), jnp.broadcast_to(sums, (4, LANES))], axis=0
    ).astype(jnp.bfloat16)
    roots[...] = jnp.concatenate([root_sides, root_ends, root_ends], axis=0)


def image_row(a, b, row):
    return a[row : row + 1, :] - b[row : row + 1, :]


def last_kernel(
    tile_az, tile, rows, columns, ids, gathered, residual, shaped, operated, shaped2, operated2, roots,
    solution_hbm, residual_hbm, solution_out, residual_out, sems
):
    half = tile_az // 8
    lane = lanes_of((8, LANES))
    total = jnp.zeros((4, LANES), jnp.float32)
    cross_x = jnp.zeros((8, LANES), jnp.float32)
    cross_y = jnp.zeros((2, LANES), jnp.float32)
    values = {}

    def decoded(i):
        x = gathered[i].astype(jnp.float32)
        return jnp.concatenate([decode_power(x[0:12, :], x[12:13, SCALE_LANE : SCALE_LANE + 1]), x[12:16, :]], axis=0)

    def value_of(i):
        if i not in values:
            values[i] = decoded(i)
        return values[i]

    for r in range(rows):
        for c in range(columns):
            i = r * columns + c
            here = value_of(i)
            total = total + here[12:16, :]
            if c + 1 < columns:
                cross_x = cross_x + pltpu.roll(here[0:8, :], LANES - half, 1) * value_of(i + 1)[0:8, :]
            if r + 1 < rows:
                cross_y = cross_y + here[10:12, :] * value_of(i + columns)[8:10, :]
    cross = jnp.sum(jnp.where(lane < half, cross_x, 0.0), keepdims=True) + jnp.sum(cross_y, keepdims=True)
    wide = total[0:1, :]
    first_lane = lanes_of((1, LANES))
    pick = [
        jnp.sum(jnp.where(first_lane % 8 == i, jnp.where(first_lane < 24, wide, 0.0), 0.0), axis=1, keepdims=True)
        for i in range(5)
    ]
    dot0, curve0, mixed, cross_dot, curve2 = pick
    curve2 = curve2 - 2.0 * cross
    alpha = dot0 / curve0
    fresh = dot0 - alpha * (mixed + curve0) + alpha * alpha * cross_dot
    beta = fresh / dot0
    grown = 1.0 + beta
    curve1 = grown * grown * curve0 - 2.0 * alpha * grown * cross_dot + alpha * alpha * curve2
    step1 = fresh / curve1
    on_first = alpha + step1 * grown
    on_second = step1 * alpha

    row, col = ids[0], ids[1]
    here = row * columns + col

    def neighbour(ok, index):
        return jnp.where(ok, index, here), jnp.where(ok, 1.0, 0.0).astype(jnp.float32)

    up, up_ok = neighbour(row > 0, here - columns)
    down, down_ok = neighbour(row < rows - 1, here + columns)
    left, left_ok = neighbour(col > 0, here - 1)
    right, right_ok = neighbour(col < columns - 1, here + 1)
    near = [decoded(i) for i in (left, right, up, down)]
    from_left = pltpu.roll(near[0][0:8, :], LANES - half, 1) * left_ok
    from_right = pltpu.roll(near[1][0:8, :], half, 1) * right_ok
    top = jnp.concatenate([near[2][10 + h : 11 + h, :] for h in range(tile // LANES)], axis=1) * up_ok
    bottom = jnp.concatenate([near[3][8 + h : 9 + h, :] for h in range(tile // LANES)], axis=1) * down_ok
    top = top * jnp.concatenate([roots[8 + h : 9 + h, :] for h in range(tile // LANES)], axis=1)
    bottom = bottom * jnp.concatenate([roots[10 + h : 11 + h, :] for h in range(tile // LANES)], axis=1)
    from_left = from_left * roots[0:8, :]
    from_right = from_right * roots[0:8, :]
    step = min(tile_az, 64)
    copies = []
    for r in range(0, tile_az, step):
        rs = slice(r, r + step)
        solution_out[rs, :] = on_first * shaped[rs, :] - on_second * shaped2[rs, :]
        q = operated2[rs, :]
        wide = lanes_of((step, tile))
        l = jnp.concatenate([spread_groups(from_left, r // 8, step // 8, 0)] * (tile // LANES), axis=1)
        q = q - jnp.where(wide == 0, l, 0.0)
        l = jnp.concatenate([spread_groups(from_right, r // 8, step // 8, LANES - 1, half)] * (tile // LANES), axis=1)
        q = q - jnp.where(wide == tile - 1, l, 0.0)
        if r == 0 or r + step == tile_az:
            deep = lax.broadcasted_iota(jnp.int32, (step, tile), 0)
        if r == 0:
            q = q - jnp.where(deep == 0, jnp.broadcast_to(top, (step, tile)), 0.0)
        if r + step == tile_az:
            q = q - jnp.where(deep == step - 1, jnp.broadcast_to(bottom, (step, tile)), 0.0)
        residual_out[rs, :] = residual[rs, :] - on_first * operated[rs, :] + on_second * q
        for n, (src, dst) in enumerate(((solution_out, solution_hbm), (residual_out, residual_hbm))):
            copy = pltpu.make_async_copy(src.at[rs, :], dst.at[rs, :], sems.at[2 * (r // step) + n])
            copy.start()
            copies.append(copy)
    for copy in copies:
        copy.wait()


def swapped(value, axis, count, step):
    if step == 0:
        pairs = [(i, i ^ 1) for i in range(count)]
    else:
        pairs = [(i, (i + 1 if i % 2 else i - 1) % count) for i in range(count)]
    return lax.ppermute(value, axis, pairs)


def shards(rows, columns, first_slc, second_slc):
    lines, width = first_slc.shape[1:]
    tile = width // columns
    tile_az = lines * columns
    axes = ("row", "col")
    exchange = "permute" if lines >= 4 * EDGE and columns <= 8 else "all_to_all"
    row, col = lax.axis_index("row"), lax.axis_index("col")
    ids = jnp.stack([row, col, row * columns + col, jnp.int32(rows * columns), col % 2, row % 2]).astype(jnp.int32)
    f32, bf16 = jnp.float32, jnp.bfloat16

    head = jnp.concatenate([first_slc[:, :HALO], second_slc[:, :HALO]], 0)
    tail = jnp.concatenate([first_slc[:, -HALO:], second_slc[:, -HALO:]], 0)
    odd = col % 2 == 1
    from_pair = swapped(jnp.where(odd, head, tail), axes, rows * columns, 0)
    from_next = swapped(jnp.where(odd, tail, head), axes, rows * columns, 1)
    wide = width + 2 * LANES
    if exchange == "permute":
        half = columns // 2
        span = half * tile + 2 * LANES
        smoothing = jnp.asarray(np.concatenate(two_parts(range_table(4 * LANES, 2 * LANES)), axis=0))
        sent = [None] * columns
        sources = (first_slc, second_slc)
        for across in (True, False):
            ranged, inner, codes, rims = interior(
                functools.partial(interior_kernel, lines, width, tile, columns, across),
                [
                    ((4, lines, span), f32),
                    ((2, lines - 2 * HALO, span), f32),
                    ((3, lines - 2 * EDGE, span), bf16),
                    ((half, 8, LANES), f32),
                ],
                (ids, *sources, smoothing),
                [
                    pltpu.VMEM((2, 2, lines, span + 2 * LANES), bf16),
                    pltpu.VMEM((4 * lines, span + 2 * LANES), bf16),
                    pltpu.VMEM((4 * lines, span + 2 * LANES), bf16),
                    pltpu.SemaphoreType.DMA((lines // 8,)),
                ],
            )
            part = call(
                functools.partial(border_kernel, lines, width, tile, columns, across),
                [((3 * lines + 16, tile), bf16)] * half,
                (ids, ranged, inner, codes, rims, from_pair, from_next),
                [
                    pltpu.VMEM((4, HALO, width + 4 * LANES), f32),
                    pltpu.VMEM((2, 4, 3 * HALO, span), f32),
                    pltpu.VMEM((2, 2 * HALO, span), f32),
                    pltpu.VMEM((8, span), f32),
                ],
                "borders",
            )
            for i, value in enumerate(part):
                sent[i + (half if across else 0)] = value
            if across:
                *part, first_slc, second_slc = lax.optimization_barrier((*part, first_slc, second_slc))
                sources = (first_slc, second_slc)
                for i, value in enumerate(part):
                    sent[i + half] = value
        arrived = [sent[0]] + [
            lax.ppermute(sent[s], "col", [(i, i ^ s) for i in range(columns)]) for s in range(1, columns)
        ]
    else:
        above = jnp.where(odd, from_pair, from_next)
        below = jnp.where(odd, from_next, from_pair)
        height = lines + 2 * HALO
        sent = call(
            functools.partial(strip_kernel, lines, width, tile, columns, exchange),
            [((columns, 2 * lines + 8, tile), f32)],
            (ids, first_slc, second_slc, above, below),
            [pltpu.VMEM((4, height, wide), f32), pltpu.VMEM((4, height, width), f32), pltpu.VMEM((2, lines, wide), f32)],
            "strips",
        )
        arrived = [lax.all_to_all(sent[0], "col", 0, 0, tiled=True)]

    tables = []
    for table in (cosine_table(tile_az), cosine_table(tile)):
        parts = [*two_parts(table), *two_parts(table.T)]
        tables.append(jnp.asarray(np.concatenate(parts, axis=0)))
    inverse = jnp.asarray(inverse_eigen(tile_az, tile))

    whole = ((tile_az, tile), f32)
    block = ((8, LANES), f32)
    padded = pltpu.VMEM((tile_az + 2 * HALO, tile), f32)
    fluxes = [
        pltpu.VMEM((tile_az, tile), f32),
        pltpu.VMEM((tile_az, LANES), f32),
        pltpu.VMEM((tile_az + 8, tile), f32),
    ]
    edge_rows = tile_az
    if exchange == "permute":
        edge_rows = half * lines
        part = ((edge_rows, tile), f32)
        side = ((edge_rows, LANES), f32)
        last = ((8, tile), f32)
        far = call(
            functools.partial(far_kernel, lines, tile, columns),
            [part, part, side, side, part, part, last, last],
            (ids, *arrived[half:]),
            [
                pltpu.VMEM((edge_rows + 2 * HALO, tile), f32),
                pltpu.VMEM((edge_rows + 2 * HALO, tile), f32),
                pltpu.VMEM((8 * half, LANES), f32),
                pltpu.VMEM((8 * half, LANES), f32),
            ],
            "far",
        )
        arrived = [*arrived[:half][::-1], *far]
    gathered_lines = pltpu.VMEM((edge_rows + 2 * HALO, tile), f32)
    residual, shaped, weight_x, rim_x, weight_y, row_pair, row_next, col_pair, col_next = call(
        functools.partial(tile_kernel, lines, tile_az, tile, columns, exchange),
        [whole, whole, whole, ((tile_az, LANES), f32), ((tile_az + 8, tile), f32), block, block, block, block],
        (ids, *arrived, *tables, inverse),
        [
            gathered_lines,
            gathered_lines,
            pltpu.VMEM((8 * columns, LANES), f32),
            pltpu.VMEM((8 * columns, LANES), f32),
            *fluxes,
            pltpu.VMEM((8, tile), f32),
            pltpu.VMEM((8, tile), f32),
        ],
        "tiles",
    )
    col_next = swapped(col_next, "col", columns, 1)
    col_pair = swapped(col_pair, "col", columns, 0)
    row_next = swapped(row_next, "row", rows, 1)
    row_pair = swapped(row_pair, "row", rows, 0)
    rims = (col_next, col_pair, row_next, row_pair)
    operated, shaped2, operated2, chunk, roots = call(
        functools.partial(second_kernel, tile_az, tile),
        [whole, whole, whole, ((16, LANES), bf16), ((16, LANES), f32)],
        (ids, residual, shaped, weight_x, rim_x, weight_y, *rims, *tables, inverse),
        [padded, *fluxes],
        "operator",
    )
    spread = jnp.broadcast_to(chunk[None], (rows * columns, 16, LANES))
    gathered = lax.all_to_all(spread, axes, 0, 0, tiled=True)
    return tuple(
        call(
            functools.partial(last_kernel, tile_az, tile, rows, columns),
            [whole, whole],
            (ids, gathered, residual, shaped, operated, shaped2, operated2, roots),
            [
                pltpu.VMEM((tile_az, tile), f32),
                pltpu.VMEM((tile_az, tile), f32),
                pltpu.SemaphoreType.DMA((2 * (tile_az // min(tile_az, 64)),)),
            ],
            "finish",
            out_space=pltpu.HBM,
        )
    )


def solution(mesh):
    placed = P(None, ("row", "col"), None)
    return jax.shard_map(
        functools.partial(shards, mesh.shape["row"], mesh.shape["col"]),
        mesh=mesh,
        in_specs=(placed, placed),
        out_specs=(P("row", "col"), P("row", "col")),
        check_vma=False,
    )
```

```python
import functools
import math

import jax
import jax.numpy as jnp
import ml_dtypes
import numpy as np
from jax import lax
from jax.experimental import pallas as pl
from jax.experimental.pallas import tpu as pltpu
from jax.sharding import PartitionSpec as P

EPS = 1e-05
DAMPING = 0.0001
RADIUS = 4
LANES = 128
HALO = 8
EDGE = 16
TURN = 2.0 * math.pi
CODE_SPAN = 248.0
POWER_BASE = 2.0**7.5
TINY = 1e-30
SCALE_LANE = 5
VMEM_LIMIT = 40 * 1024 * 1024

ATAN = (
    0.1591549409219458,
    -0.05305126669892651,
    0.03181993346630217,
    -0.022611352052724496,
    0.016957432021882463,
    -0.011990188139443825,
    0.0068498925926071,
    -0.002591499099089036,
    0.00046210915702298266,
)
COS = (
    0.9999999997806517,
    -4.934802137228286,
    4.0587091643402005,
    -1.3352120566397616,
    0.23493755882899706,
    -0.024396716411350872,
)


def taps():
    offsets = np.arange(-RADIUS, RADIUS + 1).astype(np.float64)
    weights = np.exp(-offsets * offsets / 8.0)
    weights = weights / weights.sum()
    return [float(weights[RADIUS + j]) for j in range(RADIUS + 1)]


def cosine_table(count):
    j = np.arange(count)[:, None].astype(np.float64)
    i = np.arange(count)[None, :].astype(np.float64)
    table = np.cos(np.pi * j * (i + 0.5) / count) * np.sqrt(2.0 / count)
    table[0] = np.sqrt(1.0 / count)
    return table


def two_parts(table):
    table = table.astype(np.float32)
    high = table.astype(ml_dtypes.bfloat16)
    low = (table - high.astype(np.float32)).astype(ml_dtypes.bfloat16)
    return np.ascontiguousarray(high), np.ascontiguousarray(low)


def inverse_eigen(count_az, count_rg):
    along_az = 2.0 - 2.0 * np.cos(np.pi * np.arange(count_az) / count_az)
    along_rg = 2.0 - 2.0 * np.cos(np.pi * np.arange(count_rg) / count_rg)
    return (1.0 / (DAMPING + along_az[:, None] + along_rg[None, :])).astype(np.float32)


def poly(coefficients, y):
    value = jnp.full_like(y, coefficients[-1])
    for c in coefficients[-2::-1]:
        value = value * y + c
    return value


def angle_turns(im, re):
    a, b = jnp.abs(im), jnp.abs(re)
    big, small = jnp.maximum(a, b), jnp.minimum(a, b)
    t = small / jnp.maximum(big, 1e-37)
    p = t * poly(ATAN, t * t)
    p = jnp.where(a > b, 0.25 - p, p)
    p = jnp.where(re < 0.0, 0.5 - p, p)
    return jnp.where(im < 0.0, -p, p)


def edge(phase_p, gain_p, phase_q, gain_q):
    delta = phase_q - phase_p
    delta = delta - jnp.round(delta)
    half = gain_p * gain_q * poly(COS, delta * delta)
    weight = half * half
    return weight, weight * delta


def encode_gain(value):
    return jnp.exp2(value * CODE_SPAN - 0.5 * CODE_SPAN).astype(jnp.bfloat16)


def decode_gain(code):
    return (jnp.log2(code.astype(jnp.float32)) + 0.5 * CODE_SPAN) * (1.0 / CODE_SPAN)


def encode_power(value, scale):
    share = jnp.minimum(jnp.abs(value) / jnp.maximum(scale, TINY), 1.0) * POWER_BASE
    for _ in range(4):
        share = share * share
    return jnp.where(value < 0.0, -share, share)


def decode_power(code, scale):
    share = jnp.exp2(jnp.log2(jnp.abs(code)) * (1.0 / 16.0)) * (scale * (1.0 / POWER_BASE))
    return jnp.where(code < 0.0, -share, share)


def split(value):
    high = value.astype(jnp.bfloat16)
    return high, (value - high.astype(jnp.float32)).astype(jnp.bfloat16)


def dot3(a, b):
    f = functools.partial(jnp.dot, preferred_element_type=jnp.float32)
    return f(a[0], b[1]) + f(a[1], b[0]) + f(a[0], b[0])


def lanes_of(shape):
    return lax.broadcasted_iota(jnp.int32, shape, 1)


def call(body, outs, args, scratch, name, smem_first=True, flops=1000000, out_space=pltpu.VMEM):
    specs = [pl.BlockSpec(memory_space=pltpu.VMEM)] * len(args)
    if smem_first:
        specs[0] = pl.BlockSpec(memory_space=pltpu.SMEM)
    return pl.pallas_call(
        body,
        out_shape=[jax.ShapeDtypeStruct(s, d) for s, d in outs],
        in_specs=specs,
        out_specs=[pl.BlockSpec(memory_space=out_space)] * len(outs),
        scratch_shapes=scratch,
        compiler_params=pltpu.CompilerParams(vmem_limit_bytes=VMEM_LIMIT),
        cost_estimate=pl.CostEstimate(flops=flops, bytes_accessed=4000000, transcendentals=0),
        name=name,
    )(*args)


def interior(body, outs, args, scratch):
    return pl.pallas_call(
        body,
        out_shape=[jax.ShapeDtypeStruct(s, d) for s, d in outs],
        in_specs=[pl.BlockSpec(memory_space=pltpu.SMEM)] + [pl.BlockSpec(memory_space=pltpu.HBM)] * 2
        + [pl.BlockSpec(memory_space=pltpu.VMEM)],
        out_specs=[pl.BlockSpec(memory_space=pltpu.VMEM)] * len(outs),
        scratch_shapes=scratch,
        compiler_params=pltpu.CompilerParams(vmem_limit_bytes=VMEM_LIMIT),
        cost_estimate=pl.CostEstimate(flops=8000000, bytes_accessed=4000000, transcendentals=0),
        name="interior",
    )(*args)


def phase_gain(smoothed):
    re, im, one, two = smoothed
    gain = jnp.sqrt(re * re + im * im) / (jnp.sqrt(one * two) + EPS)
    return angle_turns(im, re), jnp.sqrt(gain)


def products(ar, ai, br, bi, scale=None):
    ar, ai, br, bi = (v.astype(jnp.float32) for v in (ar, ai, br, bi))
    if scale is not None:
        ar, ai, br, bi = (v * scale for v in (ar, ai, br, bi))
    return (ar * br + ai * bi, ai * br - ar * bi, ar * ar + ai * ai, br * br + bi * bi)


def along_range(x):
    k = taps()
    n = x.shape[1]
    total = k[0] * x
    for j in range(1, RADIUS + 1):
        total = total + k[j] * (pltpu.roll(x, j, 1) + pltpu.roll(x, n - j, 1))
    return total


def along_azimuth(ref, f, row, rows, cs):
    k = taps()
    total = k[0] * ref[f, row : row + rows, cs]
    for j in range(1, RADIUS + 1):
        total = total + k[j] * (ref[f, row - j : row - j + rows, cs] + ref[f, row + j : row + j + rows, cs])
    return total


def end_weights(before):
    k = taps()
    sub = lax.broadcasted_iota(jnp.int32, (HALO, 1), 0)
    low = jnp.zeros((HALO, 1), jnp.float32)
    high = jnp.zeros((HALO, 1), jnp.float32)
    for j in range(RADIUS + 1):
        low = jnp.where(sub == (HALO - 1 - j if before else HALO - j), k[j], low)
        high = jnp.where(sub == (j - 1 if before else j), k[j], high)
    return low, high


def first_of_half(own, half, across):
    return (own & half) ^ (half if across else 0)


def window(lines, width, tile, columns, across, own, rows):
    half = columns // 2
    span = half * tile + 2 * LANES
    first_tile = first_of_half(own, half, across)
    start = pl.multiple_of(first_tile * tile, LANES)
    pixel = lanes_of((rows, span)) + (start - LANES)
    return first_tile, start, span, jnp.logical_and(pixel >= 0, pixel < width)


def range_table(tile_pair, out):
    k = taps()
    margin = (tile_pair - out) // 2
    table = np.zeros((tile_pair, out))
    for n in range(out):
        for j in range(-RADIUS, RADIUS + 1):
            table[n + margin + j, n] = k[abs(j)]
    return table


def interior_kernel(
    lines, width, tile, columns, across, ids, first, second, table, ranged, field, codes, rims, raw, high, low, sems
):
    half = columns // 2
    chunk = 16
    first_tile, start, span, _ = window(lines, width, tile, columns, across, ids[1], 8)
    upper = jnp.where(first_tile == 0, 0, 1)
    source = pl.multiple_of(upper * (width // 2 - 2 * LANES), LANES)
    target = pl.multiple_of((1 - upper) * 2 * LANES, LANES)
    size = width // 2 + 2 * LANES
    blank = pl.multiple_of(upper * size, LANES)
    copies = []
    for i in range(lines // chunk):
        rs = pl.ds(i * chunk, chunk)
        for a, ref in enumerate((first, second)):
            copy = pltpu.make_async_copy(
                ref.at[:, rs, pl.ds(source, size)], raw.at[a, :, rs, pl.ds(target, size)], sems.at[2 * i + a]
            )
            copy.start()
            copies.append(copy)
    for a in range(2):
        for part in range(2):
            raw[a, part, :, pl.ds(blank, 2 * LANES)] = jnp.zeros((lines, 2 * LANES), jnp.bfloat16)
    for i in range(lines // chunk):
        copies[2 * i].wait()
        copies[2 * i + 1].wait()
        rs = slice(i * chunk, (i + 1) * chunk)
        for c in range(0, span + 2 * LANES, 2 * LANES):
            cs = slice(c, c + 2 * LANES)
            values = products(raw[0, 0, rs, cs], raw[0, 1, rs, cs], raw[1, 0, rs, cs], raw[1, 1, rs, cs])
            for f in range(4):
                row = f * lines + i * chunk
                high[row : row + chunk, cs], low[row : row + chunk, cs] = split(values[f])
    block = 2 * LANES
    weights = table[0 : 2 * block, :], table[2 * block :, :]
    for c in range(0, span, block):
        cs = slice(c, c + 2 * block)
        total = dot3((high[:, cs], low[:, cs]), weights)
        if c == 0 or c + block == span:
            pixel = lanes_of(total.shape) + (start - LANES + c)
            total = jnp.where(jnp.logical_and(pixel >= 0, pixel < width), total, 0.0)
        for f in range(4):
            ranged[f, :, c : c + block] = total[f * lines : (f + 1) * lines, :]
    for c in range(0, span, LANES):
        cs = slice(c, c + LANES)
        steps = [(HALO, HALO)] + [(r, 16) for r in range(EDGE, lines - EDGE, 16)] + [(lines - EDGE, HALO)]
        for r, rows in steps:
            smoothed = [along_azimuth(ranged, f, r, rows, cs) for f in range(4)]
            phase, gain = phase_gain(smoothed)
            field[0, r - HALO : r - HALO + rows, cs] = phase
            field[1, r - HALO : r - HALO + rows, cs] = gain
            if rows == 16:
                at = slice(r - EDGE, r - EDGE + rows)
                codes[0, at, cs], codes[1, at, cs] = split(phase)
                codes[2, at, cs] = encode_gain(gain)
    groups = lines // 8
    for t in range(half):
        rims[t] = rim_block(field, groups, range(1, groups - 1), 1, t * tile, tile, None)


def rim_block(field, groups, which, first_group, start, tile, block, hint=None):
    lane = lanes_of((8, LANES))
    if block is None:
        block = jnp.zeros((8, LANES), jnp.float32)
    for f in range(2):
        for side in range(2):
            offset = start if side == 0 else start + LANES + tile
            at = slice(offset, offset + LANES) if hint is None else pl.ds(hint(offset, LANES), LANES)
            for g in which:
                target = (f * 2 + side) * groups + g
                row = 8 * (g - first_group)
                x = field[f, row : row + 8, at]
                shift = (target - (LANES - 1 if side == 0 else 0)) % LANES
                if shift:
                    x = pltpu.roll(x, shift, 1)
                block = jnp.where(lane == target, x, block)
    return block


def border_kernel(lines, width, tile, columns, across, ids, ranged, inside_field, codes, rims, from_next, from_pair, *rest):
    half = columns // 2
    outs, (prod, seg, field, ends) = rest[:half], rest[half:]
    own = ids[1]
    odd = ids[4]
    first_tile, start, span, in_image = window(lines, width, tile, columns, across, own, HALO)
    inside = (
        jnp.where(ids[2] == 0, 0.0, 1.0).astype(jnp.float32),
        jnp.where(ids[2] == ids[3] - 1, 0.0, 1.0).astype(jnp.float32),
    )
    zero = jnp.zeros((HALO, 2 * LANES), jnp.float32)
    own_rows = 2 * HALO
    for e in range(2):
        flag = odd if e == 0 else 1 - odd
        keep = flag.astype(jnp.float32)
        for f in range(4):
            prod[f, :, 0 : 2 * LANES] = zero
            prod[f, :, 2 * LANES + width :] = zero
        for c in range(0, width, 512):
            cs = slice(c, c + 512)
            parts = [
                from_pair[i, :, cs].astype(jnp.float32) * keep + from_next[i, :, cs].astype(jnp.float32) * (1.0 - keep)
                for i in range(4)
            ]
            values = products(*parts, inside[e])
            for f in range(4):
                prod[f, :, 2 * LANES + c : 2 * LANES + c + 512] = values[f]
        for f in range(4):
            total = along_range(prod[f, :, pl.ds(start, span + 2 * LANES)])[:, LANES : LANES + span]
            total = jnp.where(in_image, total, 0.0)
            if e == 0:
                seg[e, f, 0:HALO, :] = total
                seg[e, f, HALO:, :] = ranged[f, 0:own_rows, :]
            else:
                seg[e, f, own_rows:, :] = total
                seg[e, f, 0:own_rows, :] = ranged[f, lines - own_rows :, :]
    border = []
    for e in range(2):
        ref = seg.at[e]
        for c in range(0, span, LANES):
            cs = slice(c, c + LANES)
            smoothed = [along_azimuth(ref, f, HALO, HALO, cs) for f in range(4)]
            phase, gain = phase_gain(smoothed)
            field[0, e * HALO : (e + 1) * HALO, cs] = phase
            field[1, e * HALO : (e + 1) * HALO, cs] = gain
        low, high = end_weights(e == 0)
        r = 0 if e == 0 else own_rows - HALO
        border.append(
            [
                jnp.sum(low * ref[f, r : r + HALO, :] + high * ref[f, r + HALO : r + 2 * HALO, :], axis=0, keepdims=True)
                for f in range(4)
            ]
        )
    phase, gain = phase_gain([jnp.concatenate(pair, axis=0) for pair in zip(*border)])
    ends[0:2, :] = phase
    ends[2:4, :] = gain
    for e in range(2):
        ends[2 + e : 3 + e, :] = ends[2 + e : 3 + e, :] * inside[e]
    groups = lines // 8
    inner = lines - 2 * EDGE
    for n, s in enumerate(range(half, columns) if across else range(half)):
        out = outs[n]
        target = own ^ s
        local = pl.multiple_of((target - first_tile) * tile, LANES)
        cs = pl.ds(pl.multiple_of(local + LANES, LANES), tile)
        for i in range(3):
            out[i * lines + EDGE : i * lines + EDGE + inner, :] = codes[i, :, cs]
        for e in range(2):
            row = 0 if e == 0 else lines - EDGE
            rs = slice(e * HALO, (e + 1) * HALO)
            inner_rows = slice(0, HALO) if e == 0 else slice(lines - 3 * HALO, lines - 2 * HALO)
            pairs = [(field[i, rs, cs], inside_field[i, inner_rows, cs]) for i in range(2)]
            phase, gain = (jnp.concatenate(p if e == 0 else p[::-1], axis=0) for p in pairs)
            out[row : row + EDGE, :], out[lines + row : lines + row + EDGE, :] = split(phase)
            out[2 * lines + row : 2 * lines + row + EDGE, :] = encode_gain(gain)
        block = rims[target - first_tile]
        block = rim_block(field, groups, (0,), 0, local, tile, block, pl.multiple_of)
        block = rim_block(field, groups, (groups - 1,), groups - 2, local, tile, block, pl.multiple_of)
        rows = []
        for i in range(4):
            for h in range(tile // LANES):
                rows.append(ends[i : i + 1, pl.ds(pl.multiple_of(local + (h + 1) * LANES, LANES), LANES)])
        block = jnp.concatenate([block, jnp.concatenate(rows, axis=0)], axis=1)
        out[3 * lines :, :] = jnp.concatenate(split(block), axis=0)


def strip_kernel(lines, width, tile, columns, exchange, ids, first, second, above, below, *rest):
    n_out = len(rest) - 3
    outs, (prod, ranged, field) = rest[:n_out], rest[n_out:]
    k = taps()
    own = ids[1]
    inside_above = jnp.where(ids[2] == 0, 0.0, 1.0).astype(jnp.float32)
    inside_below = jnp.where(ids[2] == ids[3] - 1, 0.0, 1.0).astype(jnp.float32)
    height = lines + 2 * HALO

    zero = jnp.zeros((height, LANES), jnp.float32)
    for f in range(4):
        prod[f, :, 0:LANES] = zero
        prod[f, :, LANES + width :] = zero
    step = min(width, 512)
    for c in range(0, width, step):
        at = slice(LANES + c, LANES + c + step)
        cs = slice(c, c + step)
        rows = min(lines, 16)
        for r in range(0, lines, rows):
            rs = slice(r, r + rows)
            values = products(first[0, rs, cs], first[1, rs, cs], second[0, rs, cs], second[1, rs, cs])
            for f in range(4):
                prod[f, HALO + r : HALO + r + rows, at] = values[f]
        for ref, r, scale in ((above, 0, inside_above), (below, HALO + lines, inside_below)):
            values = products(ref[0, :, cs], ref[1, :, cs], ref[2, :, cs], ref[3, :, cs], scale)
            for f in range(4):
                prod[f, r : r + HALO, at] = values[f]

    step = min(width, 1024)
    for f in range(4):
        for r in range(0, height, 8):
            for c in range(0, width, step):
                x = prod[f, r : r + 8, c : c + step + 2 * LANES]
                n = step + 2 * LANES
                total = k[0] * x
                for j in range(1, RADIUS + 1):
                    total = total + k[j] * (pltpu.roll(x, j, 1) + pltpu.roll(x, n - j, 1))
                ranged[f, r : r + 8, c : c + step] = total[:, LANES : LANES + step]

    for f in range(2):
        field[f, :, 0:LANES] = zero[:lines]
        field[f, :, LANES + width :] = zero[:lines]
    rows = min(lines, 32)
    sub = lax.broadcasted_iota(jnp.int32, (HALO, 1), 0)
    low = jnp.zeros((HALO, 1), jnp.float32)
    high = jnp.zeros((HALO, 1), jnp.float32)
    for j in range(RADIUS + 1):
        low = jnp.where(sub == HALO - 1 - j, k[j], low)
        high = jnp.where(sub == j - 1, k[j], high)
    top, bottom = [], []
    for c in range(0, width, LANES):
        cs = slice(c, c + LANES)
        for r in range(0, lines, rows):
            smoothed = []
            for f in range(4):
                b = HALO + r
                total = k[0] * ranged[f, b : b + rows, cs]
                for j in range(1, RADIUS + 1):
                    total = total + k[j] * (
                        ranged[f, b - j : b - j + rows, cs] + ranged[f, b + j : b + j + rows, cs]
                    )
                smoothed.append(total)
            phase, gain = phase_gain(smoothed)
            field[0, r : r + rows, LANES + c : 2 * LANES + c] = phase
            field[1, r : r + rows, LANES + c : 2 * LANES + c] = gain

    step = min(width, 1024)
    low = low + jnp.zeros((HALO, step), jnp.float32)
    high = high + jnp.zeros((HALO, step), jnp.float32)
    mirror_low = jnp.zeros((HALO, 1), jnp.float32)
    mirror_high = jnp.zeros((HALO, 1), jnp.float32)
    for j in range(RADIUS + 1):
        mirror_high = jnp.where(sub == j, k[j], mirror_high)
        mirror_low = jnp.where(sub == HALO - j, k[j], mirror_low)
    ends = []
    for c in range(0, width, step):
        cs = slice(c, c + step)
        up = [
            jnp.sum(low * ranged[f, 0:HALO, cs] + high * ranged[f, HALO : 2 * HALO, cs], axis=0, keepdims=True)
            for f in range(4)
        ]
        down = [
            jnp.sum(
                mirror_low * ranged[f, lines : lines + HALO, cs]
                + mirror_high * ranged[f, lines + HALO : lines + 2 * HALO, cs],
                axis=0,
                keepdims=True,
            )
            for f in range(4)
        ]
        up_phase, up_gain = phase_gain(up)
        down_phase, down_gain = phase_gain(down)
        ends.append((up_phase, down_phase, up_gain * inside_above, down_gain * inside_below))
    for i, (a, b, c_, d) in enumerate(ends):
        at = slice(i * step, (i + 1) * step)
        prod[0, 0:1, at] = a
        prod[0, 1:2, at] = b
        prod[0, 2:3, at] = c_
        prod[0, 3:4, at] = d

    groups = lines // 8
    lane = lanes_of((8, LANES))

    def pack(out, start, aligned):
        hint = pl.multiple_of if aligned else (lambda v, _: v)
        out[0:lines, :] = field[0, :, pl.ds(hint(start + LANES, LANES), tile)]
        out[lines : 2 * lines, :] = field[1, :, pl.ds(hint(start + LANES, LANES), tile)]
        block = jnp.zeros((8, LANES), jnp.float32)
        for f in range(2):
            for side in range(2):
                offset = start if side == 0 else start + LANES + tile
                for g in range(groups):
                    target = (f * 2 + side) * groups + g
                    x = field[f, 8 * g : 8 * g + 8, pl.ds(hint(offset, LANES), LANES)]
                    shift = (target - (LANES - 1 if side == 0 else 0)) % LANES
                    if shift:
                        x = pltpu.roll(x, shift, 1)
                    block = jnp.where(lane == target, x, block)
        base = 2 * lines
        out[base : base + 8, 0:LANES] = block
        for i in range(4):
            for h in range(tile // LANES):
                out[base + 2 * i + h : base + 2 * i + h + 1, LANES : 2 * LANES] = prod[
                    0, i : i + 1, pl.ds(hint(start + h * LANES, LANES), LANES)
                ]

    if exchange == "permute":
        for s in range(columns):
            pack(outs[s], (own ^ s) * tile, True)
    else:
        for s in range(columns):
            pack(outs[0].at[s], s * tile, False)


def precondition(field, tables, inverse):
    az, az_t, rg, rg_t = tables
    coef = dot3(az, split(field))
    coef = dot3(split(coef), rg_t)
    coef = coef * inverse[...]
    back = dot3(az_t, split(coef))
    return dot3(split(back), rg)


def table_pairs(tables):
    pairs = []
    for ref in tables:
        n = ref.shape[1]
        parts = [ref[i * n : (i + 1) * n, :] for i in range(4)]
        pairs += [(parts[0], parts[1]), (parts[2], parts[3])]
    return pairs


def line_groups(ref, tile_az, edge_lane):
    lane = lanes_of((8, LANES))
    first = (edge_lane // LANES) * LANES
    block = jnp.zeros((8, LANES), jnp.float32)
    for g in range(tile_az // 8):
        x = ref[8 * g : 8 * g + 8, first : first + LANES]
        shift = (g - edge_lane) % LANES
        if shift:
            x = pltpu.roll(x, shift, 1)
        block = jnp.where(lane == g, x, block)
    return block


def spread_groups(block, first_group, count, target_lane, base=0):
    parts = []
    for g in range(first_group, first_group + count):
        shift = (target_lane - (base + g)) % LANES
        parts.append(pltpu.roll(block, shift, 1) if shift else block)
    return jnp.concatenate(parts, axis=0) if count > 1 else parts[0]


def shifted_right(x, left):
    lane = lanes_of(x.shape)
    if left is None:
        return jnp.where(lane == 0, 0.0, pltpu.roll(x, 1, 1))
    wide = jnp.concatenate([left] * (x.shape[1] // LANES), axis=1)
    return jnp.where(lane == 0, wide, pltpu.roll(x, 1, 1))


def shifted_left(x, right):
    lane = lanes_of(x.shape)
    wide = jnp.concatenate([right] * (x.shape[1] // LANES), axis=1)
    return jnp.where(lane == x.shape[1] - 1, wide, pltpu.roll(x, x.shape[1] - 1, 1))


def divergence(tile_az, step, along_x, rim_x, along_y, r):
    rs = slice(r, r + step)
    x = along_x[rs, :]
    return (x - shifted_left(x, rim_x[rs, :])) + along_y[rs, :] - along_y[r + 1 : r + 1 + step, :]


def edges_of(lines, count, tile, coded, sources, scratch, outs):
    phase, gain, sides, ends = scratch
    weight_x, flux_x, rim_x, flux_rim, weight_y, flux_y, weight_end, flux_end = outs
    height = count * lines
    for src, strip in sources:
        if coded:
            row, at = pl.multiple_of(strip * lines, 8), pl.ds(pl.multiple_of(strip * 8, 8), 8)
            phase[pl.ds(HALO + row, lines), :] = src[0:lines, :].astype(jnp.float32) + src[
                lines : 2 * lines, :
            ].astype(jnp.float32)
            gain[pl.ds(HALO + row, lines), :] = decode_gain(src[2 * lines : 3 * lines, :])
            both = src[3 * lines :, :].astype(jnp.float32)
            block = both[0:8, :] + both[8:16, :]
        else:
            row, at = strip * lines, pl.ds(strip * 8, 8)
            phase[pl.ds(HALO + row, lines), :] = src[0:lines, :]
            gain[pl.ds(HALO + row, lines), :] = src[lines : 2 * lines, :]
            block = src[2 * lines : 2 * lines + 8, :]
        sides[at, :] = block[:, 0:LANES]
        ends[at, :] = block[:, LANES : 2 * LANES]
    last = 8 * (count - 1)
    for h in range(tile // LANES):
        cs = slice(h * LANES, (h + 1) * LANES)
        phase[HALO - 1 : HALO, cs] = ends[h : h + 1, :]
        gain[HALO - 1 : HALO, cs] = ends[4 + h : 5 + h, :]
        phase[HALO + height : HALO + height + 1, cs] = ends[last + 2 + h : last + 3 + h, :]
        gain[HALO + height : HALO + height + 1, cs] = ends[last + 6 + h : last + 7 + h, :]

    step = min(height, 32)
    groups = lines // 8
    for r in range(0, height, step):
        rs = slice(r, r + step)
        b = HALO + r
        p, g = phase[b : b + step, :], gain[b : b + step, :]
        halo = []
        for f in range(2):
            for side in range(2):
                parts = []
                for line_group in range(r // 8, (r + step) // 8):
                    strip, inner = divmod(line_group, groups)
                    block = sides[8 * strip : 8 * strip + 8, :]
                    source_lane = (f * 2 + side) * groups + inner
                    shift = ((0 if side == 0 else LANES - 1) - source_lane) % LANES
                    parts.append(pltpu.roll(block, shift, 1) if shift else block)
                halo.append(jnp.concatenate(parts, axis=0) if len(parts) > 1 else parts[0])
        weight_x[rs, :], flux_x[rs, :] = edge(shifted_right(p, halo[0]), shifted_right(g, halo[2]), p, g)
        rim_x[rs, :], flux_rim[rs, :] = edge(p[:, tile - LANES :], g[:, tile - LANES :], halo[1], halo[3])
        weight_y[rs, :], flux_y[rs, :] = edge(phase[b - 1 : b - 1 + step, :], gain[b - 1 : b - 1 + step, :], p, g)
    b = HALO + height
    w, f = edge(phase[b - 1 : b, :], gain[b - 1 : b, :], phase[b : b + 1, :], gain[b : b + 1, :])
    weight_end[...] = jnp.broadcast_to(w, (8, tile))
    flux_end[...] = jnp.broadcast_to(f, (8, tile))


def far_kernel(lines, tile, columns, ids, *rest):
    half = columns // 2
    own = ids[1]
    sources = [(rest[n], (own ^ n) & (half - 1)) for n in range(half)]
    edges_of(lines, half, tile, True, sources, rest[half + 8 :], rest[half : half + 8])


def tile_kernel(lines, tile_az, tile, columns, exchange, ids, *rest):
    coded = exchange == "permute"
    half = columns // 2
    own = ids[1]
    count = half if coded else columns
    if coded:
        sources = [(rest[half - 1 - s], (own ^ s) & (half - 1)) for s in range(half)]
        far, rest = rest[half : half + 8], rest[half + 8 :]
    else:
        sources = [(rest[0].at[s], s) for s in range(columns)]
        rest = rest[1:]
    tables, inverse = rest[:2], rest[2]
    residual, shaped, weight_x, rim_x, weight_y, row_pair, row_next, col_pair, col_next = rest[3:12]
    phase, gain, sides, ends, flux_x, flux_rim, flux_y, weight_end, flux_end = rest[12:]
    pairs = table_pairs(tables)
    height = count * lines
    whole = (weight_x, flux_x, rim_x, flux_rim, weight_y, flux_y)
    if coded:
        lower = (own & half) // half
        at = pl.ds(pl.multiple_of(lower * height, 8), height)
        outs = [ref.at[at, :] for ref in whole]
    else:
        outs = [ref.at[pl.ds(0, height), :] for ref in whole]
    edges_of(
        lines, count, tile, coded, sources, (phase, gain, sides, ends), (*outs, weight_end, flux_end)
    )
    w, f = weight_end[...], flux_end[...]
    if coded:
        at = pl.ds(pl.multiple_of((1 - lower) * height, 8), height)
        for source, ref in zip(far, whole):
            ref[at, :] = source[...]
        w, f = jnp.where(lower == 1, w, far[6][...]), jnp.where(lower == 1, f, far[7][...])
    weight_y[tile_az : tile_az + 8, :] = w
    flux_y[tile_az : tile_az + 8, :] = f

    step = min(tile_az, 32)
    for r in range(0, tile_az, step):
        residual[r : r + step, :] = TURN * divergence(tile_az, step, flux_x, flux_rim, flux_y, r)
    shaped[...] = precondition(residual[...], pairs, inverse)
    row_odd, col_odd = ids[5] == 1, ids[4] == 1
    top = jnp.concatenate([shaped[0:1, h : h + LANES] for h in range(0, tile, LANES)], axis=0)
    bottom = jnp.concatenate([shaped[tile_az - 1 : tile_az, h : h + LANES] for h in range(0, tile, LANES)], axis=0)
    row_pair[0:2, :] = jnp.where(row_odd, top, bottom)
    row_next[0:2, :] = jnp.where(row_odd, bottom, top)
    left = line_groups(shaped, tile_az, 0)
    right = line_groups(shaped, tile_az, tile - 1)
    col_pair[...] = jnp.where(col_odd, left, right)
    col_next[...] = jnp.where(col_odd, right, left)


def apply_operator(tile_az, tile, u, weight_x, rim_x, weight_y, flux_x, flux_rim, flux_y, left, right, out):
    step = min(tile_az, 32)
    for r in range(0, tile_az, step):
        rs = slice(r, r + step)
        b = HALO + r
        x = u[b : b + step, :]
        l = None if left is None else spread_groups(left, r // 8, step // 8, 0)
        flux_x[rs, :] = weight_x[rs, :] * (x - shifted_right(x, l))
        edge_x = x[:, tile - LANES :]
        if right is None:
            flux_rim[rs, :] = -rim_x[rs, :] * edge_x
        else:
            flux_rim[rs, :] = rim_x[rs, :] * (spread_groups(right, r // 8, step // 8, LANES - 1) - edge_x)
        flux_y[rs, :] = weight_y[rs, :] * (x - u[b - 1 : b - 1 + step, :])
    b = HALO + tile_az
    flux_y[tile_az : tile_az + 1, :] = weight_y[tile_az : tile_az + 1, :] * (u[b : b + 1, :] - u[b - 1 : b, :])
    for r in range(0, tile_az, step):
        out[r : r + step, :] = DAMPING * u[HALO + r : HALO + r + step, :] + divergence(
            tile_az, step, flux_x, flux_rim, flux_y, r
        )


def inner(a, b, tile_az, offset_a=0, offset_b=0):
    total = jnp.zeros((32, a.shape[1]), jnp.float32)
    for r in range(0, tile_az, 32):
        total = total + a[offset_a + r : offset_a + r + 32, :] * b[offset_b + r : offset_b + r + 32, :]
    return jnp.sum(jnp.sum(total, axis=0, keepdims=True), axis=1, keepdims=True)


def second_kernel(
    tile_az, tile, ids, residual, shaped, weight_x, rim_x, weight_y, col_next, col_pair, row_next, row_pair, *rest
):
    tables, inverse = rest[:2], rest[2]
    operated, shaped2, operated2, chunk, roots = rest[3:8]
    u, flux_x, flux_rim, flux_y = rest[8:]
    pairs = table_pairs(tables)
    row_odd, col_odd = ids[5] == 1, ids[4] == 1
    up = jnp.where(row_odd, row_pair[0:2, :], row_next[0:2, :])
    down = jnp.where(row_odd, row_next[0:2, :], row_pair[0:2, :])
    left = jnp.where(col_odd, col_pair[...], col_next[...])
    right = jnp.where(col_odd, col_next[...], col_pair[...])
    u[HALO : HALO + tile_az, :] = shaped[...]
    for h in range(tile // LANES):
        cs = slice(h * LANES, (h + 1) * LANES)
        u[HALO - 1 : HALO, cs] = up[h : h + 1, :]
        u[HALO + tile_az : HALO + tile_az + 1, cs] = down[h : h + 1, :]
    apply_operator(
        tile_az, tile, u, weight_x, rim_x, weight_y, flux_x, flux_rim, flux_y, left, right, operated
    )
    image = precondition(operated[...], pairs, inverse)
    shaped2[...] = image
    u[HALO : HALO + tile_az, :] = image
    apply_operator(
        tile_az, tile, u, weight_x, rim_x, weight_y, flux_x, flux_rim, flux_y, left, right, operated2
    )
    lane = lanes_of((1, LANES))
    sums = jnp.zeros((1, LANES), jnp.float32)
    for i, (a, b) in enumerate(
        (
            (residual, shaped),
            (shaped, operated),
            (residual, shaped2),
            (operated, shaped2),
            (shaped2, operated2),
        )
    ):
        sums = jnp.where(lane == i, inner(a, b, tile_az), sums)
    def rows_of(x):
        return jnp.concatenate([x[:, h : h + LANES] for h in range(0, tile, LANES)], axis=0)

    weight_t, weight_b = rows_of(weight_y[0:1, :]), rows_of(weight_y[tile_az : tile_az + 1, :])
    weight_l, weight_r = line_groups(weight_x, tile_az, 0), line_groups(rim_x, tile_az, LANES - 1)
    top = rows_of(image_row(shaped2, shaped, 0))
    bottom = rows_of(image_row(shaped2, shaped, tile_az - 1))
    left_rim = line_groups(shaped2, tile_az, 0) - line_groups(shaped, tile_az, 0)
    right_rim = line_groups(shaped2, tile_az, tile - 1) - line_groups(shaped, tile_az, tile - 1)
    known = jnp.sum(weight_t * up * top + weight_b * down * bottom, keepdims=True) + jnp.sum(
        weight_l * left * left_rim + weight_r * right * right_rim, keepdims=True
    )
    sums = jnp.where(lane == 4, sums - known, sums)
    half = tile_az // 8
    wide = lanes_of((8, LANES))
    root_sides = jnp.sqrt(jnp.where(wide < half, weight_l, pltpu.roll(weight_r, half, 1)))
    sides = root_sides * jnp.where(wide < half, left_rim, pltpu.roll(right_rim, half, 1))
    root_ends = jnp.sqrt(jnp.concatenate([weight_t, weight_b], axis=0))
    ends = root_ends * jnp.concatenate([top, bottom], axis=0)
    scale = jnp.maximum(jnp.max(jnp.abs(sides), keepdims=True), jnp.max(jnp.abs(ends), keepdims=True))
    scale = (scale * 1.01).astype(jnp.bfloat16).astype(jnp.float32)
    sums = jnp.where(lane == SCALE_LANE, scale, sums)
    high = sums.astype(jnp.bfloat16).astype(jnp.float32)
    middle = (sums - high).astype(jnp.bfloat16).astype(jnp.float32)
    rest_ = sums - high - middle
    sums = high + pltpu.roll(middle, 8, 1) + pltpu.roll(rest_, 16, 1)
    chunk[...] = jnp.concatenate(
        [encode_power(sides, scale), encode_power(ends, scale), jnp.broadcast_to(sums, (4, LANES))], axis=0
    ).astype(jnp.bfloat16)
    roots[...] = jnp.concatenate([root_sides, root_ends, root_ends], axis=0)


def image_row(a, b, row):
    return a[row : row + 1, :] - b[row : row + 1, :]


def last_kernel(
    tile_az, tile, rows, columns, ids, gathered, residual, shaped, operated, shaped2, operated2, roots,
    solution_hbm, residual_hbm, solution_out, residual_out, sems
):
    half = tile_az // 8
    lane = lanes_of((8, LANES))
    total = jnp.zeros((4, LANES), jnp.float32)
    cross_x = jnp.zeros((8, LANES), jnp.float32)
    cross_y = jnp.zeros((2, LANES), jnp.float32)
    values = {}

    def decoded(i):
        x = gathered[i].astype(jnp.float32)
        return jnp.concatenate([decode_power(x[0:12, :], x[12:13, SCALE_LANE : SCALE_LANE + 1]), x[12:16, :]], axis=0)

    def value_of(i):
        if i not in values:
            values[i] = decoded(i)
        return values[i]

    for r in range(rows):
        for c in range(columns):
            i = r * columns + c
            here = value_of(i)
            total = total + here[12:16, :]
            if c + 1 < columns:
                cross_x = cross_x + pltpu.roll(here[0:8, :], LANES - half, 1) * value_of(i + 1)[0:8, :]
            if r + 1 < rows:
                cross_y = cross_y + here[10:12, :] * value_of(i + columns)[8:10, :]
    cross = jnp.sum(jnp.where(lane < half, cross_x, 0.0), keepdims=True) + jnp.sum(cross_y, keepdims=True)
    wide = total[0:1, :]
    first_lane = lanes_of((1, LANES))
    pick = [
        jnp.sum(jnp.where(first_lane % 8 == i, jnp.where(first_lane < 24, wide, 0.0), 0.0), axis=1, keepdims=True)
        for i in range(5)
    ]
    dot0, curve0, mixed, cross_dot, curve2 = pick
    curve2 = curve2 - 2.0 * cross
    alpha = dot0 / curve0
    fresh = dot0 - alpha * (mixed + curve0) + alpha * alpha * cross_dot
    beta = fresh / dot0
    grown = 1.0 + beta
    curve1 = grown * grown * curve0 - 2.0 * alpha * grown * cross_dot + alpha * alpha * curve2
    step1 = fresh / curve1
    on_first = alpha + step1 * grown
    on_second = step1 * alpha

    row, col = ids[0], ids[1]
    here = row * columns + col

    def neighbour(ok, index):
        return jnp.where(ok, index, here), jnp.where(ok, 1.0, 0.0).astype(jnp.float32)

    up, up_ok = neighbour(row > 0, here - columns)
    down, down_ok = neighbour(row < rows - 1, here + columns)
    left, left_ok = neighbour(col > 0, here - 1)
    right, right_ok = neighbour(col < columns - 1, here + 1)
    near = [decoded(i) for i in (left, right, up, down)]
    from_left = pltpu.roll(near[0][0:8, :], LANES - half, 1) * left_ok
    from_right = pltpu.roll(near[1][0:8, :], half, 1) * right_ok
    top = jnp.concatenate([near[2][10 + h : 11 + h, :] for h in range(tile // LANES)], axis=1) * up_ok
    bottom = jnp.concatenate([near[3][8 + h : 9 + h, :] for h in range(tile // LANES)], axis=1) * down_ok
    top = top * jnp.concatenate([roots[8 + h : 9 + h, :] for h in range(tile // LANES)], axis=1)
    bottom = bottom * jnp.concatenate([roots[10 + h : 11 + h, :] for h in range(tile // LANES)], axis=1)
    from_left = from_left * roots[0:8, :]
    from_right = from_right * roots[0:8, :]
    step = min(tile_az, 64)
    copies = []
    for r in range(0, tile_az, step):
        rs = slice(r, r + step)
        solution_out[rs, :] = on_first * shaped[rs, :] - on_second * shaped2[rs, :]
        q = operated2[rs, :]
        wide = lanes_of((step, tile))
        l = jnp.concatenate([spread_groups(from_left, r // 8, step // 8, 0)] * (tile // LANES), axis=1)
        q = q - jnp.where(wide == 0, l, 0.0)
        l = jnp.concatenate([spread_groups(from_right, r // 8, step // 8, LANES - 1, half)] * (tile // LANES), axis=1)
        q = q - jnp.where(wide == tile - 1, l, 0.0)
        if r == 0 or r + step == tile_az:
            deep = lax.broadcasted_iota(jnp.int32, (step, tile), 0)
        if r == 0:
            q = q - jnp.where(deep == 0, jnp.broadcast_to(top, (step, tile)), 0.0)
        if r + step == tile_az:
            q = q - jnp.where(deep == step - 1, jnp.broadcast_to(bottom, (step, tile)), 0.0)
        residual_out[rs, :] = residual[rs, :] - on_first * operated[rs, :] + on_second * q
        for n, (src, dst) in enumerate(((solution_out, solution_hbm), (residual_out, residual_hbm))):
            copy = pltpu.make_async_copy(src.at[rs, :], dst.at[rs, :], sems.at[2 * (r // step) + n])
            copy.start()
            copies.append(copy)
    for copy in copies:
        copy.wait()


def swapped(value, axis, count, step):
    if step == 0:
        pairs = [(i, i ^ 1) for i in range(count)]
    else:
        pairs = [(i, (i + 1 if i % 2 else i - 1) % count) for i in range(count)]
    return lax.ppermute(value, axis, pairs)


def shards(rows, columns, first_slc, second_slc):
    lines, width = first_slc.shape[1:]
    tile = width // columns
    tile_az = lines * columns
    axes = ("row", "col")
    exchange = "permute" if lines >= 4 * EDGE and columns <= 8 else "all_to_all"
    row, col = lax.axis_index("row"), lax.axis_index("col")
    ids = jnp.stack([row, col, row * columns + col, jnp.int32(rows * columns), col % 2, row % 2]).astype(jnp.int32)
    f32, bf16 = jnp.float32, jnp.bfloat16

    head = jnp.concatenate([first_slc[:, :HALO], second_slc[:, :HALO]], 0)
    tail = jnp.concatenate([first_slc[:, -HALO:], second_slc[:, -HALO:]], 0)
    odd = col % 2 == 1
    from_pair = swapped(jnp.where(odd, head, tail), axes, rows * columns, 0)
    from_next = swapped(jnp.where(odd, tail, head), axes, rows * columns, 1)
    wide = width + 2 * LANES
    if exchange == "permute":
        half = columns // 2
        span = half * tile + 2 * LANES
        smoothing = jnp.asarray(np.concatenate(two_parts(range_table(4 * LANES, 2 * LANES)), axis=0))
        sent = [None] * columns
        sources = (first_slc, second_slc)
        for across in (True, False):
            ranged, inner, codes, rims = interior(
                functools.partial(interior_kernel, lines, width, tile, columns, across),
                [
                    ((4, lines, span), f32),
                    ((2, lines - 2 * HALO, span), f32),
                    ((3, lines - 2 * EDGE, span), bf16),
                    ((half, 8, LANES), f32),
                ],
                (ids, *sources, smoothing),
                [
                    pltpu.VMEM((2, 2, lines, span + 2 * LANES), bf16),
                    pltpu.VMEM((4 * lines, span + 2 * LANES), bf16),
                    pltpu.VMEM((4 * lines, span + 2 * LANES), bf16),
                    pltpu.SemaphoreType.DMA((lines // 8,)),
                ],
            )
            part = call(
                functools.partial(border_kernel, lines, width, tile, columns, across),
                [((3 * lines + 16, tile), bf16)] * half,
                (ids, ranged, inner, codes, rims, from_next, from_pair),
                [
                    pltpu.VMEM((4, HALO, width + 4 * LANES), f32),
                    pltpu.VMEM((2, 4, 3 * HALO, span), f32),
                    pltpu.VMEM((2, 2 * HALO, span), f32),
                    pltpu.VMEM((8, span), f32),
                ],
                "borders",
            )
            for i, value in enumerate(part):
                sent[i + (half if across else 0)] = value
            if across:
                *part, first_slc, second_slc = lax.optimization_barrier((*part, first_slc, second_slc))
                sources = (first_slc, second_slc)
                for i, value in enumerate(part):
                    sent[i + half] = value
        arrived = [sent[0]] + [
            lax.ppermute(sent[s], "col", [(i, i ^ s) for i in range(columns)]) for s in range(1, columns)
        ]
    else:
        above = jnp.where(odd, from_pair, from_next)
        below = jnp.where(odd, from_next, from_pair)
        height = lines + 2 * HALO
        sent = call(
            functools.partial(strip_kernel, lines, width, tile, columns, exchange),
            [((columns, 2 * lines + 8, tile), f32)],
            (ids, first_slc, second_slc, above, below),
            [pltpu.VMEM((4, height, wide), f32), pltpu.VMEM((4, height, width), f32), pltpu.VMEM((2, lines, wide), f32)],
            "strips",
        )
        arrived = [lax.all_to_all(sent[0], "col", 0, 0, tiled=True)]

    tables = []
    for table in (cosine_table(tile_az), cosine_table(tile)):
        parts = [*two_parts(table), *two_parts(table.T)]
        tables.append(jnp.asarray(np.concatenate(parts, axis=0)))
    inverse = jnp.asarray(inverse_eigen(tile_az, tile))

    whole = ((tile_az, tile), f32)
    block = ((8, LANES), f32)
    padded = pltpu.VMEM((tile_az + 2 * HALO, tile), f32)
    fluxes = [
        pltpu.VMEM((tile_az, tile), f32),
        pltpu.VMEM((tile_az, LANES), f32),
        pltpu.VMEM((tile_az + 8, tile), f32),
    ]
    edge_rows = tile_az
    if exchange == "permute":
        edge_rows = half * lines
        part = ((edge_rows, tile), f32)
        side = ((edge_rows, LANES), f32)
        last = ((8, tile), f32)
        far = call(
            functools.partial(far_kernel, lines, tile, columns),
            [part, part, side, side, part, part, last, last],
            (ids, *arrived[half:]),
            [
                pltpu.VMEM((edge_rows + 2 * HALO, tile), f32),
                pltpu.VMEM((edge_rows + 2 * HALO, tile), f32),
                pltpu.VMEM((8 * half, LANES), f32),
                pltpu.VMEM((8 * half, LANES), f32),
            ],
            "far",
        )
        arrived = [*arrived[:half][::-1], *far]
    gathered_lines = pltpu.VMEM((edge_rows + 2 * HALO, tile), f32)
    residual, shaped, weight_x, rim_x, weight_y, row_pair, row_next, col_pair, col_next = call(
        functools.partial(tile_kernel, lines, tile_az, tile, columns, exchange),
        [whole, whole, whole, ((tile_az, LANES), f32), ((tile_az + 8, tile), f32), block, block, block, block],
        (ids, *arrived, *tables, inverse),
        [
            gathered_lines,
            gathered_lines,
            pltpu.VMEM((8 * columns, LANES), f32),
            pltpu.VMEM((8 * columns, LANES), f32),
            *fluxes,
            pltpu.VMEM((8, tile), f32),
            pltpu.VMEM((8, tile), f32),
        ],
        "tiles",
    )
    col_next = swapped(col_next, "col", columns, 1)
    col_pair = swapped(col_pair, "col", columns, 0)
    row_next = swapped(row_next, "row", rows, 1)
    row_pair = swapped(row_pair, "row", rows, 0)
    rims = (col_next, col_pair, row_next, row_pair)
    operated, shaped2, operated2, chunk, roots = call(
        functools.partial(second_kernel, tile_az, tile),
        [whole, whole, whole, ((16, LANES), bf16), ((16, LANES), f32)],
        (ids, residual, shaped, weight_x, rim_x, weight_y, *rims, *tables, inverse),
        [padded, *fluxes],
        "operator",
    )
    spread = jnp.broadcast_to(chunk[None], (rows * columns, 16, LANES))
    gathered = lax.all_to_all(spread, axes, 0, 0, tiled=True)
    return tuple(
        call(
            functools.partial(last_kernel, tile_az, tile, rows, columns),
            [whole, whole],
            (ids, gathered, residual, shaped, operated, shaped2, operated2, roots),
            [
                pltpu.VMEM((tile_az, tile), f32),
                pltpu.VMEM((tile_az, tile), f32),
                pltpu.SemaphoreType.DMA((2 * (tile_az // min(tile_az, 64)),)),
            ],
            "finish",
            out_space=pltpu.HBM,
        )
    )


def solution(mesh):
    placed = P(None, ("row", "col"), None)
    return jax.shard_map(
        functools.partial(shards, mesh.shape["row"], mesh.shape["col"]),
        mesh=mesh,
        in_specs=(placed, placed),
        out_specs=(P("row", "col"), P("row", "col")),
        check_vma=False,
    )
```
